32 devices in a mesh: narrow: 4 (over x, core), wide: 8 (over z, y).
Axes of the slice: x: 2, y: 2, z: 4, core: 2. Of those that a mesh axis runs over, the one named last changes fastest.
Arguments:
- vectors: float32 [512, 6144], P('wide', 'narrow'), may hold values from -63 to 63
- blocks: float32 [48, 5, 128, 128], P('narrow'), may hold values from -0.125 to 0.125
- columns: int32 [48, 5], P('narrow'), may hold values from 0 to 47, as said below
- lower_bound: float32 [1], replicated, may hold values from -0.8 to -0.2
- upper_bound: float32 [1], replicated, may hold values from 2.2 to 2.8
Outputs:
- basis: float32 [512, 6144], P(None, ('narrow', 'wide'))
The draws below stay inside these ranges and needn't reach their ends.
Inputs may be any that keep to these rules, and one draw needn't show every extreme that they name: `columns`: row r holds 5 different block-rows, each within 3 of r along the closed loop of 48 block-rows (indices taken modulo 48); r - 1 and r + 1 appear in every row, r - 3 in every even row and r + 3 in every odd row.
All inputs are finite; a program needn't handle non-finite values.
Results may differ from the reference program's by a relative error of at most 0.0001.
Values sent between devices are 32-bit elements; how exact they have to be, the bound alone decides.
No kernel may reach another device: no remote copies, remote signals or barrier semaphores. Data moves between devices by JAX's collectives and lax.ppermute only.
A program may use at most 64 MiB of HBM per device.

```python
import jax
import jax.numpy as jnp
from jax import lax

K = 512
BLOCK = 128
SLOTS = 5
REACH = 3
STEPS = 8
NB = 48
N = 6144


def draw_vectors(key, part):
    key_main = jax.random.fold_in(key, 11)
    key_cols = jax.random.fold_in(key, 12)
    noise = jnp.clip(jax.random.normal(key_main, (K, N), jnp.float32), -5.0, 5.0)
    col_scale = jnp.exp(jax.random.uniform(key_cols, (K, 1), jnp.float32, jnp.log(0.3), jnp.log(3.0)))
    row_scale = jnp.exp(jnp.log(3.0) * jnp.arange(N, dtype=jnp.float32) / N)[None, :]
    return noise * col_scale * row_scale


def draw_columns(key, part):
    key_pick = jax.random.fold_in(key, 21)
    block_ids = jnp.arange(NB, dtype=jnp.int32)
    far_side = jnp.where(block_ids % 2 == 0, -REACH, REACH).astype(jnp.int32)
    middle = jnp.array([-(REACH - 1), 0, REACH - 1], dtype=jnp.int32)
    candidates = jnp.concatenate([jnp.broadcast_to(middle[None, :], (NB, 3)), (-far_side)[:, None]], axis=1)
    scores = jax.random.randint(key_pick, (NB, 4), 0, 1 << 20) * 4 + jnp.arange(4, dtype=jnp.int32)[None, :]
    order = jnp.argsort(scores, axis=1)[:, :2]
    chosen = jnp.take_along_axis(candidates, order, axis=1)
    offsets = jnp.concatenate([jnp.full((NB, 1), -1, jnp.int32), jnp.full((NB, 1), 1, jnp.int32), far_side[:, None], chosen], axis=1)
    return ((block_ids[:, None] + offsets) % NB).astype(jnp.int32)


def block_scale(key, extent, split, smallest, high):
    def one(axis_at, parts):
        draws = jax.random.uniform(jax.random.fold_in(jax.random.fold_in(key, 6), axis_at), (parts,), jnp.float32, smallest / len(split), high / len(split))
        return jnp.repeat(jnp.exp(draws), extent[axis_at] // parts).reshape((-1,) + (1,) * (len(extent) - axis_at - 1))

    level = one(*split[0])
    for cut in split[1:]:
        level = level * one(*cut)
    return level


def normal_values(key, dims, scale, bound, split=(), held_as=jnp.bfloat16):
    gain = block_scale(key, dims, split, -0.22, 0.18) if split else 1.0
    values = jax.random.normal(key, dims, jnp.float32) * scale * gain
    return jnp.minimum(jnp.maximum(values, -bound), bound).astype(held_as)


def setup_inputs(seed: int = 0) -> dict:
    keys = jax.random.split(jax.random.key(seed), 6)
    vectors = draw_vectors(jax.random.fold_in(keys[5], 71), 0)
    blocks = normal_values(keys[1], (NB, SLOTS, BLOCK, BLOCK), (20 * BLOCK) ** -0.5, 0.125, ((0, 4),), jnp.float32)
    columns = draw_columns(jax.random.fold_in(keys[5], 71), 0)
    lower_bound = jnp.clip(jax.random.uniform(keys[3], (1,), jnp.float32, -0.8, -0.2), -0.8, -0.2)
    upper_bound = jnp.clip(jax.random.uniform(keys[4], (1,), jnp.float32, 2.2, 2.8), 2.2, 2.8)
    return {"vectors": vectors, "blocks": blocks, "columns": columns, "lower_bound": lower_bound, "upper_bound": upper_bound}


def operate(source, blocks, columns):
    count = source.shape[0]
    nblocks = blocks.shape[0]
    bsize = blocks.shape[2]
    tile_rows = source.reshape(count, nblocks, bsize)
    summed = jnp.zeros_like(tile_rows)
    for slot in range(blocks.shape[1]):
        picked = tile_rows[:, columns[:, slot], :]
        summed = summed + jnp.einsum('rij,krj->kri', blocks[:, slot], picked, precision=lax.Precision.HIGHEST)
    return source + summed.reshape(count, nblocks * bsize)

def reference(vectors, blocks, columns, lower_bound, upper_bound):
    centre = (upper_bound[0] + lower_bound[0]) * 0.5
    half_width = (upper_bound[0] - lower_bound[0]) * 0.5
    previous = vectors
    current = (operate(vectors, blocks, columns) - centre * vectors) / half_width
    for step in range(STEPS - 1):
        following = 2.0 * (operate(current, blocks, columns) - centre * current) / half_width - previous
        previous = current
        current = following
    gram_matrix = jnp.dot(current, current.T, preferred_element_type=jnp.float32, precision=lax.Precision.HIGHEST)
    frob_norm = jnp.sqrt(jnp.sum(gram_matrix * gram_matrix) + 1e-06)
    rotation = 1.5 * jnp.eye(K, dtype=gram_matrix.dtype) - 0.5 * gram_matrix / frob_norm
    rotated = jnp.dot(rotation, current, preferred_element_type=jnp.float32, precision=lax.Precision.HIGHEST)
    return jnp.sqrt(N / frob_norm) * rotated
```

```python
import functools

import jax
import jax.numpy as jnp
from jax import lax
from jax.experimental import pallas as pl
from jax.experimental.pallas import tpu as pltpu
from jax.sharding import PartitionSpec as P

REACH = 3
STEPS = 8
TILE = 128
VM = pl.BlockSpec(memory_space=pltpu.VMEM)
SM = pl.BlockSpec(memory_space=pltpu.SMEM)
NT = (((1,), (1,)), ((), ()))
NN = (((1,), (0,)), ((), ()))
F32 = jnp.float32
BF16 = jnp.bfloat16


def params():
    return pltpu.CompilerParams(vmem_limit_bytes=40 * 1024 * 1024)


def split(x):
    hi = x.astype(BF16)
    return hi, (x - hi.astype(F32)).astype(BF16)


def dot(a, b, dims):
    return lax.dot_general(a, b, dims, preferred_element_type=F32)


def dot_split(a_hi, a_both, b_hi, b_lo, dims):
    rows = a_hi.shape[0]
    upper = dot(a_both, b_hi, dims)
    return upper[:rows] + (upper[rows:] + dot(a_hi, b_lo, dims))


def setup_kernel(total_blocks, columns_ref, lower_ref, upper_ref, blocks_ref, hi_ref, lo_ref):
    rows, slots, size, _ = blocks_ref.shape
    first = lax.axis_index("narrow") * rows
    half_width = (jnp.full((1, size), upper_ref[0], F32) - jnp.full((1, size), lower_ref[0], F32)) * 0.5
    scale = 2.0 / half_width
    hi_ref[...] = jnp.zeros_like(hi_ref)
    lo_ref[...] = jnp.zeros_like(lo_ref)
    for row in range(rows):
        pair, half = divmod(row, 2)
        here = slice(half * size, half * size + size)
        for slot in range(slots):
            place = lax.rem(columns_ref[row, slot] - first + REACH + total_blocks, total_blocks) - 2 * pair
            hi, lo = split(blocks_ref[row, slot] * scale)
            there = pl.ds(pl.multiple_of(place * size, size), size)
            hi_ref[pair, here, there] = hi
            lo_ref[pair, here, there] = lo


def setup(columns, lower_bound, upper_bound, blocks, total_blocks):
    rows, _, size, _ = blocks.shape
    shape = jax.ShapeDtypeStruct((rows // 2, 2 * size, (2 * REACH + 2) * size), BF16)
    return pl.pallas_call(
        functools.partial(setup_kernel, total_blocks),
        in_specs=[SM, SM, SM, VM],
        out_specs=[VM, VM],
        out_shape=[shape, shape],
        compiler_params=params(),
        name="setup",
    )(columns, lower_bound, upper_bound, blocks)


def diagonal(lower_ref, upper_ref, width):
    upper = jnp.full((1, width), upper_ref[0], F32)
    lower = jnp.full((1, width), lower_ref[0], F32)
    return 2.0 * (1.0 - (upper + lower) * 0.5) / ((upper - lower) * 0.5)


def odd_device():
    return lax.rem(lax.axis_index("narrow"), 2) == 1


def local_kernel(first_step, lower_ref, upper_ref, *refs):
    if first_step:
        mid_ref, hi_ref, lo_ref, out_ref = refs
        current = mid_ref[...]
    else:
        mid_ref, far_ref, near_ref, previous_ref, hi_ref, lo_ref, out_ref, full_ref = refs
        edge = far_ref.shape[1]
        odd = odd_device()
        left = jnp.where(odd, near_ref[...], far_ref[...])
        right = jnp.where(odd, far_ref[...], near_ref[...])
        current = jnp.concatenate([left, mid_ref[:, edge:-edge], right], axis=1)
        full_ref[...] = current
    pairs, width, window = hi_ref.shape
    size = width // 2
    diag = diagonal(lower_ref, upper_ref, width)
    hi, lo = split(current)
    both = jnp.concatenate([hi, lo], axis=0)
    for pair in range(pairs):
        start = 2 * pair - REACH
        begin, end = max(start, 0), min(start + window // size, 2 * pairs)
        there = slice(begin * size, end * size)
        inside = slice((begin - start) * size, (end - start) * size)
        here = slice(pair * width, pair * width + width)
        total = dot_split(hi[:, there], both[:, there], hi_ref[pair, :, inside], lo_ref[pair, :, inside], NT)
        total = total + diag * current[:, here]
        out_ref[:, here] = total * 0.5 if first_step else total - previous_ref[:, here]


def local_part(bounds, state, previous, operator):
    mid = state[0]
    shape = jax.ShapeDtypeStruct(mid.shape, F32)
    first_step = previous is None
    operands = (*bounds, *state, *(() if first_step else (previous,)), *operator)
    width = operator[0].shape[1]
    return pl.pallas_call(
        functools.partial(local_kernel, first_step),
        in_specs=[SM, SM] + [VM] * (len(operands) - 2),
        out_specs=VM if first_step else [VM, VM],
        out_shape=shape if first_step else [shape, shape],
        compiler_params=params(),
        cost_estimate=pl.CostEstimate(flops=24 * mid.size * width, bytes_accessed=8 * mid.size, transcendentals=0),
        name="local_part",
    )(*operands)


def halo_sums(first_step, mid_ref, far_ref, near_ref, hi_ref, lo_ref):
    pairs, width, window = hi_ref.shape
    size = width // 2
    edge = REACH * size
    odd = odd_device()
    left = jnp.where(odd, near_ref[...], far_ref[...])
    right = jnp.where(odd, far_ref[...], near_ref[...])
    factor = 0.5 if first_step else 1.0

    def reach_into(pair, halo, inside):
        hi, lo = split(halo)
        both = jnp.concatenate([hi, lo], axis=0)
        return factor * dot_split(hi, both, hi_ref[pair, :, inside], lo_ref[pair, :, inside], NT)

    outer = reach_into(0, left, slice(0, edge))
    inner = reach_into(1, left[:, -size:], slice(0, size))
    left_out = mid_ref[:, :edge] + jnp.concatenate([outer, inner[:, :size]], axis=1)
    outer = reach_into(pairs - 1, right, slice(window - edge, window))
    inner = reach_into(pairs - 2, right[:, :size], slice(window - size, window))
    right_out = mid_ref[:, -edge:] + jnp.concatenate([inner[:, size:], outer], axis=1)
    return left_out, right_out


def halo_kernel(first_step, mid_ref, far_ref, near_ref, hi_ref, lo_ref, far_out_ref, near_out_ref):
    left, right = halo_sums(first_step, mid_ref, far_ref, near_ref, hi_ref, lo_ref)
    odd = odd_device()
    far_out_ref[...] = jnp.where(odd, right, left)
    near_out_ref[...] = jnp.where(odd, left, right)


def halo_part(first_step, mid, far, near, operator):
    return pl.pallas_call(
        functools.partial(halo_kernel, first_step),
        in_specs=[VM] * 5,
        out_specs=[VM, VM],
        out_shape=[jax.ShapeDtypeStruct(far.shape, F32)] * 2,
        compiler_params=params(),
        cost_estimate=pl.CostEstimate(flops=24 * far.size * 512, bytes_accessed=8 * mid.size, transcendentals=0),
        name="halo_part",
    )(mid, far, near, *operator)


def last_kernel(mid_ref, far_ref, near_ref, hi_ref, lo_ref, out_ref):
    left, right = halo_sums(False, mid_ref, far_ref, near_ref, hi_ref, lo_ref)
    edge = left.shape[1]
    out_ref[...] = jnp.concatenate([left, mid_ref[:, edge:-edge], right], axis=1)


def last_part(mid, far, near, operator):
    return pl.pallas_call(
        last_kernel,
        in_specs=[VM] * 5,
        out_specs=VM,
        out_shape=jax.ShapeDtypeStruct(mid.shape, F32),
        compiler_params=params(),
        name="last_part",
    )(mid, far, near, *operator)


def exchange(far, near):
    size = lax.axis_size("narrow")
    far_pairs = [(i, (i + 1) % size if i % 2 else (i - 1) % size) for i in range(size)]
    near_pairs = [(i, i ^ 1) for i in range(size)]
    return lax.ppermute(far, "narrow", far_pairs), lax.ppermute(near, "narrow", near_pairs)


def filtered_rows(vectors, blocks, columns, lower_bound, upper_bound):
    total_blocks = blocks.shape[0] * lax.axis_size("narrow")
    edge = REACH * blocks.shape[2]
    bounds = (lower_bound, upper_bound)
    odd = odd_device()
    left, right = vectors[:, :edge], vectors[:, -edge:]
    far, near = jnp.where(odd, right, left), jnp.where(odd, left, right)
    operator = setup(columns, lower_bound, upper_bound, blocks, total_blocks)
    state, previous = (vectors,), None
    for step in range(STEPS):
        halo = exchange(far, near)
        if step == 0:
            mid, full = local_part(bounds, state, None, operator), vectors
        else:
            mid, full = local_part(bounds, state, previous, operator)
        previous = full
        if step == STEPS - 1:
            return last_part(mid, *halo, operator)
        far, near = halo_part(step == 0, mid, *halo, operator)
        state = (mid, far, near)


def pair_perm(mask):
    narrow, wide = lax.axis_size("narrow"), lax.axis_size("wide")
    return [(n * wide + w, (n ^ mask[0]) * wide + (w ^ mask[1])) for n in range(narrow) for w in range(wide)]


def swap(x, mask):
    return lax.ppermute(x, ("narrow", "wide"), pair_perm(mask))


def bit_groups():
    narrow = [(1 << b, 0) for b in range(lax.axis_size("narrow").bit_length() - 1)]
    wide = [(0, 1 << b) for b in range(lax.axis_size("wide").bit_length() - 1)]
    rest = wide[1:] + narrow[2:]
    return [narrow[:1], narrow[1:2] + wide[:1]] + [rest[i : i + 2] for i in range(0, len(rest), 2)]


def masks(bits):
    out = []
    for d in range(1 << len(bits)):
        chosen = [b for k, b in enumerate(bits) if d >> k & 1]
        out.append((sum(b[0] for b in chosen), sum(b[1] for b in chosen)))
    return out


def place_in(bits):
    n, w = lax.axis_index("narrow"), lax.axis_index("wide")
    place = 0
    for k, b in enumerate(bits):
        bit = (n // b[0]) % 2 if b[0] else (w // b[1]) % 2
        place = place + (bit << k)
    return place


def all_sum(x):
    groups = bit_groups()
    for bits in groups[:-1]:
        place, members = place_in(bits), masks(bits)
        parts = x.reshape(len(members), -1, x.shape[-1])
        own = lax.dynamic_index_in_dim(parts, place, 0, keepdims=False)
        for d in range(1, len(members)):
            sent = lax.dynamic_index_in_dim(parts, place ^ d, 0, keepdims=False)
            own = own + swap(sent, members[d])
        x = own
    members = masks(groups[-1])
    x = x + sum(swap(x, members[d]) for d in range(1, len(members)))
    for bits in groups[:-1][::-1]:
        place, members = place_in(bits), masks(bits)
        parts = jnp.stack([x] + [swap(x, members[d]) for d in range(1, len(members))])
        x = jnp.concatenate([lax.dynamic_index_in_dim(parts, place ^ a, 0, keepdims=False) for a in range(len(members))])
    return x


def tile_pairs(count):
    return [(i, j) for i in range(count) for j in range(i, count)]


def gram_kernel(rows_ref, out_ref):
    count = rows_ref.shape[0] // TILE
    hi, lo = split(rows_ref[...])
    at = 0
    for i in range(count):
        here, there = slice(i * TILE, (i + 1) * TILE), slice(i * TILE, None)
        both = jnp.concatenate([hi[here], lo[here]], axis=0)
        strip = dot_split(hi[here], both, hi[there], lo[there], NT)
        for j in range(i, count):
            out_ref[at * TILE : (at + 1) * TILE, :] = strip[:, (j - i) * TILE : (j - i + 1) * TILE]
            at += 1


def gram(rows):
    count = rows.shape[0] // TILE
    return pl.pallas_call(
        gram_kernel,
        in_specs=[VM],
        out_specs=VM,
        out_shape=jax.ShapeDtypeStruct((len(tile_pairs(count)) * TILE, TILE), F32),
        compiler_params=params(),
        name="gram",
    )(rows)


def rotate_kernel(total_rows, gram_ref, rows_ref, out_ref):
    count = rows_ref.shape[0] // TILE
    order = tile_pairs(count)
    squares = jnp.zeros((TILE, TILE), F32)
    for at, (i, j) in enumerate(order):
        tile = gram_ref[at * TILE : (at + 1) * TILE, :]
        squares = squares + tile * tile * (1.0 if i == j else 2.0)
    frob = jnp.sqrt(jnp.sum(squares, axis=(0, 1), keepdims=True) + 1e-06)
    half = 0.5 / frob
    gain = jnp.sqrt(total_rows / frob)
    rows = rows_ref[...]
    rows_hi, rows_lo = split(rows)
    for i in range(count):
        pieces = []
        for j in range(count):
            at = order.index((min(i, j), max(i, j)))
            tile = gram_ref[at * TILE : (at + 1) * TILE, :]
            pieces.append(tile if i <= j else tile.T)
        strip = jnp.concatenate(pieces, axis=1) * half
        hi, lo = split(strip)
        both = jnp.concatenate([hi, lo], axis=0)
        here = slice(i * TILE, (i + 1) * TILE)
        out_ref[here, :] = gain * (1.5 * rows[here] - dot_split(hi, both, rows_hi, rows_lo, NN))


def rotate(gram_sum, rows, total_rows):
    return pl.pallas_call(
        functools.partial(rotate_kernel, float(total_rows)),
        in_specs=[VM, VM],
        out_specs=VM,
        out_shape=jax.ShapeDtypeStruct(rows.shape, F32),
        compiler_params=params(),
        name="rotate",
    )(gram_sum, rows)


def regroup(rows):
    count, length = rows.shape
    size = lax.axis_size("wide")
    own = length // size
    parts = rows.reshape(count, size, own).transpose(1, 0, 2).reshape(size, count * own // TILE, TILE)
    parts = lax.all_to_all(parts, "wide", split_axis=0, concat_axis=0, tiled=True)
    return parts.reshape(size * count, own)


def on_device(vectors, blocks, columns, lower_bound, upper_bound):
    total_rows = vectors.shape[1] * lax.axis_size("narrow")
    rows = regroup(filtered_rows(vectors, blocks, columns, lower_bound, upper_bound))
    return rotate(all_sum(gram(rows)), rows, total_rows)


def solution(mesh):
    return jax.shard_map(
        on_device,
        mesh=mesh,
        in_specs=(P("wide", "narrow"), P("narrow", None, None, None), P("narrow", None), P(), P()),
        out_specs=P(None, ("narrow", "wide")),
        check_vma=False,
    )
```

```python
import functools

import jax
import jax.numpy as jnp
from jax import lax
from jax.experimental import pallas as pl
from jax.experimental.pallas import tpu as pltpu
from jax.sharding import PartitionSpec as P

REACH = 3
STEPS = 8
TILE = 128
VM = pl.BlockSpec(memory_space=pltpu.VMEM)
SM = pl.BlockSpec(memory_space=pltpu.SMEM)
HBM = pl.BlockSpec(memory_space=pltpu.HBM)
NT = (((1,), (1,)), ((), ()))
NN = (((1,), (0,)), ((), ()))
F32 = jnp.float32
BF16 = jnp.bfloat16


def params():
    return pltpu.CompilerParams(vmem_limit_bytes=40 * 1024 * 1024)


def split(x):
    hi = x.astype(BF16)
    return hi, (x - hi.astype(F32)).astype(BF16)


def in_hbm(x):
    return pltpu.with_memory_space_constraint(x, pltpu.HBM)


def odd_device():
    return lax.rem(lax.axis_index("narrow"), 2) == 1


def dot(a, b, dims):
    return lax.dot_general(a, b, dims, preferred_element_type=F32)


def dot_split(a_hi, a_both, b_hi, b_lo, dims):
    rows = a_hi.shape[0]
    upper = dot(a_both, b_hi, dims)
    return upper[:rows] + (upper[rows:] + dot(a_hi, b_lo, dims))


def spread_kernel(total_blocks, columns_hbm, vectors_hbm, blocks_hbm, far_ref, near_ref, vectors_ref, hi_ref, lo_ref, held, columns_ref, sems, row_sems):
    rows, slots, size, _ = blocks_hbm.shape
    edge = far_ref.shape[1]
    begin = vectors_hbm.shape[1] - edge
    odd = odd_device()

    def edge_at(at):
        return vectors_hbm.at[:, pl.ds(pl.multiple_of(at, size), edge)]

    small = [
        (columns_hbm, columns_ref),
        (edge_at(jnp.where(odd, begin, 0)), far_ref),
        (edge_at(jnp.where(odd, 0, begin)), near_ref),
        (vectors_hbm, vectors_ref),
    ]
    small = [pltpu.make_async_copy(here, there, sems.at[k]) for k, (here, there) in enumerate(small)]
    large = [pltpu.make_async_copy(blocks_hbm.at[row], held.at[row], row_sems.at[row]) for row in range(rows)]
    for copy in small[:1] + large + small[1:]:
        copy.start()
    hi_ref[...] = jnp.zeros_like(hi_ref)
    lo_ref[...] = jnp.zeros_like(lo_ref)
    first = lax.axis_index("narrow") * rows
    small[0].wait()
    for row in range(rows):
        large[row].wait()
        pair, half = divmod(row, 2)
        here = slice(half * size, half * size + size)
        for slot in range(slots):
            place = columns_ref[slot, row] - first + REACH
            place = jnp.where(place < 0, place + total_blocks, place)
            place = jnp.where(place >= total_blocks, place - total_blocks, place) - 2 * pair
            hi, lo = split(held[row, slot])
            there = pl.ds(pl.multiple_of(place * size, size), size)
            hi_ref[pair, here, there] = hi
            lo_ref[pair, here, there] = lo
    for copy in small[1:]:
        copy.wait()


def spread_part(columns, vectors, blocks, total_blocks):
    rows, slots, size, _ = blocks.shape
    spread = jax.ShapeDtypeStruct((rows // 2, 2 * size, (2 * REACH + 2) * size), BF16)
    edge = jax.ShapeDtypeStruct((vectors.shape[0], REACH * size), F32)
    return pl.pallas_call(
        functools.partial(spread_kernel, total_blocks),
        in_specs=[HBM, HBM, HBM],
        out_specs=[VM] * 5,
        out_shape=[edge, edge, jax.ShapeDtypeStruct(vectors.shape, F32), spread, spread],
        scratch_shapes=[
            pltpu.VMEM(blocks.shape, F32),
            pltpu.SMEM((slots, rows), jnp.int32),
            pltpu.SemaphoreType.DMA((4,)),
            pltpu.SemaphoreType.DMA((rows,)),
        ],
        compiler_params=params(),
        name="spread_part",
    )(in_hbm(columns.T), in_hbm(vectors), in_hbm(blocks))


def local_sum(pair, hi, both, hi_ref, lo_ref):
    pairs, width, window = hi_ref.shape
    size = width // 2
    start = 2 * pair - REACH
    begin, end = max(start, 0), min(start + window // size, 2 * pairs)
    there = slice(begin * size, end * size)
    inside = slice((begin - start) * size, (end - start) * size)
    return dot_split(hi[:, there], both[:, there], hi_ref[pair, :, inside], lo_ref[pair, :, inside], NT)


def local_kernel(first_step, terms_ref, mid_ref, *refs):
    if first_step:
        hi_ref, lo_ref, out_ref = refs
        current = mid_ref[...]
    else:
        far_ref, near_ref, previous_ref, hi_ref, lo_ref, out_ref, *full_ref = refs
        edge = far_ref.shape[1]
        odd = odd_device()
        left = jnp.where(odd, near_ref[...], far_ref[...])
        right = jnp.where(odd, far_ref[...], near_ref[...])
        current = jnp.concatenate([left, mid_ref[:, edge:-edge], right], axis=1)
        if full_ref:
            full_ref[0][...] = current
    pairs, width, _ = hi_ref.shape
    scale, diag = terms_ref[0:1, :], terms_ref[1:2, :]
    hi, lo = split(current)
    both = jnp.concatenate([hi, lo], axis=0)
    for pair in range(pairs):
        here = slice(pair * width, pair * width + width)
        total = scale * local_sum(pair, hi, both, hi_ref, lo_ref) + diag * current[:, here]
        out_ref[:, here] = 0.5 * total if first_step else total - previous_ref[:, here]


def local_part(terms, state, previous, operator, last):
    mid = state[0]
    shape = jax.ShapeDtypeStruct(mid.shape, F32)
    width = operator[0].shape[1]
    first_step = previous is None
    operands = (terms, *state, *(() if first_step else (previous,)), *operator)
    outs = 1 if first_step or last else 2
    return pl.pallas_call(
        functools.partial(local_kernel, first_step),
        in_specs=[VM] * len(operands),
        out_specs=[VM] * outs,
        out_shape=[shape] * outs,
        compiler_params=params(),
        cost_estimate=pl.CostEstimate(flops=24 * mid.size * width, bytes_accessed=8 * mid.size, transcendentals=0),
        name="local_part",
    )(*operands)


def edge_sum(factor, at_right, terms_ref, mid_ref, halo_ref, hi_ref, lo_ref):
    pairs, width, window = hi_ref.shape
    size = width // 2
    edge = REACH * size
    hi, lo = split(halo_ref[...])
    both = jnp.concatenate([hi, lo], axis=0)

    def reach_into(pair, length, hi, both):
        inside = pl.ds(pl.multiple_of(jnp.where(at_right, window - length, 0), size), length)
        return dot_split(hi, both, hi_ref[pair, :, inside], lo_ref[pair, :, inside], NT)

    outer = reach_into(jnp.where(at_right, pairs - 1, 0), edge, hi, both)
    close_hi = jnp.where(at_right, hi[:, :size], hi[:, -size:])
    close_both = jnp.where(at_right, both[:, :size], both[:, -size:])
    inner = reach_into(jnp.where(at_right, pairs - 2, 1), size, close_hi, close_both)
    added = jnp.where(
        at_right,
        jnp.concatenate([inner[:, size:], outer], axis=1),
        jnp.concatenate([outer, inner[:, :size]], axis=1),
    )
    here = pl.ds(pl.multiple_of(jnp.where(at_right, mid_ref.shape[1] - edge, 0), size), edge)
    return mid_ref[:, here] + (factor * terms_ref[0:1, 0:1]) * added


def edge_kernel(factor, far, terms_ref, mid_ref, halo_ref, hi_ref, lo_ref, out_ref):
    at_right = odd_device() if far else jnp.logical_not(odd_device())
    out_ref[...] = edge_sum(factor, at_right, terms_ref, mid_ref, halo_ref, hi_ref, lo_ref)


def edge_part(factor, far, terms, mid, halo, operator):
    width = operator[0].shape[1]
    return pl.pallas_call(
        functools.partial(edge_kernel, factor, far),
        in_specs=[VM] * 5,
        out_specs=VM,
        out_shape=jax.ShapeDtypeStruct(halo.shape, F32),
        compiler_params=params(),
        cost_estimate=pl.CostEstimate(flops=12 * halo.size * width, bytes_accessed=8 * halo.size, transcendentals=0),
        name="far_part" if far else "near_part",
    )(terms, mid, halo, *operator)


def packs(count, own):
    return own % TILE == TILE // 2 and own > TILE and count % 16 == 0


def last_kernel(parts, terms_ref, mid_ref, far_ref, near_ref, hi_ref, lo_ref, out_ref):
    odd = odd_device()
    far = edge_sum(1.0, odd, terms_ref, mid_ref, far_ref, hi_ref, lo_ref)
    near = near_ref[...]
    edge = far.shape[1]
    left, right = jnp.where(odd, near, far), jnp.where(odd, far, near)
    whole = jnp.concatenate([left, mid_ref[:, edge:-edge], right], axis=1)
    if out_ref.ndim == 2:
        out_ref[...] = whole
        return
    count, own, half = whole.shape[0], whole.shape[1] // parts, TILE // 2
    for part in range(parts):
        begin = part * own
        head, tail = (begin, begin + own - half) if part % 2 == 0 else (begin + half, begin)
        at = 0
        for column in range(head, head + own - half, TILE):
            out_ref[part, at : at + count, :] = whole[:, column : column + TILE]
            at += count
        tails = whole[:, tail : tail + half]
        out_ref[part, at:, :] = jnp.concatenate([tails[: count // 2], tails[count // 2 :]], axis=1)


def last_part(terms, mid, far, near, operator, parts):
    count, length = mid.shape
    shape = (parts, count * length // parts // TILE, TILE) if packs(count, length // parts) else mid.shape
    return pl.pallas_call(
        functools.partial(last_kernel, parts),
        in_specs=[VM] * 6,
        out_specs=VM,
        out_shape=jax.ShapeDtypeStruct(shape, F32),
        compiler_params=params(),
        name="last_part",
    )(terms, mid, far, near, *operator)


def exchange(far, near):
    size = lax.axis_size("narrow")
    far_pairs = [(i, (i + 1) % size if i % 2 else (i - 1) % size) for i in range(size)]
    near_pairs = [(i, i ^ 1) for i in range(size)]
    return lax.ppermute(far, "narrow", far_pairs), lax.ppermute(near, "narrow", near_pairs)


def filtered_parts(vectors, blocks, columns, lower_bound, upper_bound):
    total_blocks = blocks.shape[0] * lax.axis_size("narrow")
    width = 2 * blocks.shape[2]
    half_width = (upper_bound - lower_bound) * 0.5
    scale = 2.0 / half_width
    diag = scale * (1.0 - (upper_bound + lower_bound) * 0.5)
    terms = jnp.concatenate([jnp.broadcast_to(scale, (1, width)), jnp.broadcast_to(diag, (1, width))])
    far, near, vectors, *operator = spread_part(columns, vectors, blocks, total_blocks)
    state, previous = (vectors,), None
    for step in range(STEPS):
        far_halo, near_halo = exchange(far, near)
        mid, *full = local_part(terms, state, previous, operator, step == STEPS - 1)
        previous = full[0] if full else vectors
        factor = 0.5 if step == 0 else 1.0
        near = edge_part(factor, False, terms, mid, near_halo, operator)
        if step < STEPS - 1:
            far = edge_part(factor, True, terms, mid, far_halo, operator)
        state = (mid, far, near)
    return last_part(terms, mid, far_halo, near, operator, lax.axis_size("wide"))


def pair_perm(mask):
    narrow, wide = lax.axis_size("narrow"), lax.axis_size("wide")
    return [(n * wide + w, (n ^ mask[0]) * wide + (w ^ mask[1])) for n in range(narrow) for w in range(wide)]


def swap(x, mask):
    return lax.ppermute(x, ("narrow", "wide"), pair_perm(mask))


def bit_groups():
    narrow = [(1 << b, 0) for b in range(lax.axis_size("narrow").bit_length() - 1)]
    wide = [(0, 1 << b) for b in range(lax.axis_size("wide").bit_length() - 1)]
    rest = wide[1:] + narrow[2:]
    return [narrow[:1], narrow[1:2] + wide[:1]] + [rest[i : i + 2] for i in range(0, len(rest), 2)]


def masks(bits):
    out = []
    for d in range(1 << len(bits)):
        chosen = [b for k, b in enumerate(bits) if d >> k & 1]
        out.append((sum(b[0] for b in chosen), sum(b[1] for b in chosen)))
    return out


def place_in(bits):
    n, w = lax.axis_index("narrow"), lax.axis_index("wide")
    place = 0
    for k, b in enumerate(bits):
        bit = lax.rem(lax.div(n, b[0]), 2) if b[0] else lax.rem(lax.div(w, b[1]), 2)
        place = place + bit * (1 << k)
    return place


def relative(place, d, count):
    out = 0
    for k in range(count.bit_length() - 1):
        bit = lax.rem(lax.div(place, 1 << k), 2)
        out = out + (1 << k) * (1 - bit if d >> k & 1 else bit)
    return out


def chunk_at(place, d, count, rows):
    return pl.ds(pl.multiple_of(relative(place, d, count) * rows, 8), rows)


def fold_kernel(bits, *refs):
    count = 1 << len(bits)
    parts, outs = refs[:-count], refs[-count:]
    place = place_in(bits)
    rows = outs[0].shape[0]
    for d in range(count):
        here = chunk_at(place, d, count, rows)
        total = parts[0][here, :]
        for part in parts[1:]:
            total = total + part[here, :]
        outs[d][...] = total


def fold(parts, bits):
    count = 1 << len(bits)
    rows, width = parts[0].shape
    return pl.pallas_call(
        functools.partial(fold_kernel, bits),
        in_specs=[VM] * len(parts),
        out_specs=[VM] * count,
        out_shape=[jax.ShapeDtypeStruct((rows // count, width), F32)] * count,
        compiler_params=params(),
        name="fold",
    )(*parts)


def fan(parts, bits):
    members = masks(bits)
    got = {d: swap(parts[d], members[d]) for d in reversed(range(1, len(members)))}
    return [parts[0]] + [got[d] for d in range(1, len(members))]


def all_sum(halves):
    groups = bit_groups()
    parts = fan(halves, groups[0])
    for bits in groups[1:-1]:
        parts = fan(fold(parts, bits), bits)
    x = sum(parts)
    x = sum(fan([x] * (1 << len(groups[-1])), groups[-1]))
    for bits in groups[1:-1][::-1]:
        blocks = fan([x] * (1 << len(bits)), bits)
        x = jnp.concatenate(blocks)
    return x, swap(x, masks(groups[0])[1])


def sum_order():
    groups = bit_groups()
    return groups[1:-1]


def tile_pairs(count):
    return [(i, j) for i in range(count) for j in range(i + 1, count)]


def packed_rows(count):
    rows = len(tile_pairs(count)) * TILE + count * TILE // 2 + count // 2 * TILE // 2
    blocks = 8
    for bits in bit_groups()[:-1]:
        blocks <<= len(bits)
    return -(-rows // blocks) * blocks


def gram_kernel(own, parts_ref, keep_ref, send_ref, rows_ref, packed):
    if parts_ref.ndim == 2:
        rows = parts_ref[...]
    else:
        parts, length, _ = parts_ref.shape
        count, half = length * TILE // own, TILE // 2
        heads = (own - half) // TILE
        odd = lax.rem(lax.axis_index("wide"), 2) == 1
        pieces = []
        for part in range(parts):
            head = [parts_ref[part, h * count : (h + 1) * count, :] for h in range(heads)]
            tails = parts_ref[part, heads * count :, :]
            swapped = pltpu.roll(tails, half, 1)
            low = lax.broadcasted_iota(jnp.int32, tails.shape, 1) < half
            tail = jnp.concatenate([jnp.where(low, tails, swapped), jnp.where(low, swapped, tails)], axis=0)
            whole = jnp.concatenate(head + [tail], axis=1)
            pieces.append(jnp.where(odd, pltpu.roll(whole, half, 1), whole)[:, :own])
        rows = jnp.concatenate(pieces, axis=0)
    rows_ref[...] = rows.T
    tiles, half = rows.shape[0] // TILE, TILE // 2
    hi, lo = split(rows)
    at, tops = 0, len(tile_pairs(tiles)) * TILE
    lasts = tops + tiles * half
    for i in range(tiles):
        here, there = slice(i * TILE, (i + 1) * TILE), slice(i * TILE, None)
        both = jnp.concatenate([hi[here], lo[here]], axis=0)
        strip = dot_split(hi[here], both, hi[there], lo[there], NT)
        packed[tops + i * half : tops + (i + 1) * half, :] = strip[:half, :TILE]
        last = strip[half:, half:TILE]
        if i % 2 == 0:
            held = last
        else:
            packed[lasts + i // 2 * half : lasts + (i // 2 + 1) * half, :] = jnp.concatenate([held, last], axis=1)
        for j in range(i + 1, tiles):
            packed[at : at + TILE, :] = strip[:, (j - i) * TILE : (j - i + 1) * TILE]
            at += TILE
    used = lasts + tiles // 2 * half
    if used < packed.shape[0]:
        packed[used:, :] = jnp.zeros((packed.shape[0] - used, TILE), F32)
    odd, size = odd_device(), keep_ref.shape[0]
    keep_ref[...] = packed[pl.ds(pl.multiple_of(jnp.where(odd, size, 0), 8), size), :]
    send_ref[...] = packed[pl.ds(pl.multiple_of(jnp.where(odd, 0, size), 8), size), :]


def gram(parts, own):
    total = parts.size // own
    size = packed_rows(total // TILE)
    half = jax.ShapeDtypeStruct((size // 2, TILE), F32)
    return pl.pallas_call(
        functools.partial(gram_kernel, own),
        in_specs=[VM],
        out_specs=[VM] * 3,
        out_shape=[half, half, jax.ShapeDtypeStruct((own, total), F32)],
        scratch_shapes=[pltpu.VMEM((size, TILE), F32)],
        compiler_params=params(),
        name="gram",
    )(parts)


def rotate_kernel(total_rows, groups, own_ref, other_ref, rows_ref, out_ref, packed, hi_ref, lo_ref, held, sems):
    size = own_ref.shape[0]
    places = [place_in(bits) for bits in groups]
    blocks = 1
    for bits in groups:
        blocks <<= len(bits)
    length = size // blocks
    odd = odd_device()
    for block in range(blocks):
        at, rest, step = 0, block, blocks
        for bits, place in zip(groups, places):
            count = 1 << len(bits)
            step //= count
            at = at + relative(place, rest // step, count) * (step * length)
            rest %= step
        here = slice(block * length, (block + 1) * length)
        packed[pl.ds(pl.multiple_of(jnp.where(odd, size, 0) + at, 8), length), :] = own_ref[here, :]
        packed[pl.ds(pl.multiple_of(jnp.where(odd, 0, size) + at, 8), length), :] = other_ref[here, :]
    tiles, half = rows_ref.shape[1] // TILE, TILE // 2
    order = tile_pairs(tiles)
    tops = len(order) * TILE
    lasts = tops + tiles * half
    above = packed[:tops, :].reshape(len(order), TILE, TILE)
    squares = jnp.sum(above * above, axis=0) * 2.0
    top = packed[tops:lasts, :].reshape(tiles, half, TILE)
    weight = jnp.where(lax.broadcasted_iota(jnp.int32, (half, TILE), 1) < half, 1.0, 2.0)
    last = packed[lasts : lasts + tiles // 2 * half, :].reshape(tiles // 2, half, TILE)
    squares = squares[:half] + squares[half:] + jnp.sum(top * top, axis=0) * weight + jnp.sum(last * last, axis=0)
    frob = jnp.sqrt(jnp.sum(squares, axis=(0, 1), keepdims=True) + 1e-06)
    factor = 0.5 / frob
    gain = jnp.sqrt(total_rows / frob)
    for at, (i, j) in enumerate(order):
        hi, lo = split(packed[at * TILE : (at + 1) * TILE, :] * factor)
        one, two = slice(i * TILE, (i + 1) * TILE), slice(j * TILE, (j + 1) * TILE)
        hi_ref[one, two] = hi
        lo_ref[one, two] = lo
        hi_ref[two, one] = hi.T
        lo_ref[two, one] = lo.T
    for i in range(tiles):
        upper = packed[tops + i * half : tops + (i + 1) * half, :]
        quarter = packed[lasts + i // 2 * half : lasts + (i // 2 + 1) * half, :][:, i % 2 * half : (i % 2 + 1) * half]
        lower = jnp.concatenate([upper[:, half:].T, quarter], axis=1)
        hi, lo = split(jnp.concatenate([upper, lower], axis=0) * factor)
        one = slice(i * TILE, (i + 1) * TILE)
        hi_ref[one, one] = hi
        lo_ref[one, one] = lo
    rows = rows_ref[...]
    rows_hi, rows_lo = split(rows)
    both = jnp.concatenate([rows_hi, rows_lo], axis=0)
    copies = []
    for strip in range(tiles // 2):
        here = slice(strip * 2 * TILE, (strip + 1) * 2 * TILE)
        turned = dot_split(rows_hi, both, hi_ref[:, here], lo_ref[:, here], NN)
        held[:, here] = gain * (1.5 * rows[:, here] - turned)
        copies.append(pltpu.make_async_copy(held.at[:, here], out_ref.at[:, here], sems.at[strip]))
        copies[-1].start()
    for copy in copies:
        copy.wait()


def rotate(halves, rows, total_rows):
    own, total = rows.shape
    return pl.pallas_call(
        functools.partial(rotate_kernel, float(total_rows), sum_order()),
        in_specs=[VM, VM, VM],
        out_specs=HBM,
        out_shape=pltpu.HBM(rows.shape, F32),
        scratch_shapes=[
            pltpu.VMEM((packed_rows(total // TILE), TILE), F32),
            pltpu.VMEM((total, total), BF16),
            pltpu.VMEM((total, total), BF16),
            pltpu.VMEM(rows.shape, F32),
            pltpu.SemaphoreType.DMA((total // TILE // 2,)),
        ],
        compiler_params=params(),
        name="rotate",
    )(*halves, rows).T


def regroup(parts):
    size = lax.axis_size("wide")
    if parts.ndim == 3:
        return lax.all_to_all(parts, "wide", split_axis=0, concat_axis=0, tiled=True)
    count, length = parts.shape
    own = length // size
    parts = parts.reshape(count, size, own).transpose(1, 0, 2).reshape(size, count * own // TILE, TILE)
    parts = lax.all_to_all(parts, "wide", split_axis=0, concat_axis=0, tiled=True)
    return parts.reshape(size * count, own)


def on_device(vectors, blocks, columns, lower_bound, upper_bound):
    length = vectors.shape[1]
    parts = regroup(filtered_parts(vectors, blocks, columns, lower_bound, upper_bound))
    *halves, rows = gram(parts, length // lax.axis_size("wide"))
    return rotate(all_sum(halves), rows, length * lax.axis_size("narrow"))


def solution(mesh):
    return jax.shard_map(
        on_device,
        mesh=mesh,
        in_specs=(P("wide", "narrow"), P("narrow", None, None, None), P("narrow", None), P(), P()),
        out_specs=P(None, ("narrow", "wide")),
        check_vma=False,
    )
```

```python
import functools

import jax
import jax.numpy as jnp
from jax import lax
from jax.experimental import pallas as pl
from jax.experimental.pallas import tpu as pltpu
from jax.sharding import PartitionSpec as P

REACH = 3
CROSS_PARTS = 4
STEPS = 8
TILE = 128
VM = pl.BlockSpec(memory_space=pltpu.VMEM)
SM = pl.BlockSpec(memory_space=pltpu.SMEM)
HBM = pl.BlockSpec(memory_space=pltpu.HBM)
NT = (((1,), (1,)), ((), ()))
NN = (((1,), (0,)), ((), ()))
F32 = jnp.float32
BF16 = jnp.bfloat16


def params():
    return pltpu.CompilerParams(vmem_limit_bytes=40 * 1024 * 1024)


def split(x):
    hi = x.astype(BF16)
    return hi, (x - hi.astype(F32)).astype(BF16)


def in_hbm(x):
    return pltpu.with_memory_space_constraint(x, pltpu.HBM)


def odd_place(axis):
    return lax.rem(lax.axis_index(axis), 2) == 1


def odd_device():
    return odd_place("narrow")


def dot(a, b, dims):
    return lax.dot_general(a, b, dims, preferred_element_type=F32)


def dot_split(a_hi, a_both, b_hi, b_lo, dims):
    rows = a_hi.shape[0]
    upper = dot(a_both, b_hi, dims)
    return upper[:rows] + (upper[rows:] + dot(a_hi, b_lo, dims))


def cross_at(row, place):
    return sum(REACH - r for r in range(row)) + place + REACH - row


def spread_kernel(total_blocks, columns_hbm, vectors_hbm, blocks_hbm, far_ref, near_ref, vectors_ref, part_ref, hi_ref, lo_ref, held, cross_ref, columns_ref, sem, vector_sems, row_sems):
    rows, slots, size, _ = blocks_hbm.shape
    edge = far_ref.shape[1]
    odd = odd_device()
    source = [jnp.where(odd, rows - 1 - row, row) for row in range(rows)]
    copies = [pltpu.make_async_copy(columns_hbm, columns_ref, sem)]
    for row in range(rows):
        here = vectors_hbm.at[:, pl.ds(pl.multiple_of(source[row] * size, size), size)]
        copies.append(pltpu.make_async_copy(here, vectors_ref.at[:, pl.ds(row * size, size)], vector_sems.at[row]))
    large = [pltpu.make_async_copy(blocks_hbm.at[source[row]], held.at[row], row_sems.at[row]) for row in range(rows)]
    for copy in copies + large:
        copy.start()
    hi_ref[...] = jnp.zeros_like(hi_ref)
    lo_ref[...] = jnp.zeros_like(lo_ref)
    cross_ref[...] = jnp.zeros_like(cross_ref)
    first = lax.axis_index("narrow") * rows
    copies[0].wait()
    for row in range(rows):
        large[row].wait()
        pair, half = divmod(row, 2)
        here = slice(half * size, half * size + size)
        for slot in range(slots):
            offset = columns_ref[slot, source[row]] - (first + source[row])
            offset = jnp.where(offset > REACH, offset - total_blocks, offset)
            offset = jnp.where(offset < -REACH, offset + total_blocks, offset)
            offset = jnp.where(odd, -offset, offset)
            hi, lo = split(held[row, slot])
            there = pl.ds(pl.multiple_of((half + offset + REACH) * size, size), size)
            hi_ref[pair, here, there] = hi
            lo_ref[pair, here, there] = lo
            if row < REACH:

                @pl.when(row + offset < 0)
                def _():
                    at = pl.multiple_of(cross_at(row, row + offset) * size, size)
                    cross_ref[pl.ds(at, size), :] = held[row, slot]

    count = part_ref.shape[0]
    part_ref[...] = cross_ref[pl.ds(pl.multiple_of(lax.rem(lax.axis_index("wide"), CROSS_PARTS) * count, 8), count), :]
    for copy in copies[1:]:
        copy.wait()
    far_ref[...] = vectors_ref[:, :edge]
    near_ref[...] = vectors_ref[:, -edge:]


def spread_part(columns, vectors, blocks, total_blocks):
    rows, slots, size, _ = blocks.shape
    spread = jax.ShapeDtypeStruct((rows // 2, 2 * size, (2 * REACH + 2) * size), BF16)
    edge = jax.ShapeDtypeStruct((vectors.shape[0], REACH * size), F32)
    crossing = REACH * (REACH + 1) // 2 * size
    cross = jax.ShapeDtypeStruct((crossing // CROSS_PARTS, size), F32)
    return pl.pallas_call(
        functools.partial(spread_kernel, total_blocks),
        in_specs=[HBM, HBM, HBM],
        out_specs=[VM] * 6,
        out_shape=[edge, edge, jax.ShapeDtypeStruct(vectors.shape, F32), cross, spread, spread],
        scratch_shapes=[
            pltpu.VMEM(blocks.shape, F32),
            pltpu.VMEM((crossing, size), F32),
            pltpu.SMEM((slots, rows), jnp.int32),
            pltpu.SemaphoreType.DMA,
            pltpu.SemaphoreType.DMA((rows,)),
            pltpu.SemaphoreType.DMA((rows,)),
        ],
        compiler_params=params(),
        name="spread_part",
    )(in_hbm(columns.T), in_hbm(vectors), in_hbm(blocks))


class Strip:
    def __init__(self, values, at, size):
        self.hi, lo = split(values)
        self.both = jnp.concatenate([self.hi, lo], axis=0)
        self.at, self.size = at, size

    def band(self, operator, pair, begin, end):
        hi_ref, lo_ref = operator
        size, start = self.size, 2 * pair - REACH
        there = slice((begin - self.at) * size, (end - self.at) * size)
        inside = slice((begin - start) * size, (end - start) * size)
        return dot_split(self.hi[:, there], self.both[:, there], hi_ref[pair, :, inside], lo_ref[pair, :, inside], NT)


def reversed_blocks(edge, size):
    return [edge[:, k * size : (k + 1) * size] for k in reversed(range(edge.shape[1] // size))]


def far_sum(operator, halo, size):
    strip = Strip(jnp.concatenate(reversed_blocks(halo, size), axis=1), -REACH, size)
    outer = strip.band(operator, 0, -REACH, 0)
    inner = strip.band(operator, 1, -1, 0)
    return jnp.concatenate([outer, inner[:, :size]], axis=1)


def near_sum(operator, halo, size):
    pairs = operator[0].shape[0]
    strip = Strip(jnp.concatenate(reversed_blocks(halo, size), axis=1), 2 * pairs, size)
    outer = strip.band(operator, pairs - 1, 2 * pairs, 2 * pairs + REACH)
    inner = strip.band(operator, pairs - 2, 2 * pairs, 2 * pairs + 1)
    return jnp.concatenate([inner[:, size:], outer], axis=1)


def own_sum(operator, strip, pair, lowest=0):
    pairs = operator[0].shape[0]
    return strip.band(operator, pair, max(2 * pair - REACH, lowest), min(2 * pair + REACH + 2, 2 * pairs))


def first_kernel(terms_ref, vectors_ref, hi_ref, lo_ref, out_ref):
    pairs, width, _ = hi_ref.shape
    scale, diag = terms_ref[0:1, :], terms_ref[1:2, :]
    strip = Strip(vectors_ref[...], 0, width // 2)
    for pair in range(pairs):
        here = slice(pair * width, pair * width + width)
        total = scale * own_sum((hi_ref, lo_ref), strip, pair) + diag * vectors_ref[:, here]
        out_ref[:, here] = 0.5 * total


def local_kernel(first_pair, terms_ref, far_ref, mid_ref, near_ref, far_before_ref, mid_before_ref, near_before_ref, hi_ref, lo_ref, out_ref, *full_ref):
    pairs, width, _ = hi_ref.shape
    edge, start = near_ref.shape[1], far_ref.shape[1]
    scale, diag = terms_ref[0:1, :], terms_ref[1:2, :]
    current = jnp.concatenate([far_ref[...], mid_ref[:, start:-edge], near_ref[...]], axis=1)
    before = jnp.concatenate([far_before_ref[...], mid_before_ref[:, edge:-edge], near_before_ref[...]], axis=1)
    if full_ref:
        full_ref[0][...] = current
    strip = Strip(current, 0, width // 2)
    for pair in range(first_pair, pairs):
        here = slice(pair * width, pair * width + width)
        total = scale * own_sum((hi_ref, lo_ref), strip, pair) + diag * current[:, here]
        out_ref[:, here] = total - before[:, here]


def second_kernel(terms_ref, mid_ref, near_ref, before_ref, hi_ref, lo_ref, out_ref):
    pairs, width, _ = hi_ref.shape
    edge = near_ref.shape[1]
    scale, diag = terms_ref[0:1, :], terms_ref[1:2, :]
    current = jnp.concatenate([mid_ref[:, edge:-edge], near_ref[...]], axis=1)
    padded = jnp.concatenate([jnp.zeros(near_ref.shape, F32), current], axis=1)
    strip = Strip(current, REACH, width // 2)
    for pair in range(pairs):
        here = slice(pair * width, pair * width + width)
        total = scale * own_sum((hi_ref, lo_ref), strip, pair, REACH) + diag * padded[:, here]
        out_ref[:, here] = total - before_ref[:, here]


def step_call(kernel, name, operands, operator, outs):
    size = operands[1].size
    width = operator[0].shape[1]
    return pl.pallas_call(
        kernel,
        in_specs=[VM] * (len(operands) + 2),
        out_specs=[VM] * len(outs),
        out_shape=[jax.ShapeDtypeStruct(shape, F32) for shape in outs],
        compiler_params=params(),
        cost_estimate=pl.CostEstimate(flops=24 * size * width, bytes_accessed=8 * size, transcendentals=0),
        name=name,
    )(*operands, *operator)


def near_kernel(factor, terms_ref, mid_ref, halo_ref, hi_ref, lo_ref, out_ref):
    size, edge = hi_ref.shape[1] // 2, halo_ref.shape[1]
    scale = factor * terms_ref[0:1, 0:1]
    out_ref[...] = mid_ref[:, -edge:] + scale * near_sum((hi_ref, lo_ref), halo_ref[...], size)


def edge_ahead(operator, scale, diag, far, before, size):
    strip = Strip(far, 0, size)
    outer = strip.band(operator, 0, 0, REACH + 2)
    inner = strip.band(operator, 1, 0, 2 * REACH)
    total = jnp.concatenate([outer, inner[:, :size]], axis=1)
    return scale * total + diag * far[:, : total.shape[1]] - before


def far_kernel(terms_ref, mid_ref, halo_ref, hi_ref, lo_ref, far_ref):
    size, edge = hi_ref.shape[1] // 2, halo_ref.shape[1]
    far_ref[...] = mid_ref[:, :edge] + 0.5 * terms_ref[0:1, 0:1] * far_sum((hi_ref, lo_ref), halo_ref[...], size)


def turn_one_kernel(terms_ref, mid_ref, halo_ref, before_ref, hi_ref, lo_ref, far_ref, send_ref):
    operator = (hi_ref, lo_ref)
    size, edge = hi_ref.shape[1] // 2, halo_ref.shape[1]
    scale, diag = terms_ref[0:1, 0:1], terms_ref[1:2, 0:1]
    edge_rows = mid_ref[:, :edge] + scale * far_sum(operator, halo_ref[...], size)
    far = jnp.concatenate([edge_rows, mid_ref[:, edge : 2 * edge]], axis=1)
    far_ref[...] = far
    send_ref[0] = edge_rows
    send_ref[1] = edge_ahead(operator, scale, diag, far, before_ref[...], size)


def turn(terms_ref, mid_ref, sent_ref, got_ref, cross_hi_ref, cross_lo_ref, operator):
    size, edge = operator[0].shape[1] // 2, sent_ref.shape[2]
    scale, diag = terms_ref[0:1, 0:1], terms_ref[1:2, 0:1]
    between = sent_ref[1] + scale * far_sum(operator, got_ref[0], size)
    def cross(ref, row):
        rows = [slice(at * size, (at + 1) * size) for at in (cross_at(row, -1 - place) for place in range(REACH - row))]
        return jnp.concatenate([ref[here, :] for here in rows], axis=1)

    own = Strip(sent_ref[0], 0, size)
    pieces = []
    for row in range(REACH):
        there = slice(0, (REACH - row) * size)
        hi, lo = cross(cross_hi_ref, row), cross(cross_lo_ref, row)
        pieces.append(dot_split(own.hi[:, there], own.both[:, there], hi, lo, NT))
    beyond = got_ref[1] + scale * jnp.concatenate(pieces, axis=1)
    strip = Strip(jnp.concatenate(reversed_blocks(beyond, size) + [between], axis=1), -REACH, size)
    total = [strip.band(operator, pair, 2 * pair - REACH, REACH) for pair in range(REACH)]
    known = jnp.concatenate([diag * between, jnp.zeros_like(between)], axis=1)
    return between, mid_ref[:, : 2 * edge] + scale * jnp.concatenate(total, axis=1) + known


def cross_kernel(mine_ref, one_ref, two_ref, hi_ref, lo_ref):
    rows = mine_ref.shape[0]
    place = lax.rem(lax.axis_index("wide"), CROSS_PARTS)
    for d, part in enumerate([mine_ref[...], one_ref[...], two_ref[:rows, :], two_ref[rows:, :]]):
        here = chunk_at(place, d, CROSS_PARTS, rows)
        hi, lo = split(part)
        hi_ref[here, :] = hi
        lo_ref[here, :] = lo


def cross_part(mine):
    one = wide_swap(mine, 1)
    two = wide_swap(jnp.concatenate([mine, one]), 2)
    rows, width = mine.shape
    return pl.pallas_call(
        cross_kernel,
        in_specs=[VM] * 3,
        out_specs=[VM] * 2,
        out_shape=[jax.ShapeDtypeStruct((CROSS_PARTS * rows, width), BF16)] * 2,
        compiler_params=params(),
        name="cross_part",
    )(mine, one, two)


def turn_two_kernel(terms_ref, mid_ref, sent_ref, got_ref, cross_hi_ref, cross_lo_ref, hi_ref, lo_ref, between_ref, far_ref, send_ref):
    operator = (hi_ref, lo_ref)
    size, edge = hi_ref.shape[1] // 2, between_ref.shape[1]
    between, far = turn(terms_ref, mid_ref, sent_ref, got_ref, cross_hi_ref, cross_lo_ref, operator)
    between_ref[...] = between
    far_ref[...] = far
    send_ref[0] = far[:, :edge]
    send_ref[1] = edge_ahead(operator, terms_ref[0:1, 0:1], terms_ref[1:2, 0:1], far, between, size)


def packs(count, own):
    return own % TILE == TILE // 2 and own > TILE and count % 16 == 0


def last_kernel(parts, terms_ref, mid_ref, sent_ref, got_ref, cross_hi_ref, cross_lo_ref, near_ref, hi_ref, lo_ref, out_ref):
    size = hi_ref.shape[1] // 2
    _, far = turn(terms_ref, mid_ref, sent_ref, got_ref, cross_hi_ref, cross_lo_ref, (hi_ref, lo_ref))
    whole = jnp.concatenate([far, mid_ref[:, far.shape[1] : -near_ref.shape[1]], near_ref[...]], axis=1)
    mirrored = jnp.concatenate(reversed_blocks(whole, size), axis=1)
    whole = jnp.where(odd_device(), mirrored, whole)
    if len(out_ref.shape) == 2:
        out_ref[...] = whole
        return
    count, own, half = whole.shape[0], whole.shape[1] // parts, TILE // 2
    for part in range(parts):
        begin = part * own
        head, tail = (begin, begin + own - half) if part % 2 == 0 else (begin + half, begin)
        at = 0
        for column in range(head, head + own - half, TILE):
            out_ref[part, at : at + count, :] = whole[:, column : column + TILE]
            at += count
        tails = whole[:, tail : tail + half]
        out_ref[part, at:, :] = jnp.concatenate([tails[: count // 2], tails[count // 2 :]], axis=1)


def far_swap(x):
    size = lax.axis_size("narrow")
    return lax.ppermute(x, "narrow", [(i, (i + 1) % size if i % 2 else (i - 1) % size) for i in range(size)])


def wide_swap(x, mask):
    return lax.ppermute(x, "wide", [(i, i ^ mask) for i in range(lax.axis_size("wide"))])


def near_swap(x):
    return lax.ppermute(x, "narrow", [(i, i ^ 1) for i in range(lax.axis_size("narrow"))])


def filtered_parts(vectors, blocks, columns, lower_bound, upper_bound):
    size = blocks.shape[2]
    width, edge, parts = 2 * size, REACH * size, lax.axis_size("wide")
    count, length = vectors.shape
    half_width = (upper_bound - lower_bound) * 0.5
    scale = 2.0 / half_width
    diag = scale * (1.0 - (upper_bound + lower_bound) * 0.5)
    terms = jnp.concatenate([jnp.broadcast_to(scale, (1, width)), jnp.broadcast_to(diag, (1, width))])
    total_blocks = blocks.shape[0] * lax.axis_size("narrow")
    far, near, vectors, cross, *operator = spread_part(columns, vectors, blocks, total_blocks)
    whole, side, double = (count, length), (count, edge), (2, count, edge)

    def near_part(factor, mid, halo):
        kernel = functools.partial(near_kernel, factor)
        return step_call(kernel, "near_part", (terms, mid, halo), operator, [side])[0]

    def local_part(first_pair, outs):
        kernel = functools.partial(local_kernel, first_pair)
        return step_call(kernel, "local_part", (terms, far, mid, near, *before), operator, [whole] * outs)

    halo, near_halo = far_swap(far), near_swap(near)
    cross = cross_part(far_swap(cross))
    (mid,) = step_call(first_kernel, "first_part", (terms, vectors), operator, [whole])
    before = (far, vectors, near)
    near = near_part(0.5, mid, near_halo)
    (far,) = step_call(far_kernel, "far_part", (terms, mid, halo), operator, [side])
    halo, near_halo = far_swap(far), near_swap(near)
    next_mid, _ = local_part(0, 2)
    before = (far, mid, near)
    mid, near = next_mid, near_part(1.0, next_mid, near_halo)
    far, send = step_call(turn_one_kernel, "turn_one", (terms, mid, halo, far), operator, [(count, 2 * edge), double])
    for step in range(2, STEPS, 2):
        got, near_halo = far_swap(send), near_swap(near)
        mid, full = local_part(1, 2)
        near = near_part(1.0, mid, near_halo)
        near_halo = near_swap(near)
        (next_mid,) = step_call(second_kernel, "second_part", (terms, mid, near, full), operator, [whole])
        next_near = near_part(1.0, next_mid, near_halo)
        operands = (terms, next_mid, send, got, *cross)
        if step < STEPS - 2:
            outs = [side, (count, 2 * edge), double]
            between, far, send = step_call(turn_two_kernel, "turn_two", operands, operator, outs)
            before = (between, mid, near)
        mid, near = next_mid, next_near
    shape = (parts, count * length // parts // TILE, TILE) if packs(count, length // parts) else whole
    return step_call(functools.partial(last_kernel, parts), "last_part", (*operands, near), operator, [shape])[0]


def pair_perm(mask):
    narrow, wide = lax.axis_size("narrow"), lax.axis_size("wide")
    return [(n * wide + w, (n ^ mask[0]) * wide + (w ^ mask[1])) for n in range(narrow) for w in range(wide)]


def swap(x, mask):
    return lax.ppermute(x, ("narrow", "wide"), pair_perm(mask))


def bit_groups():
    narrow = [(1 << b, 0) for b in range(lax.axis_size("narrow").bit_length() - 1)]
    wide = [(0, 1 << b) for b in range(lax.axis_size("wide").bit_length() - 1)]
    rest = wide[1:] + narrow[2:]
    return [narrow[:1], narrow[1:2] + wide[:1]] + [rest[i : i + 2] for i in range(0, len(rest), 2)]


def masks(bits):
    out = []
    for d in range(1 << len(bits)):
        chosen = [b for k, b in enumerate(bits) if d >> k & 1]
        out.append((sum(b[0] for b in chosen), sum(b[1] for b in chosen)))
    return out


def place_in(bits):
    n, w = lax.axis_index("narrow"), lax.axis_index("wide")
    place = 0
    for k, b in enumerate(bits):
        bit = lax.rem(lax.div(n, b[0]), 2) if b[0] else lax.rem(lax.div(w, b[1]), 2)
        place = place + bit * (1 << k)
    return place


def relative(place, d, count):
    out = 0
    for k in range(count.bit_length() - 1):
        bit = lax.rem(lax.div(place, 1 << k), 2)
        out = out + (1 << k) * (1 - bit if d >> k & 1 else bit)
    return out


def chunk_at(place, d, count, rows):
    return pl.ds(pl.multiple_of(relative(place, d, count) * rows, 8), rows)


def fold_kernel(bits, *refs):
    count = 1 << len(bits)
    parts, outs = refs[:-count], refs[-count:]
    place = place_in(bits)
    rows = outs[0].shape[0]
    for d in range(count):
        here = chunk_at(place, d, count, rows)
        total = parts[0][here, :]
        for part in parts[1:]:
            total = total + part[here, :]
        outs[d][...] = total


def fold(parts, bits):
    count = 1 << len(bits)
    rows, width = parts[0].shape
    return pl.pallas_call(
        functools.partial(fold_kernel, bits),
        in_specs=[VM] * len(parts),
        out_specs=[VM] * count,
        out_shape=[jax.ShapeDtypeStruct((rows // count, width), F32)] * count,
        compiler_params=params(),
        name="fold",
    )(*parts)


def fan(parts, bits):
    members = masks(bits)
    return [parts[0]] + [swap(parts[d], members[d]) for d in range(1, len(members))]


def all_sum(halves):
    groups = bit_groups()
    parts = fan(halves, groups[0])
    for bits in groups[1:-1]:
        parts = fan(fold(parts, bits), bits)
    x = sum(parts)
    x = sum(fan([x] * (1 << len(groups[-1])), groups[-1]))
    for bits in groups[1:-1][::-1]:
        blocks = fan([x] * (1 << len(bits)), bits)
        x = jnp.concatenate(blocks)
    return x, swap(x, masks(groups[0])[1])


def sum_order():
    groups = bit_groups()
    return groups[1:-1]


def tile_pairs(count):
    return [(i, j) for i in range(count) for j in range(i + 1, count)]


def packed_rows(count):
    rows = len(tile_pairs(count)) * TILE + count * TILE // 2 + count // 2 * TILE // 2
    blocks = 8
    for bits in bit_groups()[:-1]:
        blocks <<= len(bits)
    return -(-rows // blocks) * blocks


def gram_kernel(own, parts_ref, keep_ref, send_ref, rows_ref, packed):
    if parts_ref.ndim == 2:
        rows = parts_ref[...]
    else:
        parts, length, _ = parts_ref.shape
        count, half = length * TILE // own, TILE // 2
        heads = (own - half) // TILE
        odd = lax.rem(lax.axis_index("wide"), 2) == 1
        pieces = []
        for part in range(parts):
            head = [parts_ref[part, h * count : (h + 1) * count, :] for h in range(heads)]
            tails = parts_ref[part, heads * count :, :]
            swapped = pltpu.roll(tails, half, 1)
            low = lax.broadcasted_iota(jnp.int32, tails.shape, 1) < half
            tail = jnp.concatenate([jnp.where(low, tails, swapped), jnp.where(low, swapped, tails)], axis=0)
            whole = jnp.concatenate(head + [tail], axis=1)
            pieces.append(jnp.where(odd, pltpu.roll(whole, half, 1), whole)[:, :own])
        rows = jnp.concatenate(pieces, axis=0)
    rows_ref[...] = rows.T
    tiles, half = rows.shape[0] // TILE, TILE // 2
    hi, lo = split(rows)
    at, tops = 0, len(tile_pairs(tiles)) * TILE
    lasts = tops + tiles * half
    for i in range(tiles):
        here, there = slice(i * TILE, (i + 1) * TILE), slice(i * TILE, None)
        both = jnp.concatenate([hi[here], lo[here]], axis=0)
        strip = dot_split(hi[here], both, hi[there], lo[there], NT)
        packed[tops + i * half : tops + (i + 1) * half, :] = strip[:half, :TILE]
        last = strip[half:, half:TILE]
        if i % 2 == 0:
            held = last
        else:
            packed[lasts + i // 2 * half : lasts + (i // 2 + 1) * half, :] = jnp.concatenate([held, last], axis=1)
        for j in range(i + 1, tiles):
            packed[at : at + TILE, :] = strip[:, (j - i) * TILE : (j - i + 1) * TILE]
            at += TILE
    used = lasts + tiles // 2 * half
    if used < packed.shape[0]:
        packed[used:, :] = jnp.zeros((packed.shape[0] - used, TILE), F32)
    odd, size = odd_device(), keep_ref.shape[0]
    keep_ref[...] = packed[pl.ds(pl.multiple_of(jnp.where(odd, size, 0), 8), size), :]
    send_ref[...] = packed[pl.ds(pl.multiple_of(jnp.where(odd, 0, size), 8), size), :]


def gram(parts, own):
    total = parts.size // own
    size = packed_rows(total // TILE)
    half = jax.ShapeDtypeStruct((size // 2, TILE), F32)
    return pl.pallas_call(
        functools.partial(gram_kernel, own),
        in_specs=[VM],
        out_specs=[VM] * 3,
        out_shape=[half, half, jax.ShapeDtypeStruct((own, total), F32)],
        scratch_shapes=[pltpu.VMEM((size, TILE), F32)],
        compiler_params=params(),
        name="gram",
    )(parts)


def rotate_kernel(total_rows, groups, own_ref, other_ref, rows_ref, out_ref, packed, hi_ref, lo_ref, held, sems):
    size = own_ref.shape[0]
    places = [place_in(bits) for bits in groups]
    blocks = 1
    for bits in groups:
        blocks <<= len(bits)
    length = size // blocks
    odd = odd_device()
    for block in range(blocks):
        at, rest, step = 0, block, blocks
        for bits, place in zip(groups, places):
            count = 1 << len(bits)
            step //= count
            at = at + relative(place, rest // step, count) * (step * length)
            rest %= step
        here = slice(block * length, (block + 1) * length)
        packed[pl.ds(pl.multiple_of(jnp.where(odd, size, 0) + at, 8), length), :] = own_ref[here, :]
        packed[pl.ds(pl.multiple_of(jnp.where(odd, 0, size) + at, 8), length), :] = other_ref[here, :]
    tiles, half = rows_ref.shape[1] // TILE, TILE // 2
    order = tile_pairs(tiles)
    tops = len(order) * TILE
    lasts = tops + tiles * half
    above = packed[:tops, :].reshape(len(order), TILE, TILE)
    squares = jnp.sum(above * above, axis=0) * 2.0
    top = packed[tops:lasts, :].reshape(tiles, half, TILE)
    weight = jnp.where(lax.broadcasted_iota(jnp.int32, (half, TILE), 1) < half, 1.0, 2.0)
    last = packed[lasts : lasts + tiles // 2 * half, :].reshape(tiles // 2, half, TILE)
    squares = squares[:half] + squares[half:] + jnp.sum(top * top, axis=0) * weight + jnp.sum(last * last, axis=0)
    frob = jnp.sqrt(jnp.sum(squares, axis=(0, 1), keepdims=True) + 1e-06)
    factor = 0.5 / frob
    gain = jnp.sqrt(total_rows / frob)
    for at, (i, j) in enumerate(order):
        hi, lo = split(packed[at * TILE : (at + 1) * TILE, :] * factor)
        one, two = slice(i * TILE, (i + 1) * TILE), slice(j * TILE, (j + 1) * TILE)
        hi_ref[one, two] = hi
        lo_ref[one, two] = lo
        hi_ref[two, one] = hi.T
        lo_ref[two, one] = lo.T
    for i in range(tiles):
        upper = packed[tops + i * half : tops + (i + 1) * half, :]
        quarter = packed[lasts + i // 2 * half : lasts + (i // 2 + 1) * half, :][:, i % 2 * half : (i % 2 + 1) * half]
        lower = jnp.concatenate([upper[:, half:].T, quarter], axis=1)
        hi, lo = split(jnp.concatenate([upper, lower], axis=0) * factor)
        one = slice(i * TILE, (i + 1) * TILE)
        hi_ref[one, one] = hi
        lo_ref[one, one] = lo
    rows = rows_ref[...]
    rows_hi, rows_lo = split(rows)
    both = jnp.concatenate([rows_hi, rows_lo], axis=0)
    copies = []
    for strip in range(tiles // 2):
        here = slice(strip * 2 * TILE, (strip + 1) * 2 * TILE)
        turned = dot_split(rows_hi, both, hi_ref[:, here], lo_ref[:, here], NN)
        held[:, here] = gain * (1.5 * rows[:, here] - turned)
        copies.append(pltpu.make_async_copy(held.at[:, here], out_ref.at[:, here], sems.at[strip]))
        copies[-1].start()
    for copy in copies:
        copy.wait()


def rotate(halves, rows, total_rows):
    own, total = rows.shape
    return pl.pallas_call(
        functools.partial(rotate_kernel, float(total_rows), sum_order()),
        in_specs=[VM, VM, VM],
        out_specs=HBM,
        out_shape=pltpu.HBM(rows.shape, F32),
        scratch_shapes=[
            pltpu.VMEM((packed_rows(total // TILE), TILE), F32),
            pltpu.VMEM((total, total), BF16),
            pltpu.VMEM((total, total), BF16),
            pltpu.VMEM(rows.shape, F32),
            pltpu.SemaphoreType.DMA((total // TILE // 2,)),
        ],
        compiler_params=params(),
        name="rotate",
    )(*halves, rows).T


def regroup(parts):
    size = lax.axis_size("wide")
    if parts.ndim == 3:
        return lax.all_to_all(parts, "wide", split_axis=0, concat_axis=0, tiled=True)
    count, length = parts.shape
    own = length // size
    parts = parts.reshape(count, size, own).transpose(1, 0, 2).reshape(size, count * own // TILE, TILE)
    parts = lax.all_to_all(parts, "wide", split_axis=0, concat_axis=0, tiled=True)
    return parts.reshape(size * count, own)


def on_device(vectors, blocks, columns, lower_bound, upper_bound):
    length = vectors.shape[1]
    parts = regroup(filtered_parts(vectors, blocks, columns, lower_bound, upper_bound))
    *halves, rows = gram(parts, length // lax.axis_size("wide"))
    return rotate(all_sum(halves), rows, length * lax.axis_size("narrow"))


def solution(mesh):
    return jax.shard_map(
        on_device,
        mesh=mesh,
        in_specs=(P("wide", "narrow"), P("narrow", None, None, None), P("narrow", None), P(), P()),
        out_specs=P(None, ("narrow", "wide")),
        check_vma=False,
    )
```

```python
import functools

import jax
import jax.numpy as jnp
from jax import lax
from jax.experimental import pallas as pl
from jax.experimental.pallas import tpu as pltpu
from jax.sharding import PartitionSpec as P

REACH = 3
CROSS_PARTS = 4
STEPS = 8
TILE = 128
VM = pl.BlockSpec(memory_space=pltpu.VMEM)
SM = pl.BlockSpec(memory_space=pltpu.SMEM)
HBM = pl.BlockSpec(memory_space=pltpu.HBM)
NT = (((1,), (1,)), ((), ()))
NN = (((1,), (0,)), ((), ()))
F32 = jnp.float32
BF16 = jnp.bfloat16


def params():
    return pltpu.CompilerParams(vmem_limit_bytes=40 * 1024 * 1024)


def split(x):
    hi = x.astype(BF16)
    return hi, (x - hi.astype(F32)).astype(BF16)


def in_hbm(x):
    return pltpu.with_memory_space_constraint(x, pltpu.HBM)


def odd_place(axis):
    return lax.rem(lax.axis_index(axis), 2) == 1


def odd_device():
    return odd_place("narrow")


def dot(a, b, dims):
    return lax.dot_general(a, b, dims, preferred_element_type=F32)


def dot_split(a_hi, a_both, b_hi, b_lo, dims):
    rows = a_hi.shape[0]
    upper = dot(a_both, b_hi, dims)
    return upper[:rows] + (upper[rows:] + dot(a_hi, b_lo, dims))


def cross_at(row, place):
    return sum(REACH - r for r in range(row)) + place + REACH - row


def spread_kernel(total_blocks, columns_hbm, vectors_hbm, blocks_hbm, far_ref, near_ref, vectors_ref, part_ref, hi_ref, lo_ref, held, cross_ref, columns_ref, sem, vector_sems, row_sems):
    rows, slots, size, _ = blocks_hbm.shape
    edge = far_ref.shape[1]
    odd = odd_device()
    source = [jnp.where(odd, rows - 1 - row, row) for row in range(rows)]
    copies = [pltpu.make_async_copy(columns_hbm, columns_ref, sem)]
    for row in range(rows):
        here = vectors_hbm.at[:, pl.ds(pl.multiple_of(source[row] * size, size), size)]
        copies.append(pltpu.make_async_copy(here, vectors_ref.at[:, pl.ds(row * size, size)], vector_sems.at[row]))
    large = [pltpu.make_async_copy(blocks_hbm.at[source[row]], held.at[row], row_sems.at[row]) for row in range(rows)]
    for copy in copies + large:
        copy.start()
    hi_ref[...] = jnp.zeros_like(hi_ref)
    lo_ref[...] = jnp.zeros_like(lo_ref)
    cross_ref[...] = jnp.zeros_like(cross_ref)
    first = lax.axis_index("narrow") * rows
    copies[0].wait()
    for row in range(rows):
        large[row].wait()
        pair, half = divmod(row, 2)
        here = slice(half * size, half * size + size)
        for slot in range(slots):
            offset = columns_ref[slot, source[row]] - (first + source[row])
            offset = jnp.where(offset > REACH, offset - total_blocks, offset)
            offset = jnp.where(offset < -REACH, offset + total_blocks, offset)
            offset = jnp.where(odd, -offset, offset)
            hi, lo = split(held[row, slot])
            there = pl.ds(pl.multiple_of((half + offset + REACH) * size, size), size)
            hi_ref[pair, here, there] = hi
            lo_ref[pair, here, there] = lo
            if row < REACH:

                @pl.when(row + offset < 0)
                def _():
                    at = pl.multiple_of(cross_at(row, row + offset) * size, size)
                    cross_ref[pl.ds(at, size), :] = held[row, slot]

    count = part_ref.shape[0]
    part_ref[...] = cross_ref[pl.ds(pl.multiple_of(lax.rem(lax.axis_index("wide"), CROSS_PARTS) * count, 8), count), :]
    for copy in copies[1:]:
        copy.wait()
    far_ref[...] = vectors_ref[:, :edge]
    near_ref[...] = vectors_ref[:, -edge:]


def spread_part(columns, vectors, blocks, total_blocks):
    rows, slots, size, _ = blocks.shape
    spread = jax.ShapeDtypeStruct((rows // 2, 2 * size, (2 * REACH + 2) * size), BF16)
    edge = jax.ShapeDtypeStruct((vectors.shape[0], REACH * size), F32)
    crossing = REACH * (REACH + 1) // 2 * size
    cross = jax.ShapeDtypeStruct((crossing // CROSS_PARTS, size), F32)
    return pl.pallas_call(
        functools.partial(spread_kernel, total_blocks),
        in_specs=[HBM, HBM, HBM],
        out_specs=[VM] * 6,
        out_shape=[edge, edge, jax.ShapeDtypeStruct(vectors.shape, F32), cross, spread, spread],
        scratch_shapes=[
            pltpu.VMEM(blocks.shape, F32),
            pltpu.VMEM((crossing, size), F32),
            pltpu.SMEM((slots, rows), jnp.int32),
            pltpu.SemaphoreType.DMA,
            pltpu.SemaphoreType.DMA((rows,)),
            pltpu.SemaphoreType.DMA((rows,)),
        ],
        compiler_params=params(),
        name="spread_part",
    )(in_hbm(columns.T), in_hbm(vectors), in_hbm(blocks))


class Strip:
    def __init__(self, values, at, size):
        self.hi, lo = split(values)
        self.both = jnp.concatenate([self.hi, lo], axis=0)
        self.at, self.size = at, size

    def band(self, operator, pair, begin, end, half=None):
        hi_ref, lo_ref = operator
        size, start = self.size, 2 * pair - REACH
        there = slice((begin - self.at) * size, (end - self.at) * size)
        inside = slice((begin - start) * size, (end - start) * size)
        rows = slice(None) if half is None else slice(half * size, (half + 1) * size)
        hi, lo = hi_ref[pair, rows, inside], lo_ref[pair, rows, inside]
        return dot_split(self.hi[:, there], self.both[:, there], hi, lo, NT)


def reversed_blocks(edge, size):
    return [edge[:, k * size : (k + 1) * size] for k in reversed(range(edge.shape[1] // size))]


def far_sum(operator, halo, size):
    strip = Strip(jnp.concatenate(reversed_blocks(halo, size), axis=1), -REACH, size)
    outer = strip.band(operator, 0, -REACH, 0)
    inner = strip.band(operator, 1, -1, 0, 0)
    return jnp.concatenate([outer, inner], axis=1)


def near_sum(operator, halo, size):
    pairs = operator[0].shape[0]
    strip = Strip(jnp.concatenate(reversed_blocks(halo, size), axis=1), 2 * pairs, size)
    outer = strip.band(operator, pairs - 1, 2 * pairs, 2 * pairs + REACH)
    inner = strip.band(operator, pairs - 2, 2 * pairs, 2 * pairs + 1, 1)
    return jnp.concatenate([inner, outer], axis=1)


def own_sum(operator, strip, pair, lowest=0):
    pairs = operator[0].shape[0]
    return strip.band(operator, pair, max(2 * pair - REACH, lowest), min(2 * pair + REACH + 2, 2 * pairs))


def first_kernel(terms_ref, vectors_ref, hi_ref, lo_ref, out_ref):
    pairs, width, _ = hi_ref.shape
    scale, diag = terms_ref[0:1, :], terms_ref[1:2, :]
    strip = Strip(vectors_ref[...], 0, width // 2)
    for pair in range(pairs):
        here = slice(pair * width, pair * width + width)
        total = scale * own_sum((hi_ref, lo_ref), strip, pair) + diag * vectors_ref[:, here]
        out_ref[:, here] = 0.5 * total


def local_kernel(first_pair, terms_ref, far_ref, mid_ref, near_ref, far_before_ref, mid_before_ref, near_before_ref, hi_ref, lo_ref, out_ref, *full_ref):
    pairs, width, _ = hi_ref.shape
    edge, start = near_ref.shape[1], far_ref.shape[1]
    scale, diag = terms_ref[0:1, :], terms_ref[1:2, :]
    current = jnp.concatenate([far_ref[...], mid_ref[:, start:-edge], near_ref[...]], axis=1)
    before = jnp.concatenate([far_before_ref[...], mid_before_ref[:, edge:-edge], near_before_ref[...]], axis=1)
    if full_ref:
        full_ref[0][...] = current
    strip = Strip(current, 0, width // 2)
    for pair in range(first_pair, pairs):
        here = slice(pair * width, pair * width + width)
        total = scale * own_sum((hi_ref, lo_ref), strip, pair) + diag * current[:, here]
        out_ref[:, here] = total - before[:, here]


def second_kernel(terms_ref, mid_ref, near_ref, before_ref, hi_ref, lo_ref, out_ref):
    pairs, width, _ = hi_ref.shape
    edge = near_ref.shape[1]
    scale, diag = terms_ref[0:1, :], terms_ref[1:2, :]
    current = jnp.concatenate([mid_ref[:, edge:-edge], near_ref[...]], axis=1)
    padded = jnp.concatenate([jnp.zeros(near_ref.shape, F32), current], axis=1)
    strip = Strip(current, REACH, width // 2)
    for pair in range(pairs):
        here = slice(pair * width, pair * width + width)
        total = scale * own_sum((hi_ref, lo_ref), strip, pair, REACH) + diag * padded[:, here]
        out_ref[:, here] = total - before_ref[:, here]


def step_call(kernel, name, operands, operator, outs):
    size = operands[1].size
    width = operator[0].shape[1]
    return pl.pallas_call(
        kernel,
        in_specs=[VM] * (len(operands) + 2),
        out_specs=[VM] * len(outs),
        out_shape=[jax.ShapeDtypeStruct(shape, F32) for shape in outs],
        compiler_params=params(),
        cost_estimate=pl.CostEstimate(flops=24 * size * width, bytes_accessed=8 * size, transcendentals=0),
        name=name,
    )(*operands, *operator)


def near_kernel(factor, terms_ref, mid_ref, halo_ref, hi_ref, lo_ref, out_ref):
    size, edge = hi_ref.shape[1] // 2, halo_ref.shape[1]
    scale = factor * terms_ref[0:1, 0:1]
    out_ref[...] = mid_ref[:, -edge:] + scale * near_sum((hi_ref, lo_ref), halo_ref[...], size)


def edge_ahead(operator, scale, diag, far, before, size):
    strip = Strip(far, 0, size)
    outer = strip.band(operator, 0, 0, REACH + 2)
    inner = strip.band(operator, 1, 0, 2 * REACH, 0)
    total = jnp.concatenate([outer, inner], axis=1)
    return scale * total + diag * far[:, : total.shape[1]] - before


def far_kernel(terms_ref, mid_ref, halo_ref, hi_ref, lo_ref, far_ref):
    size, edge = hi_ref.shape[1] // 2, halo_ref.shape[1]
    far_ref[...] = mid_ref[:, :edge] + 0.5 * terms_ref[0:1, 0:1] * far_sum((hi_ref, lo_ref), halo_ref[...], size)


def turn_one_kernel(terms_ref, mid_ref, halo_ref, before_ref, hi_ref, lo_ref, far_ref, send_ref):
    operator = (hi_ref, lo_ref)
    size, edge = hi_ref.shape[1] // 2, halo_ref.shape[1]
    scale, diag = terms_ref[0:1, 0:1], terms_ref[1:2, 0:1]
    edge_rows = mid_ref[:, :edge] + scale * far_sum(operator, halo_ref[...], size)
    far = jnp.concatenate([edge_rows, mid_ref[:, edge : 2 * edge]], axis=1)
    far_ref[...] = far
    send_ref[0] = edge_rows
    send_ref[1] = edge_ahead(operator, scale, diag, far, before_ref[...], size)


def beyond_sum(terms_ref, sent_ref, cross_hi_ref, cross_lo_ref):
    size = cross_hi_ref.shape[1]

    def cross(ref, row):
        rows = [slice(at * size, (at + 1) * size) for at in (cross_at(row, -1 - place) for place in range(REACH - row))]
        return jnp.concatenate([ref[here, :] for here in rows], axis=1)

    own = Strip(sent_ref[0], 0, size)
    pieces = []
    for row in range(REACH):
        there = slice(0, (REACH - row) * size)
        hi, lo = cross(cross_hi_ref, row), cross(cross_lo_ref, row)
        pieces.append(dot_split(own.hi[:, there], own.both[:, there], hi, lo, NT))
    return terms_ref[0:1, 0:1] * jnp.concatenate(pieces, axis=1)


def beyond_kernel(terms_ref, sent_ref, cross_hi_ref, cross_lo_ref, out_ref):
    out_ref[...] = beyond_sum(terms_ref, sent_ref, cross_hi_ref, cross_lo_ref)


def turn(terms_ref, mid_ref, sent_ref, got_ref, beyond_refs, operator):
    size, edge = operator[0].shape[1] // 2, sent_ref.shape[2]
    scale, diag = terms_ref[0:1, 0:1], terms_ref[1:2, 0:1]
    between = sent_ref[1] + scale * far_sum(operator, got_ref[0], size)
    beyond = beyond_refs[0][...] if len(beyond_refs) == 1 else beyond_sum(terms_ref, sent_ref, *beyond_refs)
    beyond = got_ref[1] + beyond
    strip = Strip(jnp.concatenate(reversed_blocks(beyond, size) + [between], axis=1), -REACH, size)
    total = [strip.band(operator, pair, 2 * pair - REACH, REACH) for pair in range(REACH)]
    known = jnp.concatenate([diag * between, jnp.zeros_like(between)], axis=1)
    return between, mid_ref[:, : 2 * edge] + scale * jnp.concatenate(total, axis=1) + known


def cross_kernel(mine_ref, one_ref, two_ref, hi_ref, lo_ref):
    rows = mine_ref.shape[0]
    place = lax.rem(lax.axis_index("wide"), CROSS_PARTS)
    for d, part in enumerate([mine_ref[...], one_ref[...], two_ref[:rows, :], two_ref[rows:, :]]):
        here = chunk_at(place, d, CROSS_PARTS, rows)
        hi, lo = split(part)
        hi_ref[here, :] = hi
        lo_ref[here, :] = lo


def cross_part(mine):
    one = wide_swap(mine, 1)
    two = wide_swap(jnp.concatenate([mine, one]), 2)
    rows, width = mine.shape
    return pl.pallas_call(
        cross_kernel,
        in_specs=[VM] * 3,
        out_specs=[VM] * 2,
        out_shape=[jax.ShapeDtypeStruct((CROSS_PARTS * rows, width), BF16)] * 2,
        compiler_params=params(),
        name="cross_part",
    )(mine, one, two)


def turn_two_kernel(terms_ref, mid_ref, sent_ref, got_ref, *refs):
    *beyond_refs, hi_ref, lo_ref, between_ref, far_ref, send_ref = refs
    operator = (hi_ref, lo_ref)
    size, edge = hi_ref.shape[1] // 2, between_ref.shape[1]
    between, far = turn(terms_ref, mid_ref, sent_ref, got_ref, beyond_refs, operator)
    between_ref[...] = between
    far_ref[...] = far
    send_ref[0] = far[:, :edge]
    send_ref[1] = edge_ahead(operator, terms_ref[0:1, 0:1], terms_ref[1:2, 0:1], far, between, size)


def packs(count, own):
    return own % TILE == TILE // 2 and own > TILE and count % 16 == 0


def last_kernel(parts, terms_ref, mid_ref, sent_ref, got_ref, beyond_ref, near_ref, hi_ref, lo_ref, out_ref):
    size = hi_ref.shape[1] // 2
    _, far = turn(terms_ref, mid_ref, sent_ref, got_ref, (beyond_ref,), (hi_ref, lo_ref))
    whole = jnp.concatenate([far, mid_ref[:, far.shape[1] : -near_ref.shape[1]], near_ref[...]], axis=1)
    mirrored = jnp.concatenate(reversed_blocks(whole, size), axis=1)
    whole = jnp.where(odd_device(), mirrored, whole)
    if len(out_ref.shape) == 2:
        out_ref[...] = whole
        return
    count, own, half = whole.shape[0], whole.shape[1] // parts, TILE // 2
    for part in range(parts):
        begin = part * own
        head, tail = (begin, begin + own - half) if part % 2 == 0 else (begin + half, begin)
        at = 0
        for column in range(head, head + own - half, TILE):
            out_ref[part, at : at + count, :] = whole[:, column : column + TILE]
            at += count
        tails = whole[:, tail : tail + half]
        out_ref[part, at:, :] = jnp.concatenate([tails[: count // 2], tails[count // 2 :]], axis=1)


def far_swap(x):
    size = lax.axis_size("narrow")
    return lax.ppermute(x, "narrow", [(i, (i + 1) % size if i % 2 else (i - 1) % size) for i in range(size)])


def wide_swap(x, mask):
    return lax.ppermute(x, "wide", [(i, i ^ mask) for i in range(lax.axis_size("wide"))])


def near_swap(x):
    return lax.ppermute(x, "narrow", [(i, i ^ 1) for i in range(lax.axis_size("narrow"))])


def filtered_parts(vectors, blocks, columns, lower_bound, upper_bound):
    size = blocks.shape[2]
    width, edge, parts = 2 * size, REACH * size, lax.axis_size("wide")
    count, length = vectors.shape
    half_width = (upper_bound - lower_bound) * 0.5
    scale = 2.0 / half_width
    diag = scale * (1.0 - (upper_bound + lower_bound) * 0.5)
    terms = jnp.concatenate([jnp.broadcast_to(scale, (1, width)), jnp.broadcast_to(diag, (1, width))])
    total_blocks = blocks.shape[0] * lax.axis_size("narrow")
    far, near, vectors, cross, *operator = spread_part(columns, vectors, blocks, total_blocks)
    whole, side, double = (count, length), (count, edge), (2, count, edge)

    def near_part(factor, mid, halo):
        kernel = functools.partial(near_kernel, factor)
        return step_call(kernel, "near_part", (terms, mid, halo), operator, [side])[0]

    def local_part(first_pair, outs):
        kernel = functools.partial(local_kernel, first_pair)
        return step_call(kernel, "local_part", (terms, far, mid, near, *before), operator, [whole] * outs)

    halo, near_halo = far_swap(far), near_swap(near)
    cross = cross_part(far_swap(cross))
    (mid,) = step_call(first_kernel, "first_part", (terms, vectors), operator, [whole])
    before = (far, vectors, near)
    near = near_part(0.5, mid, near_halo)
    (far,) = step_call(far_kernel, "far_part", (terms, mid, halo), operator, [side])
    halo, near_halo = far_swap(far), near_swap(near)
    (next_mid,) = local_part(0, 1)
    before = (far, mid, near)
    mid, near = next_mid, near_part(1.0, next_mid, near_halo)
    far, send = step_call(turn_one_kernel, "turn_one", (terms, mid, halo, far), operator, [(count, 2 * edge), double])
    for step in range(2, STEPS, 2):
        got, near_halo = far_swap(send), near_swap(near)
        mid, full = local_part(1, 2)
        near = near_part(1.0, mid, near_halo)
        near_halo = near_swap(near)
        (next_mid,) = step_call(second_kernel, "second_part", (terms, mid, near, full), operator, [whole])
        next_near = near_part(1.0, next_mid, near_halo)
        beyond = cross
        if step > 2:
            beyond = step_call(beyond_kernel, "beyond_part", (terms, send), cross, [side])
        operands = (terms, next_mid, send, got, *beyond)
        if step < STEPS - 2:
            outs = [side, (count, 2 * edge), double]
            between, far, send = step_call(turn_two_kernel, "turn_two", operands, operator, outs)
            before = (between, mid, near)
        mid, near = next_mid, next_near
    shape = (parts, count * length // parts // TILE, TILE) if packs(count, length // parts) else whole
    return step_call(functools.partial(last_kernel, parts), "last_part", (*operands, near), operator, [shape])[0]


def pair_perm(mask):
    narrow, wide = lax.axis_size("narrow"), lax.axis_size("wide")
    return [(n * wide + w, (n ^ mask[0]) * wide + (w ^ mask[1])) for n in range(narrow) for w in range(wide)]


def swap(x, mask):
    return lax.ppermute(x, ("narrow", "wide"), pair_perm(mask))


def bit_groups():
    narrow = [(1 << b, 0) for b in range(lax.axis_size("narrow").bit_length() - 1)]
    wide = [(0, 1 << b) for b in range(lax.axis_size("wide").bit_length() - 1)]
    rest = wide[1:] + narrow[2:]
    return [narrow[:1], narrow[1:2] + wide[:1]] + [rest[i : i + 2] for i in range(0, len(rest), 2)]


def masks(bits):
    out = []
    for d in range(1 << len(bits)):
        chosen = [b for k, b in enumerate(bits) if d >> k & 1]
        out.append((sum(b[0] for b in chosen), sum(b[1] for b in chosen)))
    return out


def place_in(bits):
    n, w = lax.axis_index("narrow"), lax.axis_index("wide")
    place = 0
    for k, b in enumerate(bits):
        bit = lax.rem(lax.div(n, b[0]), 2) if b[0] else lax.rem(lax.div(w, b[1]), 2)
        place = place + bit * (1 << k)
    return place


def relative(place, d, count):
    out = 0
    for k in range(count.bit_length() - 1):
        bit = lax.rem(lax.div(place, 1 << k), 2)
        out = out + (1 << k) * (1 - bit if d >> k & 1 else bit)
    return out


def chunk_at(place, d, count, rows):
    return pl.ds(pl.multiple_of(relative(place, d, count) * rows, 8), rows)


def fold_kernel(bits, *refs):
    count = 1 << len(bits)
    parts, outs = refs[:-count], refs[-count:]
    place = place_in(bits)
    rows = outs[0].shape[0]
    for d in range(count):
        here = chunk_at(place, d, count, rows)
        total = parts[0][here, :]
        for part in parts[1:]:
            total = total + part[here, :]
        outs[d][...] = total


def fold(parts, bits):
    count = 1 << len(bits)
    rows, width = parts[0].shape
    return pl.pallas_call(
        functools.partial(fold_kernel, bits),
        in_specs=[VM] * len(parts),
        out_specs=[VM] * count,
        out_shape=[jax.ShapeDtypeStruct((rows // count, width), F32)] * count,
        compiler_params=params(),
        name="fold",
    )(*parts)


def fan(parts, bits):
    members = masks(bits)
    return [parts[0]] + [swap(parts[d], members[d]) for d in range(1, len(members))]


def all_sum(halves):
    groups = bit_groups()
    parts = fan(halves, groups[0])
    for bits in groups[1:-1]:
        parts = fan(fold(parts, bits), bits)
    x = sum(parts)
    x = sum(fan([x] * (1 << len(groups[-1])), groups[-1]))
    for bits in groups[1:-1][::-1]:
        blocks = fan([x] * (1 << len(bits)), bits)
        x = jnp.concatenate(blocks)
    return x, swap(x, masks(groups[0])[1])


def sum_order():
    groups = bit_groups()
    return groups[1:-1]


def tile_pairs(count):
    return [(i, j) for i in range(count) for j in range(i + 1, count)]


def packed_rows(count):
    rows = len(tile_pairs(count)) * TILE + count * TILE // 2 + count // 2 * TILE // 2
    blocks = 8
    for bits in bit_groups()[:-1]:
        blocks <<= len(bits)
    return -(-rows // blocks) * blocks


def gram_kernel(own, parts_ref, keep_ref, send_ref, rows_ref, packed):
    if parts_ref.ndim == 2:
        rows = parts_ref[...]
    else:
        parts, length, _ = parts_ref.shape
        count, half = length * TILE // own, TILE // 2
        heads = (own - half) // TILE
        pieces = []
        for part in range(parts):
            head = [parts_ref[part, h * count : (h + 1) * count, :] for h in range(heads)]
            tails = parts_ref[part, heads * count :, :]
            swapped = pltpu.roll(tails, half, 1)
            low = lax.broadcasted_iota(jnp.int32, tails.shape, 1) < half
            tail = jnp.concatenate([jnp.where(low, tails, swapped), jnp.where(low, swapped, tails)], axis=0)
            pieces.append(jnp.concatenate(head + [tail], axis=1)[:, :own])
        rows = jnp.concatenate(pieces, axis=0)
    rows_ref[...] = rows
    tiles, half = rows.shape[0] // TILE, TILE // 2
    hi, lo = split(rows)
    at, tops = 0, len(tile_pairs(tiles)) * TILE
    lasts = tops + tiles * half
    for i in range(tiles):
        here, there = slice(i * TILE, (i + 1) * TILE), slice(i * TILE, None)
        both = jnp.concatenate([hi[here], lo[here]], axis=0)
        strip = dot_split(hi[here], both, hi[there], lo[there], NT)
        packed[tops + i * half : tops + (i + 1) * half, :] = strip[:half, :TILE]
        last = strip[half:, half:TILE]
        if i % 2 == 0:
            held = last
        else:
            packed[lasts + i // 2 * half : lasts + (i // 2 + 1) * half, :] = jnp.concatenate([held, last], axis=1)
        for j in range(i + 1, tiles):
            packed[at : at + TILE, :] = strip[:, (j - i) * TILE : (j - i + 1) * TILE]
            at += TILE
    used = lasts + tiles // 2 * half
    if used < packed.shape[0]:
        packed[used:, :] = jnp.zeros((packed.shape[0] - used, TILE), F32)
    odd, size = odd_device(), keep_ref.shape[0]
    keep_ref[...] = packed[pl.ds(pl.multiple_of(jnp.where(odd, size, 0), 8), size), :]
    send_ref[...] = packed[pl.ds(pl.multiple_of(jnp.where(odd, 0, size), 8), size), :]


def gram(parts, own):
    total = parts.size // own
    size = packed_rows(total // TILE)
    half = jax.ShapeDtypeStruct((size // 2, TILE), F32)
    return pl.pallas_call(
        functools.partial(gram_kernel, own),
        in_specs=[VM],
        out_specs=[VM] * 3,
        out_shape=[half, half, jax.ShapeDtypeStruct((total, own), F32)],
        scratch_shapes=[pltpu.VMEM((size, TILE), F32)],
        compiler_params=params(),
        name="gram",
    )(parts)


def turned_kernel(packed, rows_ref, out_ref):
    rows = rows_ref[...].T
    if packed:
        half = TILE // 2
        rows = jnp.where(odd_place("wide"), jnp.concatenate([rows[-half:], rows[:-half]], axis=0), rows)
    out_ref[...] = rows


def turned(rows, packed):
    return pl.pallas_call(
        functools.partial(turned_kernel, packed),
        in_specs=[VM],
        out_specs=VM,
        out_shape=jax.ShapeDtypeStruct(rows.shape[::-1], F32),
        compiler_params=params(),
        name="turned",
    )(rows)


def rotate_kernel(total_rows, groups, own_ref, other_ref, rows_ref, out_ref, packed, hi_ref, lo_ref, held, sems):
    size = own_ref.shape[0]
    places = [place_in(bits) for bits in groups]
    blocks = 1
    for bits in groups:
        blocks <<= len(bits)
    length = size // blocks
    odd = odd_device()
    for block in range(blocks):
        at, rest, step = 0, block, blocks
        for bits, place in zip(groups, places):
            count = 1 << len(bits)
            step //= count
            at = at + relative(place, rest // step, count) * (step * length)
            rest %= step
        here = slice(block * length, (block + 1) * length)
        packed[pl.ds(pl.multiple_of(jnp.where(odd, size, 0) + at, 8), length), :] = own_ref[here, :]
        packed[pl.ds(pl.multiple_of(jnp.where(odd, 0, size) + at, 8), length), :] = other_ref[here, :]
    tiles, half = rows_ref.shape[1] // TILE, TILE // 2
    order = tile_pairs(tiles)
    tops = len(order) * TILE
    lasts = tops + tiles * half
    above = packed[:tops, :].reshape(len(order), TILE, TILE)
    squares = jnp.sum(above * above, axis=0) * 2.0
    top = packed[tops:lasts, :].reshape(tiles, half, TILE)
    weight = jnp.where(lax.broadcasted_iota(jnp.int32, (half, TILE), 1) < half, 1.0, 2.0)
    last = packed[lasts : lasts + tiles // 2 * half, :].reshape(tiles // 2, half, TILE)
    squares = squares[:half] + squares[half:] + jnp.sum(top * top, axis=0) * weight + jnp.sum(last * last, axis=0)
    frob = jnp.sqrt(jnp.sum(squares, axis=(0, 1), keepdims=True) + 1e-06)
    factor = 0.5 / frob
    gain = jnp.sqrt(total_rows / frob)
    for at, (i, j) in enumerate(order):
        hi, lo = split(packed[at * TILE : (at + 1) * TILE, :] * factor)
        one, two = slice(i * TILE, (i + 1) * TILE), slice(j * TILE, (j + 1) * TILE)
        hi_ref[one, two] = hi
        lo_ref[one, two] = lo
        hi_ref[two, one] = hi.T
        lo_ref[two, one] = lo.T
    for i in range(tiles):
        upper = packed[tops + i * half : tops + (i + 1) * half, :]
        quarter = packed[lasts + i // 2 * half : lasts + (i // 2 + 1) * half, :][:, i % 2 * half : (i % 2 + 1) * half]
        lower = jnp.concatenate([upper[:, half:].T, quarter], axis=1)
        hi, lo = split(jnp.concatenate([upper, lower], axis=0) * factor)
        one = slice(i * TILE, (i + 1) * TILE)
        hi_ref[one, one] = hi
        lo_ref[one, one] = lo
    rows = rows_ref[...]
    rows_hi, rows_lo = split(rows)
    both = jnp.concatenate([rows_hi, rows_lo], axis=0)
    copies = []
    for strip in range(tiles // 2):
        here = slice(strip * 2 * TILE, (strip + 1) * 2 * TILE)
        turned = dot_split(rows_hi, both, hi_ref[:, here], lo_ref[:, here], NN)
        held[:, here] = gain * (1.5 * rows[:, here] - turned)
        copies.append(pltpu.make_async_copy(held.at[:, here], out_ref.at[:, here], sems.at[strip]))
        copies[-1].start()
    for copy in copies:
        copy.wait()


def rotate(halves, rows, total_rows):
    own, total = rows.shape
    return pl.pallas_call(
        functools.partial(rotate_kernel, float(total_rows), sum_order()),
        in_specs=[VM, VM, VM],
        out_specs=HBM,
        out_shape=pltpu.HBM(rows.shape, F32),
        scratch_shapes=[
            pltpu.VMEM((packed_rows(total // TILE), TILE), F32),
            pltpu.VMEM((total, total), BF16),
            pltpu.VMEM((total, total), BF16),
            pltpu.VMEM(rows.shape, F32),
            pltpu.SemaphoreType.DMA((total // TILE // 2,)),
        ],
        compiler_params=params(),
        name="rotate",
    )(*halves, rows).T


def regroup(parts):
    size = lax.axis_size("wide")
    if parts.ndim == 3:
        return lax.all_to_all(parts, "wide", split_axis=0, concat_axis=0, tiled=True)
    count, length = parts.shape
    own = length // size
    parts = parts.reshape(count, size, own).transpose(1, 0, 2).reshape(size, count * own // TILE, TILE)
    parts = lax.all_to_all(parts, "wide", split_axis=0, concat_axis=0, tiled=True)
    return parts.reshape(size * count, own)


def on_device(vectors, blocks, columns, lower_bound, upper_bound):
    length = vectors.shape[1]
    parts = regroup(filtered_parts(vectors, blocks, columns, lower_bound, upper_bound))
    *halves, rows = gram(parts, length // lax.axis_size("wide"))
    return rotate(all_sum(halves), turned(rows, parts.ndim == 3), length * lax.axis_size("narrow"))


def solution(mesh):
    return jax.shard_map(
        on_device,
        mesh=mesh,
        in_specs=(P("wide", "narrow"), P("narrow", None, None, None), P("narrow", None), P(), P()),
        out_specs=P(None, ("narrow", "wide")),
        check_vma=False,
    )
```

```python
import functools

import jax
import jax.numpy as jnp
from jax import lax
from jax.experimental import pallas as pl
from jax.experimental.pallas import tpu as pltpu
from jax.sharding import PartitionSpec as P

REACH = 3
CROSS_PARTS = 4
STEPS = 8
TILE = 128
VM = pl.BlockSpec(memory_space=pltpu.VMEM)
SM = pl.BlockSpec(memory_space=pltpu.SMEM)
HBM = pl.BlockSpec(memory_space=pltpu.HBM)
NT = (((1,), (1,)), ((), ()))
NN = (((1,), (0,)), ((), ()))
F32 = jnp.float32
BF16 = jnp.bfloat16


def params():
    return pltpu.CompilerParams(vmem_limit_bytes=40 * 1024 * 1024)


def split(x):
    hi = x.astype(BF16)
    return hi, (x - hi.astype(F32)).astype(BF16)


def in_hbm(x):
    return pltpu.with_memory_space_constraint(x, pltpu.HBM)


def odd_place(axis):
    return lax.rem(lax.axis_index(axis), 2) == 1


def odd_device():
    return odd_place("narrow")


def dot(a, b, dims):
    return lax.dot_general(a, b, dims, preferred_element_type=F32)


def dot_split(a_hi, a_both, b_hi, b_lo, dims):
    rows = a_hi.shape[0]
    upper = dot(a_both, b_hi, dims)
    return upper[:rows] + (upper[rows:] + dot(a_hi, b_lo, dims))


def cross_at(row, place):
    return sum(REACH - r for r in range(row)) + place + REACH - row


def spread_kernel(total_blocks, columns_hbm, vectors_hbm, blocks_hbm, far_ref, near_ref, vectors_ref, part_ref, hi_ref, lo_ref, held, straight, cross_ref, columns_ref, sems, pair_sems):
    rows, slots, size, _ = blocks_hbm.shape
    edge = far_ref.shape[1]
    odd = odd_device()
    source = [jnp.where(odd, rows - 1 - row, row) for row in range(rows)]
    copies = [
        pltpu.make_async_copy(columns_hbm, columns_ref, sems.at[0]),
        pltpu.make_async_copy(vectors_hbm, straight, sems.at[1]),
    ]
    large = []
    for pair in range(rows // 2):
        begin = jnp.where(odd, rows - 2 - 2 * pair, 2 * pair)
        large.append(pltpu.make_async_copy(blocks_hbm.at[pl.ds(begin, 2)], held.at[pl.ds(2 * pair, 2)], pair_sems.at[pair]))
    for copy in copies + large:
        copy.start()
    hi_ref[...] = jnp.zeros_like(hi_ref)
    lo_ref[...] = jnp.zeros_like(lo_ref)
    cross_ref[...] = jnp.zeros_like(cross_ref)
    first = lax.axis_index("narrow") * rows
    copies[0].wait()
    for row in range(rows):
        pair, half = divmod(row, 2)
        if half == 0:
            large[pair].wait()
        place = 2 * pair + jnp.where(odd, 1 - half, half)
        here = slice(half * size, half * size + size)
        for slot in range(slots):
            offset = columns_ref[slot, source[row]] - (first + source[row])
            offset = jnp.where(offset > REACH, offset - total_blocks, offset)
            offset = jnp.where(offset < -REACH, offset + total_blocks, offset)
            offset = jnp.where(odd, -offset, offset)
            block = held[place, slot]
            hi, lo = split(block)
            there = pl.ds(pl.multiple_of((half + offset + REACH) * size, size), size)
            hi_ref[pair, here, there] = hi
            lo_ref[pair, here, there] = lo
            if row < REACH:

                @pl.when(row + offset < 0)
                def _():
                    at = pl.multiple_of(cross_at(row, row + offset) * size, size)
                    cross_ref[pl.ds(at, size), :] = block

    count = part_ref.shape[0]
    part_ref[...] = cross_ref[pl.ds(pl.multiple_of(lax.rem(lax.axis_index("wide"), CROSS_PARTS) * count, 8), count), :]
    copies[1].wait()
    whole = straight[...]
    vectors_ref[...] = jnp.where(odd, jnp.concatenate(reversed_blocks(whole, size), axis=1), whole)
    far_ref[...] = vectors_ref[:, :edge]
    near_ref[...] = vectors_ref[:, -edge:]


def spread_part(columns, vectors, blocks, total_blocks):
    rows, slots, size, _ = blocks.shape
    spread = jax.ShapeDtypeStruct((rows // 2, 2 * size, (2 * REACH + 2) * size), BF16)
    edge = jax.ShapeDtypeStruct((vectors.shape[0], REACH * size), F32)
    crossing = REACH * (REACH + 1) // 2 * size
    cross = jax.ShapeDtypeStruct((crossing // CROSS_PARTS, size), F32)
    return pl.pallas_call(
        functools.partial(spread_kernel, total_blocks),
        in_specs=[HBM, HBM, HBM],
        out_specs=[VM] * 6,
        out_shape=[edge, edge, jax.ShapeDtypeStruct(vectors.shape, F32), cross, spread, spread],
        scratch_shapes=[
            pltpu.VMEM(blocks.shape, F32),
            pltpu.VMEM(vectors.shape, F32),
            pltpu.VMEM((crossing, size), F32),
            pltpu.SMEM((slots, rows), jnp.int32),
            pltpu.SemaphoreType.DMA((2,)),
            pltpu.SemaphoreType.DMA((rows // 2,)),
        ],
        compiler_params=params(),
        name="spread_part",
    )(in_hbm(columns.T), in_hbm(vectors), in_hbm(blocks))


class Strip:
    def __init__(self, values, at, size):
        self.hi, lo = split(values)
        self.both = jnp.concatenate([self.hi, lo], axis=0)
        self.at, self.size = at, size

    def band(self, operator, pair, begin, end, half=None):
        hi_ref, lo_ref = operator
        size, start = self.size, 2 * pair - REACH
        there = slice((begin - self.at) * size, (end - self.at) * size)
        inside = slice((begin - start) * size, (end - start) * size)
        rows = slice(None) if half is None else slice(half * size, (half + 1) * size)
        hi, lo = hi_ref[pair, rows, inside], lo_ref[pair, rows, inside]
        return dot_split(self.hi[:, there], self.both[:, there], hi, lo, NT)


def reversed_blocks(edge, size):
    return [edge[:, k * size : (k + 1) * size] for k in reversed(range(edge.shape[1] // size))]


def far_sum(operator, halo, size):
    strip = Strip(jnp.concatenate(reversed_blocks(halo, size), axis=1), -REACH, size)
    outer = strip.band(operator, 0, -REACH, 0)
    inner = strip.band(operator, 1, -1, 0, 0)
    return jnp.concatenate([outer, inner], axis=1)


def near_sum(operator, halo, size):
    pairs = operator[0].shape[0]
    strip = Strip(jnp.concatenate(reversed_blocks(halo, size), axis=1), 2 * pairs, size)
    outer = strip.band(operator, pairs - 1, 2 * pairs, 2 * pairs + REACH)
    inner = strip.band(operator, pairs - 2, 2 * pairs, 2 * pairs + 1, 1)
    return jnp.concatenate([inner, outer], axis=1)


def own_sum(operator, strip, pair, lowest=0):
    pairs = operator[0].shape[0]
    return strip.band(operator, pair, max(2 * pair - REACH, lowest), min(2 * pair + REACH + 2, 2 * pairs))


def first_kernel(terms_ref, vectors_ref, hi_ref, lo_ref, out_ref):
    pairs, width, _ = hi_ref.shape
    scale, diag = terms_ref[0:1, :], terms_ref[1:2, :]
    strip = Strip(vectors_ref[...], 0, width // 2)
    for pair in range(pairs):
        here = slice(pair * width, pair * width + width)
        total = scale * own_sum((hi_ref, lo_ref), strip, pair) + diag * vectors_ref[:, here]
        out_ref[:, here] = 0.5 * total


def local_kernel(first_pair, terms_ref, far_ref, mid_ref, near_ref, far_before_ref, mid_before_ref, near_before_ref, hi_ref, lo_ref, out_ref, *full_ref):
    pairs, width, _ = hi_ref.shape
    edge, start = near_ref.shape[1], far_ref.shape[1]
    scale, diag = terms_ref[0:1, :], terms_ref[1:2, :]
    current = jnp.concatenate([far_ref[...], mid_ref[:, start:-edge], near_ref[...]], axis=1)
    before = jnp.concatenate([far_before_ref[...], mid_before_ref[:, edge:-edge], near_before_ref[...]], axis=1)
    if full_ref:
        full_ref[0][...] = current
    strip = Strip(current, 0, width // 2)
    for pair in range(first_pair, pairs):
        here = slice(pair * width, pair * width + width)
        total = scale * own_sum((hi_ref, lo_ref), strip, pair) + diag * current[:, here]
        out_ref[:, here] = total - before[:, here]


def second_kernel(terms_ref, mid_ref, near_ref, before_ref, hi_ref, lo_ref, out_ref):
    pairs, width, _ = hi_ref.shape
    edge = near_ref.shape[1]
    scale, diag = terms_ref[0:1, :], terms_ref[1:2, :]
    current = jnp.concatenate([mid_ref[:, edge:-edge], near_ref[...]], axis=1)
    padded = jnp.concatenate([jnp.zeros(near_ref.shape, F32), current], axis=1)
    strip = Strip(current, REACH, width // 2)
    for pair in range(pairs):
        here = slice(pair * width, pair * width + width)
        total = scale * own_sum((hi_ref, lo_ref), strip, pair, REACH) + diag * padded[:, here]
        out_ref[:, here] = total - before_ref[:, here]


def step_call(kernel, name, operands, operator, outs):
    size = operands[1].size
    width = operator[0].shape[1]
    return pl.pallas_call(
        kernel,
        in_specs=[VM] * (len(operands) + 2),
        out_specs=[VM] * len(outs),
        out_shape=[jax.ShapeDtypeStruct(shape, F32) for shape in outs],
        compiler_params=params(),
        cost_estimate=pl.CostEstimate(flops=24 * size * width, bytes_accessed=8 * size, transcendentals=0),
        name=name,
    )(*operands, *operator)


def near_kernel(factor, terms_ref, mid_ref, halo_ref, hi_ref, lo_ref, out_ref):
    size, edge = hi_ref.shape[1] // 2, halo_ref.shape[1]
    scale = factor * terms_ref[0:1, 0:1]
    out_ref[...] = mid_ref[:, -edge:] + scale * near_sum((hi_ref, lo_ref), halo_ref[...], size)


def edge_ahead(operator, scale, diag, far, before, size):
    strip = Strip(far, 0, size)
    outer = strip.band(operator, 0, 0, REACH + 2)
    inner = strip.band(operator, 1, 0, 2 * REACH, 0)
    total = jnp.concatenate([outer, inner], axis=1)
    return scale * total + diag * far[:, : total.shape[1]] - before


def far_kernel(terms_ref, mid_ref, halo_ref, hi_ref, lo_ref, far_ref):
    size, edge = hi_ref.shape[1] // 2, halo_ref.shape[1]
    far_ref[...] = mid_ref[:, :edge] + 0.5 * terms_ref[0:1, 0:1] * far_sum((hi_ref, lo_ref), halo_ref[...], size)


def turn_one_kernel(terms_ref, mid_ref, halo_ref, before_ref, hi_ref, lo_ref, far_ref, send_ref):
    operator = (hi_ref, lo_ref)
    size, edge = hi_ref.shape[1] // 2, halo_ref.shape[1]
    scale, diag = terms_ref[0:1, 0:1], terms_ref[1:2, 0:1]
    edge_rows = mid_ref[:, :edge] + scale * far_sum(operator, halo_ref[...], size)
    far = jnp.concatenate([edge_rows, mid_ref[:, edge : 2 * edge]], axis=1)
    far_ref[...] = far
    send_ref[0] = edge_rows
    send_ref[1] = edge_ahead(operator, scale, diag, far, before_ref[...], size)


def beyond_sum(terms_ref, sent_ref, cross_hi_ref, cross_lo_ref):
    size = cross_hi_ref.shape[1]

    def cross(ref, row):
        rows = [slice(at * size, (at + 1) * size) for at in (cross_at(row, -1 - place) for place in range(REACH - row))]
        return jnp.concatenate([ref[here, :] for here in rows], axis=1)

    own = Strip(sent_ref[0], 0, size)
    pieces = []
    for row in range(REACH):
        there = slice(0, (REACH - row) * size)
        hi, lo = cross(cross_hi_ref, row), cross(cross_lo_ref, row)
        pieces.append(dot_split(own.hi[:, there], own.both[:, there], hi, lo, NT))
    return terms_ref[0:1, 0:1] * jnp.concatenate(pieces, axis=1)


def beyond_kernel(terms_ref, sent_ref, cross_hi_ref, cross_lo_ref, out_ref):
    out_ref[...] = beyond_sum(terms_ref, sent_ref, cross_hi_ref, cross_lo_ref)


def turn(terms_ref, mid_ref, sent_ref, got_ref, beyond_refs, operator):
    size, edge = operator[0].shape[1] // 2, sent_ref.shape[2]
    scale, diag = terms_ref[0:1, 0:1], terms_ref[1:2, 0:1]
    between = sent_ref[1] + scale * far_sum(operator, got_ref[0], size)
    beyond = beyond_refs[0][...] if len(beyond_refs) == 1 else beyond_sum(terms_ref, sent_ref, *beyond_refs)
    beyond = got_ref[1] + beyond
    strip = Strip(jnp.concatenate(reversed_blocks(beyond, size) + [between], axis=1), -REACH, size)
    total = [strip.band(operator, pair, 2 * pair - REACH, REACH) for pair in range(REACH)]
    known = jnp.concatenate([diag * between, jnp.zeros_like(between)], axis=1)
    return between, mid_ref[:, : 2 * edge] + scale * jnp.concatenate(total, axis=1) + known


def cross_kernel(mine_ref, one_ref, two_ref, hi_ref, lo_ref):
    rows = mine_ref.shape[0]
    place = lax.rem(lax.axis_index("wide"), CROSS_PARTS)
    for d, part in enumerate([mine_ref[...], one_ref[...], two_ref[:rows, :], two_ref[rows:, :]]):
        here = chunk_at(place, d, CROSS_PARTS, rows)
        hi, lo = split(part)
        hi_ref[here, :] = hi
        lo_ref[here, :] = lo


def cross_part(mine):
    one = wide_swap(mine, 1)
    two = wide_swap(jnp.concatenate([mine, one]), 2)
    rows, width = mine.shape
    return pl.pallas_call(
        cross_kernel,
        in_specs=[VM] * 3,
        out_specs=[VM] * 2,
        out_shape=[jax.ShapeDtypeStruct((CROSS_PARTS * rows, width), BF16)] * 2,
        compiler_params=params(),
        name="cross_part",
    )(mine, one, two)


def turn_two_kernel(terms_ref, mid_ref, sent_ref, got_ref, *refs):
    *beyond_refs, hi_ref, lo_ref, between_ref, far_ref, send_ref = refs
    operator = (hi_ref, lo_ref)
    size, edge = hi_ref.shape[1] // 2, between_ref.shape[1]
    between, far = turn(terms_ref, mid_ref, sent_ref, got_ref, beyond_refs, operator)
    between_ref[...] = between
    far_ref[...] = far
    send_ref[0] = far[:, :edge]
    send_ref[1] = edge_ahead(operator, terms_ref[0:1, 0:1], terms_ref[1:2, 0:1], far, between, size)


def packs(count, own):
    return own % TILE == TILE // 2 and own > TILE and count % 16 == 0


def last_kernel(parts, terms_ref, mid_ref, sent_ref, got_ref, beyond_ref, near_ref, hi_ref, lo_ref, out_ref):
    size = hi_ref.shape[1] // 2
    _, far = turn(terms_ref, mid_ref, sent_ref, got_ref, (beyond_ref,), (hi_ref, lo_ref))
    whole = jnp.concatenate([far, mid_ref[:, far.shape[1] : -near_ref.shape[1]], near_ref[...]], axis=1)
    mirrored = jnp.concatenate(reversed_blocks(whole, size), axis=1)
    whole = jnp.where(odd_device(), mirrored, whole)
    if len(out_ref.shape) == 2:
        out_ref[...] = whole
        return
    count, own, half = whole.shape[0], whole.shape[1] // parts, TILE // 2
    for part in range(parts):
        begin = part * own
        head, tail = (begin, begin + own - half) if part % 2 == 0 else (begin + half, begin)
        at = 0
        for column in range(head, head + own - half, TILE):
            out_ref[part, at : at + count, :] = whole[:, column : column + TILE]
            at += count
        tails = whole[:, tail : tail + half]
        out_ref[part, at:, :] = jnp.concatenate([tails[: count // 2], tails[count // 2 :]], axis=1)


def far_swap(x):
    size = lax.axis_size("narrow")
    return lax.ppermute(x, "narrow", [(i, (i + 1) % size if i % 2 else (i - 1) % size) for i in range(size)])


def wide_swap(x, mask):
    return lax.ppermute(x, "wide", [(i, i ^ mask) for i in range(lax.axis_size("wide"))])


def near_swap(x):
    return lax.ppermute(x, "narrow", [(i, i ^ 1) for i in range(lax.axis_size("narrow"))])


def filtered_parts(vectors, blocks, columns, lower_bound, upper_bound):
    size = blocks.shape[2]
    width, edge, parts = 2 * size, REACH * size, lax.axis_size("wide")
    count, length = vectors.shape
    half_width = (upper_bound - lower_bound) * 0.5
    scale = 2.0 / half_width
    diag = scale * (1.0 - (upper_bound + lower_bound) * 0.5)
    terms = jnp.concatenate([jnp.broadcast_to(scale, (1, width)), jnp.broadcast_to(diag, (1, width))])
    total_blocks = blocks.shape[0] * lax.axis_size("narrow")
    far, near, vectors, cross, *operator = spread_part(columns, vectors, blocks, total_blocks)
    whole, side, double = (count, length), (count, edge), (2, count, edge)

    def near_part(factor, mid, halo):
        kernel = functools.partial(near_kernel, factor)
        return step_call(kernel, "near_part", (terms, mid, halo), operator, [side])[0]

    def local_part(first_pair, outs):
        kernel = functools.partial(local_kernel, first_pair)
        return step_call(kernel, "local_part", (terms, far, mid, near, *before), operator, [whole] * outs)

    halo, near_halo = far_swap(far), near_swap(near)
    cross = cross_part(far_swap(cross))
    (mid,) = step_call(first_kernel, "first_part", (terms, vectors), operator, [whole])
    before = (far, vectors, near)
    near = near_part(0.5, mid, near_halo)
    (far,) = step_call(far_kernel, "far_part", (terms, mid, halo), operator, [side])
    halo, near_halo = far_swap(far), near_swap(near)
    (next_mid,) = local_part(0, 1)
    before = (far, mid, near)
    mid, near = next_mid, near_part(1.0, next_mid, near_halo)
    far, send = step_call(turn_one_kernel, "turn_one", (terms, mid, halo, far), operator, [(count, 2 * edge), double])
    for step in range(2, STEPS, 2):
        got, near_halo = far_swap(send), near_swap(near)
        mid, full = local_part(1, 2)
        near = near_part(1.0, mid, near_halo)
        near_halo = near_swap(near)
        (next_mid,) = step_call(second_kernel, "second_part", (terms, mid, near, full), operator, [whole])
        next_near = near_part(1.0, next_mid, near_halo)
        beyond = cross
        if step > 2:
            beyond = step_call(beyond_kernel, "beyond_part", (terms, send), cross, [side])
        operands = (terms, next_mid, send, got, *beyond)
        if step < STEPS - 2:
            outs = [side, (count, 2 * edge), double]
            between, far, send = step_call(turn_two_kernel, "turn_two", operands, operator, outs)
            before = (between, mid, near)
        mid, near = next_mid, next_near
    shape = (parts, count * length // parts // TILE, TILE) if packs(count, length // parts) else whole
    return step_call(functools.partial(last_kernel, parts), "last_part", (*operands, near), operator, [shape])[0]


def pair_perm(mask):
    narrow, wide = lax.axis_size("narrow"), lax.axis_size("wide")
    return [(n * wide + w, (n ^ mask[0]) * wide + (w ^ mask[1])) for n in range(narrow) for w in range(wide)]


def swap(x, mask):
    return lax.ppermute(x, ("narrow", "wide"), pair_perm(mask))


def bit_groups():
    narrow = [(1 << b, 0) for b in range(lax.axis_size("narrow").bit_length() - 1)]
    wide = [(0, 1 << b) for b in range(lax.axis_size("wide").bit_length() - 1)]
    rest = wide[1:] + narrow[2:]
    return [narrow[:1], narrow[1:2] + wide[:1]] + [rest[i : i + 2] for i in range(0, len(rest), 2)]


def masks(bits):
    out = []
    for d in range(1 << len(bits)):
        chosen = [b for k, b in enumerate(bits) if d >> k & 1]
        out.append((sum(b[0] for b in chosen), sum(b[1] for b in chosen)))
    return out


def place_in(bits):
    n, w = lax.axis_index("narrow"), lax.axis_index("wide")
    place = 0
    for k, b in enumerate(bits):
        bit = lax.rem(lax.div(n, b[0]), 2) if b[0] else lax.rem(lax.div(w, b[1]), 2)
        place = place + bit * (1 << k)
    return place


def relative(place, d, count):
    out = 0
    for k in range(count.bit_length() - 1):
        bit = lax.rem(lax.div(place, 1 << k), 2)
        out = out + (1 << k) * (1 - bit if d >> k & 1 else bit)
    return out


def chunk_at(place, d, count, rows):
    return pl.ds(pl.multiple_of(relative(place, d, count) * rows, 8), rows)


def fold_kernel(bits, *refs):
    count = 1 << len(bits)
    parts, outs = refs[:-count], refs[-count:]
    place = place_in(bits)
    rows = outs[0].shape[0]
    for d in range(count):
        here = chunk_at(place, d, count, rows)
        total = parts[0][here, :]
        for part in parts[1:]:
            total = total + part[here, :]
        outs[d][...] = total


def fold(parts, bits):
    count = 1 << len(bits)
    rows, width = parts[0].shape
    return pl.pallas_call(
        functools.partial(fold_kernel, bits),
        in_specs=[VM] * len(parts),
        out_specs=[VM] * count,
        out_shape=[jax.ShapeDtypeStruct((rows // count, width), F32)] * count,
        compiler_params=params(),
        name="fold",
    )(*parts)


def fan(parts, bits):
    members = masks(bits)
    return [parts[0]] + [swap(parts[d], members[d]) for d in range(1, len(members))]


def all_sum(halves):
    groups = bit_groups()
    parts = fan(halves, groups[0])
    for bits in groups[1:-1]:
        parts = fan(fold(parts, bits), bits)
    x = sum(parts)
    x = sum(fan([x] * (1 << len(groups[-1])), groups[-1]))
    for bits in groups[1:-1][::-1]:
        blocks = fan([x] * (1 << len(bits)), bits)
        x = jnp.concatenate(blocks)
    return x, swap(x, masks(groups[0])[1])


def sum_order():
    groups = bit_groups()
    return groups[1:-1]


def tile_pairs(count):
    return [(i, j) for i in range(count) for j in range(i + 1, count)]


def packed_rows(count):
    rows = len(tile_pairs(count)) * TILE + count * TILE // 2 + count // 2 * TILE // 2
    blocks = 8
    for bits in bit_groups()[:-1]:
        blocks <<= len(bits)
    return -(-rows // blocks) * blocks


def gram_kernel(own, parts_ref, keep_ref, send_ref, rows_ref, packed):
    if parts_ref.ndim == 2:
        rows = parts_ref[...]
    else:
        parts, length, _ = parts_ref.shape
        count, half = length * TILE // own, TILE // 2
        heads = (own - half) // TILE
        pieces = []
        for part in range(parts):
            head = [parts_ref[part, h * count : (h + 1) * count, :] for h in range(heads)]
            tails = parts_ref[part, heads * count :, :]
            swapped = pltpu.roll(tails, half, 1)
            low = lax.broadcasted_iota(jnp.int32, tails.shape, 1) < half
            tail = jnp.concatenate([jnp.where(low, tails, swapped), jnp.where(low, swapped, tails)], axis=0)
            pieces.append(jnp.concatenate(head + [tail], axis=1)[:, :own])
        rows = jnp.concatenate(pieces, axis=0)
    rows_ref[...] = rows
    tiles, half = rows.shape[0] // TILE, TILE // 2
    hi, lo = split(rows)
    at, tops = 0, len(tile_pairs(tiles)) * TILE
    lasts = tops + tiles * half
    for i in range(tiles):
        here, there = slice(i * TILE, (i + 1) * TILE), slice(i * TILE, None)
        both = jnp.concatenate([hi[here], lo[here]], axis=0)
        strip = dot_split(hi[here], both, hi[there], lo[there], NT)
        packed[tops + i * half : tops + (i + 1) * half, :] = strip[:half, :TILE]
        last = strip[half:, half:TILE]
        if i % 2 == 0:
            held = last
        else:
            packed[lasts + i // 2 * half : lasts + (i // 2 + 1) * half, :] = jnp.concatenate([held, last], axis=1)
        for j in range(i + 1, tiles):
            packed[at : at + TILE, :] = strip[:, (j - i) * TILE : (j - i + 1) * TILE]
            at += TILE
    used = lasts + tiles // 2 * half
    if used < packed.shape[0]:
        packed[used:, :] = jnp.zeros((packed.shape[0] - used, TILE), F32)
    odd, size = odd_device(), keep_ref.shape[0]
    keep_ref[...] = packed[pl.ds(pl.multiple_of(jnp.where(odd, size, 0), 8), size), :]
    send_ref[...] = packed[pl.ds(pl.multiple_of(jnp.where(odd, 0, size), 8), size), :]


def gram(parts, own):
    total = parts.size // own
    size = packed_rows(total // TILE)
    half = jax.ShapeDtypeStruct((size // 2, TILE), F32)
    return pl.pallas_call(
        functools.partial(gram_kernel, own),
        in_specs=[VM],
        out_specs=[VM] * 3,
        out_shape=[half, half, jax.ShapeDtypeStruct((total, own), F32)],
        scratch_shapes=[pltpu.VMEM((size, TILE), F32)],
        compiler_params=params(),
        name="gram",
    )(parts)


def turned_kernel(packed, rows_ref, out_ref):
    rows = rows_ref[...].T
    if packed:
        half = TILE // 2
        rows = jnp.where(odd_place("wide"), jnp.concatenate([rows[-half:], rows[:-half]], axis=0), rows)
    out_ref[...] = rows


def turned(rows, packed):
    return pl.pallas_call(
        functools.partial(turned_kernel, packed),
        in_specs=[VM],
        out_specs=VM,
        out_shape=jax.ShapeDtypeStruct(rows.shape[::-1], F32),
        compiler_params=params(),
        name="turned",
    )(rows)


def rotate_kernel(total_rows, groups, own_ref, other_ref, rows_ref, out_ref, packed, hi_ref, lo_ref, held, sems):
    size = own_ref.shape[0]
    places = [place_in(bits) for bits in groups]
    blocks = 1
    for bits in groups:
        blocks <<= len(bits)
    length = size // blocks
    odd = odd_device()
    for block in range(blocks):
        at, rest, step = 0, block, blocks
        for bits, place in zip(groups, places):
            count = 1 << len(bits)
            step //= count
            at = at + relative(place, rest // step, count) * (step * length)
            rest %= step
        here = slice(block * length, (block + 1) * length)
        packed[pl.ds(pl.multiple_of(jnp.where(odd, size, 0) + at, 8), length), :] = own_ref[here, :]
        packed[pl.ds(pl.multiple_of(jnp.where(odd, 0, size) + at, 8), length), :] = other_ref[here, :]
    tiles, half = rows_ref.shape[1] // TILE, TILE // 2
    order = tile_pairs(tiles)
    tops = len(order) * TILE
    lasts = tops + tiles * half
    above = packed[:tops, :].reshape(len(order), TILE, TILE)
    squares = jnp.sum(above * above, axis=0) * 2.0
    top = packed[tops:lasts, :].reshape(tiles, half, TILE)
    weight = jnp.where(lax.broadcasted_iota(jnp.int32, (half, TILE), 1) < half, 1.0, 2.0)
    last = packed[lasts : lasts + tiles // 2 * half, :].reshape(tiles // 2, half, TILE)
    squares = squares[:half] + squares[half:] + jnp.sum(top * top, axis=0) * weight + jnp.sum(last * last, axis=0)
    frob = jnp.sqrt(jnp.sum(squares, axis=(0, 1), keepdims=True) + 1e-06)
    factor = 0.5 / frob
    gain = jnp.sqrt(total_rows / frob)
    for at, (i, j) in enumerate(order):
        hi, lo = split(packed[at * TILE : (at + 1) * TILE, :] * factor)
        one, two = slice(i * TILE, (i + 1) * TILE), slice(j * TILE, (j + 1) * TILE)
        hi_ref[one, two] = hi
        lo_ref[one, two] = lo
        hi_ref[two, one] = hi.T
        lo_ref[two, one] = lo.T
    for i in range(tiles):
        upper = packed[tops + i * half : tops + (i + 1) * half, :]
        quarter = packed[lasts + i // 2 * half : lasts + (i // 2 + 1) * half, :][:, i % 2 * half : (i % 2 + 1) * half]
        lower = jnp.concatenate([upper[:, half:].T, quarter], axis=1)
        hi, lo = split(jnp.concatenate([upper, lower], axis=0) * factor)
        one = slice(i * TILE, (i + 1) * TILE)
        hi_ref[one, one] = hi
        lo_ref[one, one] = lo
    rows = rows_ref[...]
    rows_hi, rows_lo = split(rows)
    both = jnp.concatenate([rows_hi, rows_lo], axis=0)
    copies = []
    for strip in range(tiles // 2):
        here = slice(strip * 2 * TILE, (strip + 1) * 2 * TILE)
        turned = dot_split(rows_hi, both, hi_ref[:, here], lo_ref[:, here], NN)
        held[:, here] = gain * (1.5 * rows[:, here] - turned)
        copies.append(pltpu.make_async_copy(held.at[:, here], out_ref.at[:, here], sems.at[strip]))
        copies[-1].start()
    for copy in copies:
        copy.wait()


def rotate(halves, rows, total_rows):
    own, total = rows.shape
    return pl.pallas_call(
        functools.partial(rotate_kernel, float(total_rows), sum_order()),
        in_specs=[VM, VM, VM],
        out_specs=HBM,
        out_shape=pltpu.HBM(rows.shape, F32),
        scratch_shapes=[
            pltpu.VMEM((packed_rows(total // TILE), TILE), F32),
            pltpu.VMEM((total, total), BF16),
            pltpu.VMEM((total, total), BF16),
            pltpu.VMEM(rows.shape, F32),
            pltpu.SemaphoreType.DMA((total // TILE // 2,)),
        ],
        compiler_params=params(),
        name="rotate",
    )(*halves, rows).T


def regroup(parts):
    size = lax.axis_size("wide")
    if parts.ndim == 3:
        return lax.all_to_all(parts, "wide", split_axis=0, concat_axis=0, tiled=True)
    count, length = parts.shape
    own = length // size
    parts = parts.reshape(count, size, own).transpose(1, 0, 2).reshape(size, count * own // TILE, TILE)
    parts = lax.all_to_all(parts, "wide", split_axis=0, concat_axis=0, tiled=True)
    return parts.reshape(size * count, own)


def on_device(vectors, blocks, columns, lower_bound, upper_bound):
    length = vectors.shape[1]
    parts = regroup(filtered_parts(vectors, blocks, columns, lower_bound, upper_bound))
    *halves, rows = gram(parts, length // lax.axis_size("wide"))
    return rotate(all_sum(halves), turned(rows, parts.ndim == 3), length * lax.axis_size("narrow"))


def solution(mesh):
    return jax.shard_map(
        on_device,
        mesh=mesh,
        in_specs=(P("wide", "narrow"), P("narrow", None, None, None), P("narrow", None), P(), P()),
        out_specs=P(None, ("narrow", "wide")),
        check_vma=False,
    )
```

```python
import functools

import jax
import jax.numpy as jnp
from jax import lax
from jax.experimental import pallas as pl
from jax.experimental.pallas import tpu as pltpu
from jax.sharding import PartitionSpec as P

REACH = 3
CROSS_PARTS = 4
STEPS = 8
TILE = 128
VM = pl.BlockSpec(memory_space=pltpu.VMEM)
SM = pl.BlockSpec(memory_space=pltpu.SMEM)
HBM = pl.BlockSpec(memory_space=pltpu.HBM)
NT = (((1,), (1,)), ((), ()))
NN = (((1,), (0,)), ((), ()))
F32 = jnp.float32
BF16 = jnp.bfloat16


def params():
    return pltpu.CompilerParams(vmem_limit_bytes=40 * 1024 * 1024)


def split(x):
    hi = x.astype(BF16)
    return hi, (x - hi.astype(F32)).astype(BF16)


def in_hbm(x):
    return pltpu.with_memory_space_constraint(x, pltpu.HBM)


def odd_place(axis):
    return lax.rem(lax.axis_index(axis), 2) == 1


def odd_device():
    return odd_place("narrow")


def dot(a, b, dims):
    return lax.dot_general(a, b, dims, preferred_element_type=F32)


def dot_split(a_hi, a_both, b_hi, b_lo, dims):
    rows = a_hi.shape[0]
    upper = dot(a_both, b_hi, dims)
    return upper[:rows] + (upper[rows:] + dot(a_hi, b_lo, dims))


def cross_at(row, place):
    return sum(REACH - r for r in range(row)) + place + REACH - row


def spread_kernel(total_blocks, columns_hbm, vectors_hbm, blocks_hbm, far_ref, near_ref, vectors_ref, part_ref, hi_ref, lo_ref, held, straight, cross_ref, columns_ref, sems, pair_sems):
    rows, slots, size, _ = blocks_hbm.shape
    edge = far_ref.shape[1]
    odd = odd_device()
    source = [jnp.where(odd, rows - 1 - row, row) for row in range(rows)]
    copies = [
        pltpu.make_async_copy(columns_hbm, columns_ref, sems.at[0]),
        pltpu.make_async_copy(vectors_hbm, straight, sems.at[1]),
    ]
    large = []
    for pair in range(rows // 2):
        begin = jnp.where(odd, rows - 2 - 2 * pair, 2 * pair)
        large.append(pltpu.make_async_copy(blocks_hbm.at[pl.ds(begin, 2)], held.at[pl.ds(2 * pair, 2)], pair_sems.at[pair]))
    for copy in copies + large:
        copy.start()
    hi_ref[...] = jnp.zeros_like(hi_ref)
    lo_ref[...] = jnp.zeros_like(lo_ref)
    cross_ref[...] = jnp.zeros_like(cross_ref)
    first = lax.axis_index("narrow") * rows
    copies[0].wait()
    for row in range(rows):
        pair, half = divmod(row, 2)
        if half == 0:
            large[pair].wait()
        place = 2 * pair + jnp.where(odd, 1 - half, half)
        here = slice(half * size, half * size + size)
        for slot in range(slots):
            offset = columns_ref[slot, source[row]] - (first + source[row])
            offset = jnp.where(offset > REACH, offset - total_blocks, offset)
            offset = jnp.where(offset < -REACH, offset + total_blocks, offset)
            offset = jnp.where(odd, -offset, offset)
            block = held[place, slot]
            hi, lo = split(block)
            there = pl.ds(pl.multiple_of((half + offset + REACH) * size, size), size)
            hi_ref[pair, there, here] = hi.T
            lo_ref[pair, there, here] = lo.T
            if row < REACH:

                @pl.when(row + offset < 0)
                def _():
                    at = pl.multiple_of(cross_at(row, row + offset) * size, size)
                    cross_ref[pl.ds(at, size), :] = block

    count = part_ref.shape[0]
    part_ref[...] = cross_ref[pl.ds(pl.multiple_of(lax.rem(lax.axis_index("wide"), CROSS_PARTS) * count, 8), count), :]
    copies[1].wait()
    whole = straight[...]
    vectors_ref[...] = jnp.where(odd, jnp.concatenate(reversed_blocks(whole, size), axis=1), whole)
    far_ref[...] = vectors_ref[:, :edge]
    near_ref[...] = vectors_ref[:, -edge:]


def spread_part(columns, vectors, blocks, total_blocks):
    rows, slots, size, _ = blocks.shape
    spread = jax.ShapeDtypeStruct((rows // 2, (2 * REACH + 2) * size, 2 * size), BF16)
    edge = jax.ShapeDtypeStruct((vectors.shape[0], REACH * size), F32)
    crossing = REACH * (REACH + 1) // 2 * size
    cross = jax.ShapeDtypeStruct((crossing // CROSS_PARTS, size), F32)
    return pl.pallas_call(
        functools.partial(spread_kernel, total_blocks),
        in_specs=[HBM, HBM, HBM],
        out_specs=[VM] * 6,
        out_shape=[edge, edge, jax.ShapeDtypeStruct(vectors.shape, F32), cross, spread, spread],
        scratch_shapes=[
            pltpu.VMEM(blocks.shape, F32),
            pltpu.VMEM(vectors.shape, F32),
            pltpu.VMEM((crossing, size), F32),
            pltpu.SMEM((slots, rows), jnp.int32),
            pltpu.SemaphoreType.DMA((2,)),
            pltpu.SemaphoreType.DMA((rows // 2,)),
        ],
        compiler_params=params(),
        name="spread_part",
    )(in_hbm(columns.T), in_hbm(vectors), in_hbm(blocks))


class Strip:
    def __init__(self, values, at, size):
        self.hi, lo = split(values)
        self.both = jnp.concatenate([self.hi, lo], axis=0)
        self.at, self.size = at, size

    def band(self, operator, pair, begin, end, half=None):
        hi_ref, lo_ref = operator
        size, start = self.size, 2 * pair - REACH
        there = slice((begin - self.at) * size, (end - self.at) * size)
        inside = slice((begin - start) * size, (end - start) * size)
        rows = slice(None) if half is None else slice(half * size, (half + 1) * size)
        hi, lo = hi_ref[pair, inside, rows], lo_ref[pair, inside, rows]
        return dot_split(self.hi[:, there], self.both[:, there], hi, lo, NN)


def reversed_blocks(edge, size):
    return [edge[:, k * size : (k + 1) * size] for k in reversed(range(edge.shape[1] // size))]


def far_sum(operator, halo, size):
    strip = Strip(jnp.concatenate(reversed_blocks(halo, size), axis=1), -REACH, size)
    outer = strip.band(operator, 0, -REACH, 0)
    inner = strip.band(operator, 1, -1, 0, 0)
    return jnp.concatenate([outer, inner], axis=1)


def near_sum(operator, halo, size):
    pairs = operator[0].shape[0]
    strip = Strip(jnp.concatenate(reversed_blocks(halo, size), axis=1), 2 * pairs, size)
    outer = strip.band(operator, pairs - 1, 2 * pairs, 2 * pairs + REACH)
    inner = strip.band(operator, pairs - 2, 2 * pairs, 2 * pairs + 1, 1)
    return jnp.concatenate([inner, outer], axis=1)


def own_sum(operator, strip, pair, lowest=0):
    pairs = operator[0].shape[0]
    return strip.band(operator, pair, max(2 * pair - REACH, lowest), min(2 * pair + REACH + 2, 2 * pairs))


def first_kernel(terms_ref, vectors_ref, hi_ref, lo_ref, out_ref):
    pairs, _, width = hi_ref.shape
    scale, diag = terms_ref[0:1, :], terms_ref[1:2, :]
    strip = Strip(vectors_ref[...], 0, width // 2)
    for pair in range(pairs):
        here = slice(pair * width, pair * width + width)
        total = scale * own_sum((hi_ref, lo_ref), strip, pair) + diag * vectors_ref[:, here]
        out_ref[:, here] = 0.5 * total


def local_kernel(first_pair, terms_ref, far_ref, mid_ref, near_ref, far_before_ref, mid_before_ref, near_before_ref, hi_ref, lo_ref, out_ref, *full_ref):
    pairs, _, width = hi_ref.shape
    edge, start = near_ref.shape[1], far_ref.shape[1]
    scale, diag = terms_ref[0:1, :], terms_ref[1:2, :]
    current = jnp.concatenate([far_ref[...], mid_ref[:, start:-edge], near_ref[...]], axis=1)
    before = jnp.concatenate([far_before_ref[...], mid_before_ref[:, edge:-edge], near_before_ref[...]], axis=1)
    if full_ref:
        full_ref[0][...] = current
    strip = Strip(current, 0, width // 2)
    for pair in range(first_pair, pairs):
        here = slice(pair * width, pair * width + width)
        total = scale * own_sum((hi_ref, lo_ref), strip, pair) + diag * current[:, here]
        out_ref[:, here] = total - before[:, here]


def second_kernel(terms_ref, mid_ref, near_ref, before_ref, hi_ref, lo_ref, out_ref):
    pairs, _, width = hi_ref.shape
    edge = near_ref.shape[1]
    scale, diag = terms_ref[0:1, :], terms_ref[1:2, :]
    current = jnp.concatenate([mid_ref[:, edge:-edge], near_ref[...]], axis=1)
    padded = jnp.concatenate([jnp.zeros(near_ref.shape, F32), current], axis=1)
    strip = Strip(current, REACH, width // 2)
    for pair in range(pairs):
        here = slice(pair * width, pair * width + width)
        total = scale * own_sum((hi_ref, lo_ref), strip, pair, REACH) + diag * padded[:, here]
        out_ref[:, here] = total - before_ref[:, here]


def step_call(kernel, name, operands, operator, outs):
    size = operands[1].size
    width = operator[0].shape[-1]
    return pl.pallas_call(
        kernel,
        in_specs=[VM] * (len(operands) + 2),
        out_specs=[VM] * len(outs),
        out_shape=[jax.ShapeDtypeStruct(shape, F32) for shape in outs],
        compiler_params=params(),
        cost_estimate=pl.CostEstimate(flops=24 * size * width, bytes_accessed=8 * size, transcendentals=0),
        name=name,
    )(*operands, *operator)


def near_kernel(factor, terms_ref, mid_ref, halo_ref, hi_ref, lo_ref, out_ref):
    size, edge = hi_ref.shape[2] // 2, halo_ref.shape[1]
    scale = factor * terms_ref[0:1, 0:1]
    out_ref[...] = mid_ref[:, -edge:] + scale * near_sum((hi_ref, lo_ref), halo_ref[...], size)


def edge_ahead(operator, scale, diag, far, before, size):
    strip = Strip(far, 0, size)
    outer = strip.band(operator, 0, 0, REACH + 2)
    inner = strip.band(operator, 1, 0, 2 * REACH, 0)
    total = jnp.concatenate([outer, inner], axis=1)
    return scale * total + diag * far[:, : total.shape[1]] - before


def far_kernel(terms_ref, mid_ref, halo_ref, hi_ref, lo_ref, far_ref):
    size, edge = hi_ref.shape[2] // 2, halo_ref.shape[1]
    far_ref[...] = mid_ref[:, :edge] + 0.5 * terms_ref[0:1, 0:1] * far_sum((hi_ref, lo_ref), halo_ref[...], size)


def turn_one_kernel(terms_ref, mid_ref, halo_ref, before_ref, hi_ref, lo_ref, far_ref, send_ref):
    operator = (hi_ref, lo_ref)
    size, edge = hi_ref.shape[2] // 2, halo_ref.shape[1]
    scale, diag = terms_ref[0:1, 0:1], terms_ref[1:2, 0:1]
    edge_rows = mid_ref[:, :edge] + scale * far_sum(operator, halo_ref[...], size)
    far = jnp.concatenate([edge_rows, mid_ref[:, edge : 2 * edge]], axis=1)
    far_ref[...] = far
    send_ref[0] = edge_rows
    send_ref[1] = edge_ahead(operator, scale, diag, far, before_ref[...], size)


def beyond_sum(terms_ref, sent_ref, cross_hi_ref, cross_lo_ref):
    size = cross_hi_ref.shape[1]

    def cross(ref, row):
        rows = [slice(at * size, (at + 1) * size) for at in (cross_at(row, -1 - place) for place in range(REACH - row))]
        return jnp.concatenate([ref[here, :] for here in rows], axis=1)

    own = Strip(sent_ref[0], 0, size)
    pieces = []
    for row in range(REACH):
        there = slice(0, (REACH - row) * size)
        hi, lo = cross(cross_hi_ref, row), cross(cross_lo_ref, row)
        pieces.append(dot_split(own.hi[:, there], own.both[:, there], hi, lo, NT))
    return terms_ref[0:1, 0:1] * jnp.concatenate(pieces, axis=1)


def beyond_kernel(terms_ref, sent_ref, cross_hi_ref, cross_lo_ref, out_ref):
    out_ref[...] = beyond_sum(terms_ref, sent_ref, cross_hi_ref, cross_lo_ref)


def turn(terms_ref, mid_ref, sent_ref, got_ref, beyond_refs, operator):
    size, edge = operator[0].shape[2] // 2, sent_ref.shape[2]
    scale, diag = terms_ref[0:1, 0:1], terms_ref[1:2, 0:1]
    between = sent_ref[1] + scale * far_sum(operator, got_ref[0], size)
    beyond = beyond_refs[0][...] if len(beyond_refs) == 1 else beyond_sum(terms_ref, sent_ref, *beyond_refs)
    beyond = got_ref[1] + beyond
    strip = Strip(jnp.concatenate(reversed_blocks(beyond, size) + [between], axis=1), -REACH, size)
    total = [strip.band(operator, pair, 2 * pair - REACH, REACH) for pair in range(REACH)]
    known = jnp.concatenate([diag * between, jnp.zeros_like(between)], axis=1)
    return between, mid_ref[:, : 2 * edge] + scale * jnp.concatenate(total, axis=1) + known


def cross_kernel(mine_ref, one_ref, two_ref, hi_ref, lo_ref):
    rows = mine_ref.shape[0]
    place = lax.rem(lax.axis_index("wide"), CROSS_PARTS)
    for d, part in enumerate([mine_ref[...], one_ref[...], two_ref[:rows, :], two_ref[rows:, :]]):
        here = chunk_at(place, d, CROSS_PARTS, rows)
        hi, lo = split(part)
        hi_ref[here, :] = hi
        lo_ref[here, :] = lo


def cross_part(mine):
    one = wide_swap(mine, 1)
    two = wide_swap(jnp.concatenate([mine, one]), 2)
    rows, width = mine.shape
    return pl.pallas_call(
        cross_kernel,
        in_specs=[VM] * 3,
        out_specs=[VM] * 2,
        out_shape=[jax.ShapeDtypeStruct((CROSS_PARTS * rows, width), BF16)] * 2,
        compiler_params=params(),
        name="cross_part",
    )(mine, one, two)


def turn_two_kernel(terms_ref, mid_ref, sent_ref, got_ref, *refs):
    *beyond_refs, hi_ref, lo_ref, between_ref, far_ref, send_ref = refs
    operator = (hi_ref, lo_ref)
    size, edge = hi_ref.shape[2] // 2, between_ref.shape[1]
    between, far = turn(terms_ref, mid_ref, sent_ref, got_ref, beyond_refs, operator)
    between_ref[...] = between
    far_ref[...] = far
    send_ref[0] = far[:, :edge]
    send_ref[1] = edge_ahead(operator, terms_ref[0:1, 0:1], terms_ref[1:2, 0:1], far, between, size)


def packs(count, own):
    return own % TILE == TILE // 2 and own > TILE and count % 16 == 0


def last_kernel(parts, terms_ref, mid_ref, sent_ref, got_ref, beyond_ref, near_ref, hi_ref, lo_ref, out_ref):
    size = hi_ref.shape[2] // 2
    _, far = turn(terms_ref, mid_ref, sent_ref, got_ref, (beyond_ref,), (hi_ref, lo_ref))
    whole = jnp.concatenate([far, mid_ref[:, far.shape[1] : -near_ref.shape[1]], near_ref[...]], axis=1)
    mirrored = jnp.concatenate(reversed_blocks(whole, size), axis=1)
    whole = jnp.where(odd_device(), mirrored, whole)
    if len(out_ref.shape) == 2:
        out_ref[...] = whole
        return
    count, own, half = whole.shape[0], whole.shape[1] // parts, TILE // 2
    for part in range(parts):
        begin = part * own
        head, tail = (begin, begin + own - half) if part % 2 == 0 else (begin + half, begin)
        at = 0
        for column in range(head, head + own - half, TILE):
            out_ref[part, at : at + count, :] = whole[:, column : column + TILE]
            at += count
        tails = whole[:, tail : tail + half]
        out_ref[part, at:, :] = jnp.concatenate([tails[: count // 2], tails[count // 2 :]], axis=1)


def far_swap(x):
    size = lax.axis_size("narrow")
    return lax.ppermute(x, "narrow", [(i, (i + 1) % size if i % 2 else (i - 1) % size) for i in range(size)])


def wide_swap(x, mask):
    return lax.ppermute(x, "wide", [(i, i ^ mask) for i in range(lax.axis_size("wide"))])


def near_swap(x):
    return lax.ppermute(x, "narrow", [(i, i ^ 1) for i in range(lax.axis_size("narrow"))])


def filtered_parts(vectors, blocks, columns, lower_bound, upper_bound):
    size = blocks.shape[2]
    width, edge, parts = 2 * size, REACH * size, lax.axis_size("wide")
    count, length = vectors.shape
    half_width = (upper_bound - lower_bound) * 0.5
    scale = 2.0 / half_width
    diag = scale * (1.0 - (upper_bound + lower_bound) * 0.5)
    terms = jnp.concatenate([jnp.broadcast_to(scale, (1, width)), jnp.broadcast_to(diag, (1, width))])
    total_blocks = blocks.shape[0] * lax.axis_size("narrow")
    far, near, vectors, cross, *operator = spread_part(columns, vectors, blocks, total_blocks)
    whole, side, double = (count, length), (count, edge), (2, count, edge)

    def near_part(factor, mid, halo):
        kernel = functools.partial(near_kernel, factor)
        return step_call(kernel, "near_part", (terms, mid, halo), operator, [side])[0]

    def local_part(first_pair, outs):
        kernel = functools.partial(local_kernel, first_pair)
        return step_call(kernel, "local_part", (terms, far, mid, near, *before), operator, [whole] * outs)

    halo, near_halo = far_swap(far), near_swap(near)
    cross = cross_part(far_swap(cross))
    (mid,) = step_call(first_kernel, "first_part", (terms, vectors), operator, [whole])
    before = (far, vectors, near)
    near = near_part(0.5, mid, near_halo)
    (far,) = step_call(far_kernel, "far_part", (terms, mid, halo), operator, [side])
    halo, near_halo = far_swap(far), near_swap(near)
    (next_mid,) = local_part(0, 1)
    before = (far, mid, near)
    mid, near = next_mid, near_part(1.0, next_mid, near_halo)
    far, send = step_call(turn_one_kernel, "turn_one", (terms, mid, halo, far), operator, [(count, 2 * edge), double])
    for step in range(2, STEPS, 2):
        got, near_halo = far_swap(send), near_swap(near)
        mid, full = local_part(1, 2)
        near = near_part(1.0, mid, near_halo)
        near_halo = near_swap(near)
        (next_mid,) = step_call(second_kernel, "second_part", (terms, mid, near, full), operator, [whole])
        next_near = near_part(1.0, next_mid, near_halo)
        beyond = cross
        if step > 2:
            beyond = step_call(beyond_kernel, "beyond_part", (terms, send), cross, [side])
        operands = (terms, next_mid, send, got, *beyond)
        if step < STEPS - 2:
            outs = [side, (count, 2 * edge), double]
            between, far, send = step_call(turn_two_kernel, "turn_two", operands, operator, outs)
            before = (between, mid, near)
        mid, near = next_mid, next_near
    shape = (parts, count * length // parts // TILE, TILE) if packs(count, length // parts) else whole
    return step_call(functools.partial(last_kernel, parts), "last_part", (*operands, near), operator, [shape])[0]


def pair_perm(mask):
    narrow, wide = lax.axis_size("narrow"), lax.axis_size("wide")
    return [(n * wide + w, (n ^ mask[0]) * wide + (w ^ mask[1])) for n in range(narrow) for w in range(wide)]


def swap(x, mask):
    return lax.ppermute(x, ("narrow", "wide"), pair_perm(mask))


def bit_groups():
    narrow = [(1 << b, 0) for b in range(lax.axis_size("narrow").bit_length() - 1)]
    wide = [(0, 1 << b) for b in range(lax.axis_size("wide").bit_length() - 1)]
    rest = wide[1:] + narrow[2:]
    return [narrow[:1], narrow[1:2] + wide[:1]] + [rest[i : i + 2] for i in range(0, len(rest), 2)]


def masks(bits):
    out = []
    for d in range(1 << len(bits)):
        chosen = [b for k, b in enumerate(bits) if d >> k & 1]
        out.append((sum(b[0] for b in chosen), sum(b[1] for b in chosen)))
    return out


def place_in(bits):
    n, w = lax.axis_index("narrow"), lax.axis_index("wide")
    place = 0
    for k, b in enumerate(bits):
        bit = lax.rem(lax.div(n, b[0]), 2) if b[0] else lax.rem(lax.div(w, b[1]), 2)
        place = place + bit * (1 << k)
    return place


def relative(place, d, count):
    out = 0
    for k in range(count.bit_length() - 1):
        bit = lax.rem(lax.div(place, 1 << k), 2)
        out = out + (1 << k) * (1 - bit if d >> k & 1 else bit)
    return out


def chunk_at(place, d, count, rows):
    return pl.ds(pl.multiple_of(relative(place, d, count) * rows, 8), rows)


def fold_kernel(bits, *refs):
    count = 1 << len(bits)
    parts, outs = refs[:-count], refs[-count:]
    place = place_in(bits)
    rows = outs[0].shape[0]
    for d in range(count):
        here = chunk_at(place, d, count, rows)
        total = parts[0][here, :]
        for part in parts[1:]:
            total = total + part[here, :]
        outs[d][...] = total


def fold(parts, bits):
    count = 1 << len(bits)
    rows, width = parts[0].shape
    return pl.pallas_call(
        functools.partial(fold_kernel, bits),
        in_specs=[VM] * len(parts),
        out_specs=[VM] * count,
        out_shape=[jax.ShapeDtypeStruct((rows // count, width), F32)] * count,
        compiler_params=params(),
        name="fold",
    )(*parts)


def fan(parts, bits):
    members = masks(bits)
    return [parts[0]] + [swap(parts[d], members[d]) for d in range(1, len(members))]


def all_sum(halves):
    groups = bit_groups()
    parts = fan(halves, groups[0])
    for bits in groups[1:-1]:
        parts = fan(fold(parts, bits), bits)
    x = sum(parts)
    x = sum(fan([x] * (1 << len(groups[-1])), groups[-1]))
    for bits in groups[1:-1][::-1]:
        blocks = fan([x] * (1 << len(bits)), bits)
        x = jnp.concatenate(blocks)
    return x, swap(x, masks(groups[0])[1])


def sum_order():
    groups = bit_groups()
    return groups[1:-1]


def tile_pairs(count):
    return [(i, j) for i in range(count) for j in range(i + 1, count)]


def packed_rows(count):
    rows = len(tile_pairs(count)) * TILE + count * TILE // 2 + count // 2 * TILE // 2
    blocks = 8
    for bits in bit_groups()[:-1]:
        blocks <<= len(bits)
    return -(-rows // blocks) * blocks


def gram_kernel(own, parts_ref, keep_ref, send_ref, rows_ref, packed):
    if parts_ref.ndim == 2:
        rows = parts_ref[...]
    else:
        parts, length, _ = parts_ref.shape
        count, half = length * TILE // own, TILE // 2
        heads = (own - half) // TILE
        pieces = []
        for part in range(parts):
            head = [parts_ref[part, h * count : (h + 1) * count, :] for h in range(heads)]
            tails = parts_ref[part, heads * count :, :]
            swapped = pltpu.roll(tails, half, 1)
            low = lax.broadcasted_iota(jnp.int32, tails.shape, 1) < half
            tail = jnp.concatenate([jnp.where(low, tails, swapped), jnp.where(low, swapped, tails)], axis=0)
            pieces.append(jnp.concatenate(head + [tail], axis=1)[:, :own])
        rows = jnp.concatenate(pieces, axis=0)
    rows_ref[...] = rows
    tiles, half = rows.shape[0] // TILE, TILE // 2
    hi, lo = split(rows)
    at, tops = 0, len(tile_pairs(tiles)) * TILE
    lasts = tops + tiles * half
    for i in range(tiles):
        here, there = slice(i * TILE, (i + 1) * TILE), slice(i * TILE, None)
        both = jnp.concatenate([hi[here], lo[here]], axis=0)
        strip = dot_split(hi[here], both, hi[there], lo[there], NT)
        packed[tops + i * half : tops + (i + 1) * half, :] = strip[:half, :TILE]
        last = strip[half:, half:TILE]
        if i % 2 == 0:
            held = last
        else:
            packed[lasts + i // 2 * half : lasts + (i // 2 + 1) * half, :] = jnp.concatenate([held, last], axis=1)
        for j in range(i + 1, tiles):
            packed[at : at + TILE, :] = strip[:, (j - i) * TILE : (j - i + 1) * TILE]
            at += TILE
    used = lasts + tiles // 2 * half
    if used < packed.shape[0]:
        packed[used:, :] = jnp.zeros((packed.shape[0] - used, TILE), F32)
    odd, size = odd_device(), keep_ref.shape[0]
    keep_ref[...] = packed[pl.ds(pl.multiple_of(jnp.where(odd, size, 0), 8), size), :]
    send_ref[...] = packed[pl.ds(pl.multiple_of(jnp.where(odd, 0, size), 8), size), :]


def gram(parts, own):
    total = parts.size // own
    size = packed_rows(total // TILE)
    half = jax.ShapeDtypeStruct((size // 2, TILE), F32)
    return pl.pallas_call(
        functools.partial(gram_kernel, own),
        in_specs=[VM],
        out_specs=[VM] * 3,
        out_shape=[half, half, jax.ShapeDtypeStruct((total, own), F32)],
        scratch_shapes=[pltpu.VMEM((size, TILE), F32)],
        compiler_params=params(),
        name="gram",
    )(parts)


def turned_kernel(packed, rows_ref, out_ref):
    rows = rows_ref[...].T
    if packed:
        half = TILE // 2
        rows = jnp.where(odd_place("wide"), jnp.concatenate([rows[-half:], rows[:-half]], axis=0), rows)
    out_ref[...] = rows


def turned(rows, packed):
    return pl.pallas_call(
        functools.partial(turned_kernel, packed),
        in_specs=[VM],
        out_specs=VM,
        out_shape=jax.ShapeDtypeStruct(rows.shape[::-1], F32),
        compiler_params=params(),
        name="turned",
    )(rows)


def rotate_kernel(total_rows, groups, own_ref, other_ref, rows_ref, out_ref, packed, hi_ref, lo_ref, held, sems):
    size = own_ref.shape[0]
    places = [place_in(bits) for bits in groups]
    blocks = 1
    for bits in groups:
        blocks <<= len(bits)
    length = size // blocks
    odd = odd_device()
    for block in range(blocks):
        at, rest, step = 0, block, blocks
        for bits, place in zip(groups, places):
            count = 1 << len(bits)
            step //= count
            at = at + relative(place, rest // step, count) * (step * length)
            rest %= step
        here = slice(block * length, (block + 1) * length)
        packed[pl.ds(pl.multiple_of(jnp.where(odd, size, 0) + at, 8), length), :] = own_ref[here, :]
        packed[pl.ds(pl.multiple_of(jnp.where(odd, 0, size) + at, 8), length), :] = other_ref[here, :]
    tiles, half = rows_ref.shape[1] // TILE, TILE // 2
    order = tile_pairs(tiles)
    tops = len(order) * TILE
    lasts = tops + tiles * half
    above = packed[:tops, :].reshape(len(order), TILE, TILE)
    squares = jnp.sum(above * above, axis=0) * 2.0
    top = packed[tops:lasts, :].reshape(tiles, half, TILE)
    weight = jnp.where(lax.broadcasted_iota(jnp.int32, (half, TILE), 1) < half, 1.0, 2.0)
    last = packed[lasts : lasts + tiles // 2 * half, :].reshape(tiles // 2, half, TILE)
    squares = squares[:half] + squares[half:] + jnp.sum(top * top, axis=0) * weight + jnp.sum(last * last, axis=0)
    frob = jnp.sqrt(jnp.sum(squares, axis=(0, 1), keepdims=True) + 1e-06)
    factor = 0.5 / frob
    gain = jnp.sqrt(total_rows / frob)
    for at, (i, j) in enumerate(order):
        hi, lo = split(packed[at * TILE : (at + 1) * TILE, :] * factor)
        one, two = slice(i * TILE, (i + 1) * TILE), slice(j * TILE, (j + 1) * TILE)
        hi_ref[one, two] = hi
        lo_ref[one, two] = lo
        hi_ref[two, one] = hi.T
        lo_ref[two, one] = lo.T
    for i in range(tiles):
        upper = packed[tops + i * half : tops + (i + 1) * half, :]
        quarter = packed[lasts + i // 2 * half : lasts + (i // 2 + 1) * half, :][:, i % 2 * half : (i % 2 + 1) * half]
        lower = jnp.concatenate([upper[:, half:].T, quarter], axis=1)
        hi, lo = split(jnp.concatenate([upper, lower], axis=0) * factor)
        one = slice(i * TILE, (i + 1) * TILE)
        hi_ref[one, one] = hi
        lo_ref[one, one] = lo
    rows = rows_ref[...]
    rows_hi, rows_lo = split(rows)
    both = jnp.concatenate([rows_hi, rows_lo], axis=0)
    copies = []
    for strip in range(tiles // 2):
        here = slice(strip * 2 * TILE, (strip + 1) * 2 * TILE)
        turned = dot_split(rows_hi, both, hi_ref[:, here], lo_ref[:, here], NN)
        held[:, here] = gain * (1.5 * rows[:, here] - turned)
        copies.append(pltpu.make_async_copy(held.at[:, here], out_ref.at[:, here], sems.at[strip]))
        copies[-1].start()
    for copy in copies:
        copy.wait()


def rotate(halves, rows, total_rows):
    own, total = rows.shape
    return pl.pallas_call(
        functools.partial(rotate_kernel, float(total_rows), sum_order()),
        in_specs=[VM, VM, VM],
        out_specs=HBM,
        out_shape=pltpu.HBM(rows.shape, F32),
        scratch_shapes=[
            pltpu.VMEM((packed_rows(total // TILE), TILE), F32),
            pltpu.VMEM((total, total), BF16),
            pltpu.VMEM((total, total), BF16),
            pltpu.VMEM(rows.shape, F32),
            pltpu.SemaphoreType.DMA((total // TILE // 2,)),
        ],
        compiler_params=params(),
        name="rotate",
    )(*halves, rows).T


def regroup(parts):
    size = lax.axis_size("wide")
    if parts.ndim == 3:
        return lax.all_to_all(parts, "wide", split_axis=0, concat_axis=0, tiled=True)
    count, length = parts.shape
    own = length // size
    parts = parts.reshape(count, size, own).transpose(1, 0, 2).reshape(size, count * own // TILE, TILE)
    parts = lax.all_to_all(parts, "wide", split_axis=0, concat_axis=0, tiled=True)
    return parts.reshape(size * count, own)


def on_device(vectors, blocks, columns, lower_bound, upper_bound):
    length = vectors.shape[1]
    parts = regroup(filtered_parts(vectors, blocks, columns, lower_bound, upper_bound))
    *halves, rows = gram(parts, length // lax.axis_size("wide"))
    return rotate(all_sum(halves), turned(rows, parts.ndim == 3), length * lax.axis_size("narrow"))


def solution(mesh):
    return jax.shard_map(
        on_device,
        mesh=mesh,
        in_specs=(P("wide", "narrow"), P("narrow", None, None, None), P("narrow", None), P(), P()),
        out_specs=P(None, ("narrow", "wide")),
        check_vma=False,
    )
```

```python
import functools

import jax
import jax.numpy as jnp
from jax import lax
from jax.experimental import pallas as pl
from jax.experimental.pallas import tpu as pltpu
from jax.sharding import PartitionSpec as P

REACH = 3
CROSS_PARTS = 4
STEPS = 8
TILE = 128
VM = pl.BlockSpec(memory_space=pltpu.VMEM)
SM = pl.BlockSpec(memory_space=pltpu.SMEM)
HBM = pl.BlockSpec(memory_space=pltpu.HBM)
NT = (((1,), (1,)), ((), ()))
NN = (((1,), (0,)), ((), ()))
F32 = jnp.float32
BF16 = jnp.bfloat16


def params():
    return pltpu.CompilerParams(vmem_limit_bytes=40 * 1024 * 1024)


def split(x):
    hi = x.astype(BF16)
    return hi, (x - hi.astype(F32)).astype(BF16)


def in_hbm(x):
    return pltpu.with_memory_space_constraint(x, pltpu.HBM)


def odd_place(axis):
    return lax.rem(lax.axis_index(axis), 2) == 1


def odd_device():
    return odd_place("narrow")


def dot(a, b, dims):
    return lax.dot_general(a, b, dims, preferred_element_type=F32)


def dot_split(a_hi, a_both, b_hi, b_lo, dims):
    rows = a_hi.shape[0]
    upper = dot(a_both, b_hi, dims)
    return upper[:rows] + (upper[rows:] + dot(a_hi, b_lo, dims))


def cross_at(row, place):
    return sum(REACH - r for r in range(row)) + place + REACH - row


def spread_kernel(total_blocks, columns_hbm, vectors_hbm, blocks_hbm, far_ref, near_ref, vectors_ref, part_ref, hi_ref, lo_ref, held, straight, cross_ref, columns_ref, sems, pair_sems):
    rows, slots, size, _ = blocks_hbm.shape
    edge = far_ref.shape[1]
    odd = odd_device()
    source = [jnp.where(odd, rows - 1 - row, row) for row in range(rows)]
    copies = [
        pltpu.make_async_copy(columns_hbm, columns_ref, sems.at[0]),
        pltpu.make_async_copy(vectors_hbm, straight, sems.at[1]),
    ]
    large = []
    for pair in range(rows // 2):
        begin = jnp.where(odd, rows - 2 - 2 * pair, 2 * pair)
        large.append(pltpu.make_async_copy(blocks_hbm.at[pl.ds(begin, 2)], held.at[pl.ds(2 * pair, 2)], pair_sems.at[pair]))
    for copy in copies + large:
        copy.start()
    hi_ref[...] = jnp.zeros_like(hi_ref)
    lo_ref[...] = jnp.zeros_like(lo_ref)
    cross_ref[...] = jnp.zeros_like(cross_ref)
    first = lax.axis_index("narrow") * rows
    copies[0].wait()
    for row in range(rows):
        pair, half = divmod(row, 2)
        if half == 0:
            large[pair].wait()
        place = 2 * pair + jnp.where(odd, 1 - half, half)
        here = slice(half * size, half * size + size)
        for slot in range(slots):
            offset = columns_ref[slot, source[row]] - (first + source[row])
            offset = jnp.where(offset > REACH, offset - total_blocks, offset)
            offset = jnp.where(offset < -REACH, offset + total_blocks, offset)
            offset = jnp.where(odd, -offset, offset)
            block = held[place, slot]
            hi, lo = split(block)
            there = pl.ds(pl.multiple_of((half + offset + REACH) * size, size), size)
            hi_ref[pair, there, here] = hi.T
            lo_ref[pair, there, here] = lo.T
            if row < REACH:

                @pl.when(row + offset < 0)
                def _():
                    at = pl.multiple_of(cross_at(row, row + offset) * size, size)
                    cross_ref[pl.ds(at, size), :] = block

    count = part_ref.shape[0]
    part_ref[...] = cross_ref[pl.ds(pl.multiple_of(lax.rem(lax.axis_index("wide"), CROSS_PARTS) * count, 8), count), :]
    copies[1].wait()
    whole = straight[...]
    vectors_ref[...] = jnp.where(odd, jnp.concatenate(reversed_blocks(whole, size), axis=1), whole)
    far_ref[...] = vectors_ref[:, :edge]
    near_ref[...] = vectors_ref[:, -edge:]


def spread_part(columns, vectors, blocks, total_blocks):
    rows, slots, size, _ = blocks.shape
    spread = jax.ShapeDtypeStruct((rows // 2, (2 * REACH + 2) * size, 2 * size), BF16)
    edge = jax.ShapeDtypeStruct((vectors.shape[0], REACH * size), F32)
    crossing = REACH * (REACH + 1) // 2 * size
    cross = jax.ShapeDtypeStruct((crossing // CROSS_PARTS, size), F32)
    return pl.pallas_call(
        functools.partial(spread_kernel, total_blocks),
        in_specs=[HBM, HBM, HBM],
        out_specs=[VM] * 6,
        out_shape=[edge, edge, jax.ShapeDtypeStruct(vectors.shape, F32), cross, spread, spread],
        scratch_shapes=[
            pltpu.VMEM(blocks.shape, F32),
            pltpu.VMEM(vectors.shape, F32),
            pltpu.VMEM((crossing, size), F32),
            pltpu.SMEM((slots, rows), jnp.int32),
            pltpu.SemaphoreType.DMA((2,)),
            pltpu.SemaphoreType.DMA((rows // 2,)),
        ],
        compiler_params=params(),
        name="spread_part",
    )(in_hbm(columns.T), in_hbm(vectors), in_hbm(blocks))


class Strip:
    def __init__(self, values, at, size):
        self.hi, lo = split(values)
        self.both = jnp.concatenate([self.hi, lo], axis=0)
        self.at, self.size = at, size

    def band(self, operator, pair, begin, end, half=None):
        hi_ref, lo_ref = operator
        size, start = self.size, 2 * pair - REACH
        there = slice((begin - self.at) * size, (end - self.at) * size)
        inside = slice((begin - start) * size, (end - start) * size)
        rows = slice(None) if half is None else slice(half * size, (half + 1) * size)
        hi, lo = hi_ref[pair, inside, rows], lo_ref[pair, inside, rows]
        return dot_split(self.hi[:, there], self.both[:, there], hi, lo, NN)


def reversed_blocks(edge, size):
    return [edge[:, k * size : (k + 1) * size] for k in reversed(range(edge.shape[1] // size))]


def far_sum(operator, halo, size):
    strip = Strip(jnp.concatenate(reversed_blocks(halo, size), axis=1), -REACH, size)
    outer = strip.band(operator, 0, -REACH, 0)
    inner = strip.band(operator, 1, -1, 0, 0)
    return jnp.concatenate([outer, inner], axis=1)


def near_sum(operator, halo, size):
    pairs = operator[0].shape[0]
    strip = Strip(jnp.concatenate(reversed_blocks(halo, size), axis=1), 2 * pairs, size)
    outer = strip.band(operator, pairs - 1, 2 * pairs, 2 * pairs + REACH)
    inner = strip.band(operator, pairs - 2, 2 * pairs, 2 * pairs + 1, 1)
    return jnp.concatenate([inner, outer], axis=1)


def own_sum(operator, strip, pair, lowest=0):
    pairs = operator[0].shape[0]
    return strip.band(operator, pair, max(2 * pair - REACH, lowest), min(2 * pair + REACH + 2, 2 * pairs))


def first_kernel(terms_ref, vectors_ref, hi_ref, lo_ref, out_ref):
    pairs, _, width = hi_ref.shape
    scale, diag = terms_ref[0:1, :], terms_ref[1:2, :]
    strip = Strip(vectors_ref[...], 0, width // 2)
    for pair in range(pairs):
        here = slice(pair * width, pair * width + width)
        total = scale * own_sum((hi_ref, lo_ref), strip, pair) + diag * vectors_ref[:, here]
        out_ref[:, here] = 0.5 * total


def local_kernel(first_pair, terms_ref, far_ref, mid_ref, near_ref, far_before_ref, mid_before_ref, near_before_ref, hi_ref, lo_ref, out_ref, *full_ref):
    pairs, _, width = hi_ref.shape
    edge, start = near_ref.shape[1], far_ref.shape[1]
    scale, diag = terms_ref[0:1, :], terms_ref[1:2, :]
    current = jnp.concatenate([far_ref[...], mid_ref[:, start:-edge], near_ref[...]], axis=1)
    before = jnp.concatenate([far_before_ref[...], mid_before_ref[:, edge:-edge], near_before_ref[...]], axis=1)
    if full_ref:
        full_ref[0][...] = current
    strip = Strip(current, 0, width // 2)
    for pair in range(first_pair, pairs):
        here = slice(pair * width, pair * width + width)
        total = scale * own_sum((hi_ref, lo_ref), strip, pair) + diag * current[:, here]
        out_ref[:, here] = total - before[:, here]


def second_kernel(terms_ref, mid_ref, near_ref, before_ref, hi_ref, lo_ref, out_ref):
    pairs, _, width = hi_ref.shape
    edge = near_ref.shape[1]
    scale, diag = terms_ref[0:1, :], terms_ref[1:2, :]
    current = jnp.concatenate([mid_ref[:, edge:-edge], near_ref[...]], axis=1)
    padded = jnp.concatenate([jnp.zeros(near_ref.shape, F32), current], axis=1)
    strip = Strip(current, REACH, width // 2)
    for pair in range(pairs):
        here = slice(pair * width, pair * width + width)
        total = scale * own_sum((hi_ref, lo_ref), strip, pair, REACH) + diag * padded[:, here]
        out_ref[:, here] = total - before_ref[:, here]


def step_call(kernel, name, operands, operator, outs):
    size = operands[1].size
    width = operator[0].shape[-1]
    return pl.pallas_call(
        kernel,
        in_specs=[VM] * (len(operands) + 2),
        out_specs=[VM] * len(outs),
        out_shape=[jax.ShapeDtypeStruct(shape, F32) for shape in outs],
        compiler_params=params(),
        cost_estimate=pl.CostEstimate(flops=24 * size * width, bytes_accessed=8 * size, transcendentals=0),
        name=name,
    )(*operands, *operator)


def near_kernel(factor, terms_ref, mid_ref, halo_ref, hi_ref, lo_ref, out_ref):
    size, edge = hi_ref.shape[2] // 2, halo_ref.shape[1]
    scale = factor * terms_ref[0:1, 0:1]
    out_ref[...] = mid_ref[:, -edge:] + scale * near_sum((hi_ref, lo_ref), halo_ref[...], size)


def edge_ahead(operator, scale, diag, far, before, size):
    strip = Strip(far, 0, size)
    outer = strip.band(operator, 0, 0, REACH + 2)
    inner = strip.band(operator, 1, 0, 2 * REACH, 0)
    total = jnp.concatenate([outer, inner], axis=1)
    return scale * total + diag * far[:, : total.shape[1]] - before


def far_kernel(terms_ref, mid_ref, halo_ref, hi_ref, lo_ref, far_ref):
    size, edge = hi_ref.shape[2] // 2, halo_ref.shape[1]
    far_ref[...] = mid_ref[:, :edge] + 0.5 * terms_ref[0:1, 0:1] * far_sum((hi_ref, lo_ref), halo_ref[...], size)


def turn_one_kernel(terms_ref, mid_ref, halo_ref, before_ref, hi_ref, lo_ref, far_ref, send_ref):
    operator = (hi_ref, lo_ref)
    size, edge = hi_ref.shape[2] // 2, halo_ref.shape[1]
    scale, diag = terms_ref[0:1, 0:1], terms_ref[1:2, 0:1]
    edge_rows = mid_ref[:, :edge] + scale * far_sum(operator, halo_ref[...], size)
    far = jnp.concatenate([edge_rows, mid_ref[:, edge : 2 * edge]], axis=1)
    far_ref[...] = far
    send_ref[0] = edge_rows
    send_ref[1] = edge_ahead(operator, scale, diag, far, before_ref[...], size)


def beyond_sum(terms_ref, sent_ref, cross_hi_ref, cross_lo_ref):
    size = cross_hi_ref.shape[1]

    def cross(ref, row):
        rows = [slice(at * size, (at + 1) * size) for at in (cross_at(row, -1 - place) for place in range(REACH - row))]
        return jnp.concatenate([ref[here, :] for here in rows], axis=1)

    own = Strip(sent_ref[0], 0, size)
    pieces = []
    for row in range(REACH):
        there = slice(0, (REACH - row) * size)
        hi, lo = cross(cross_hi_ref, row), cross(cross_lo_ref, row)
        pieces.append(dot_split(own.hi[:, there], own.both[:, there], hi, lo, NT))
    return terms_ref[0:1, 0:1] * jnp.concatenate(pieces, axis=1)


def beyond_kernel(terms_ref, sent_ref, cross_hi_ref, cross_lo_ref, out_ref):
    out_ref[...] = beyond_sum(terms_ref, sent_ref, cross_hi_ref, cross_lo_ref)


def turn(terms_ref, mid_ref, sent_ref, got_ref, beyond_refs, operator):
    size, edge = operator[0].shape[2] // 2, sent_ref.shape[2]
    scale, diag = terms_ref[0:1, 0:1], terms_ref[1:2, 0:1]
    between = sent_ref[1] + scale * far_sum(operator, got_ref[0], size)
    beyond = beyond_refs[0][...] if len(beyond_refs) == 1 else beyond_sum(terms_ref, sent_ref, *beyond_refs)
    beyond = got_ref[1] + beyond
    strip = Strip(jnp.concatenate(reversed_blocks(beyond, size) + [between], axis=1), -REACH, size)
    total = [strip.band(operator, pair, 2 * pair - REACH, REACH) for pair in range(REACH)]
    known = jnp.concatenate([diag * between, jnp.zeros_like(between)], axis=1)
    return between, mid_ref[:, : 2 * edge] + scale * jnp.concatenate(total, axis=1) + known


def cross_kernel(mine_ref, one_ref, two_ref, hi_ref, lo_ref):
    rows = mine_ref.shape[0]
    place = lax.rem(lax.axis_index("wide"), CROSS_PARTS)
    for d, part in enumerate([mine_ref[...], one_ref[...], two_ref[:rows, :], two_ref[rows:, :]]):
        here = chunk_at(place, d, CROSS_PARTS, rows)
        hi, lo = split(part)
        hi_ref[here, :] = hi
        lo_ref[here, :] = lo


def cross_part(mine):
    one = wide_swap(mine, 1)
    two = wide_swap(jnp.concatenate([mine, one]), 2)
    rows, width = mine.shape
    return pl.pallas_call(
        cross_kernel,
        in_specs=[VM] * 3,
        out_specs=[VM] * 2,
        out_shape=[jax.ShapeDtypeStruct((CROSS_PARTS * rows, width), BF16)] * 2,
        compiler_params=params(),
        name="cross_part",
    )(mine, one, two)


def turn_two_kernel(terms_ref, mid_ref, sent_ref, got_ref, *refs):
    *beyond_refs, hi_ref, lo_ref, between_ref, far_ref, send_ref = refs
    operator = (hi_ref, lo_ref)
    size, edge = hi_ref.shape[2] // 2, between_ref.shape[1]
    between, far = turn(terms_ref, mid_ref, sent_ref, got_ref, beyond_refs, operator)
    between_ref[...] = between
    far_ref[...] = far
    send_ref[0] = far[:, :edge]
    send_ref[1] = edge_ahead(operator, terms_ref[0:1, 0:1], terms_ref[1:2, 0:1], far, between, size)


def packs(count, own):
    return own % TILE == TILE // 2 and own > TILE and count % 16 == 0


def last_kernel(parts, terms_ref, mid_ref, sent_ref, got_ref, beyond_ref, near_ref, hi_ref, lo_ref, out_ref):
    size = hi_ref.shape[2] // 2
    _, far = turn(terms_ref, mid_ref, sent_ref, got_ref, (beyond_ref,), (hi_ref, lo_ref))
    whole = jnp.concatenate([far, mid_ref[:, far.shape[1] : -near_ref.shape[1]], near_ref[...]], axis=1)
    mirrored = jnp.concatenate(reversed_blocks(whole, size), axis=1)
    whole = jnp.where(odd_device(), mirrored, whole)
    if len(out_ref.shape) == 2:
        out_ref[...] = whole
        return
    count, own, half = whole.shape[0], whole.shape[1] // parts, TILE // 2
    for part in range(parts):
        begin = part * own
        head, tail = (begin, begin + own - half) if part % 2 == 0 else (begin + half, begin)
        at = 0
        for column in range(head, head + own - half, TILE):
            out_ref[part, at : at + count, :] = whole[:, column : column + TILE]
            at += count
        tails = whole[:, tail : tail + half]
        out_ref[part, at:, :] = jnp.concatenate([tails[: count // 2], tails[count // 2 :]], axis=1)


def far_swap(x):
    size = lax.axis_size("narrow")
    return lax.ppermute(x, "narrow", [(i, (i + 1) % size if i % 2 else (i - 1) % size) for i in range(size)])


def wide_swap(x, mask):
    return lax.ppermute(x, "wide", [(i, i ^ mask) for i in range(lax.axis_size("wide"))])


def near_swap(x):
    return lax.ppermute(x, "narrow", [(i, i ^ 1) for i in range(lax.axis_size("narrow"))])


def filtered_parts(vectors, blocks, columns, lower_bound, upper_bound):
    size = blocks.shape[2]
    width, edge, parts = 2 * size, REACH * size, lax.axis_size("wide")
    count, length = vectors.shape
    half_width = (upper_bound - lower_bound) * 0.5
    scale = 2.0 / half_width
    diag = scale * (1.0 - (upper_bound + lower_bound) * 0.5)
    terms = jnp.concatenate([jnp.broadcast_to(scale, (1, width)), jnp.broadcast_to(diag, (1, width))])
    total_blocks = blocks.shape[0] * lax.axis_size("narrow")
    far, near, vectors, cross, *operator = spread_part(columns, vectors, blocks, total_blocks)
    whole, side, double = (count, length), (count, edge), (2, count, edge)

    def near_part(factor, mid, halo):
        kernel = functools.partial(near_kernel, factor)
        return step_call(kernel, "near_part", (terms, mid, halo), operator, [side])[0]

    def local_part(first_pair, outs):
        kernel = functools.partial(local_kernel, first_pair)
        return step_call(kernel, "local_part", (terms, far, mid, near, *before), operator, [whole] * outs)

    halo, near_halo = far_swap(far), near_swap(near)
    cross = cross_part(far_swap(cross))
    (mid,) = step_call(first_kernel, "first_part", (terms, vectors), operator, [whole])
    before = (far, vectors, near)
    near = near_part(0.5, mid, near_halo)
    (far,) = step_call(far_kernel, "far_part", (terms, mid, halo), operator, [side])
    halo, near_halo = far_swap(far), near_swap(near)
    (next_mid,) = local_part(0, 1)
    before = (far, mid, near)
    mid, near = next_mid, near_part(1.0, next_mid, near_halo)
    far, send = step_call(turn_one_kernel, "turn_one", (terms, mid, halo, far), operator, [(count, 2 * edge), double])
    for step in range(2, STEPS, 2):
        got, near_halo = far_swap(send), near_swap(near)
        mid, full = local_part(1, 2)
        near = near_part(1.0, mid, near_halo)
        near_halo = near_swap(near)
        (next_mid,) = step_call(second_kernel, "second_part", (terms, mid, near, full), operator, [whole])
        next_near = near_part(1.0, next_mid, near_halo)
        beyond = cross
        if step > 2:
            beyond = step_call(beyond_kernel, "beyond_part", (terms, send), cross, [side])
        operands = (terms, next_mid, send, got, *beyond)
        if step < STEPS - 2:
            outs = [side, (count, 2 * edge), double]
            between, far, send = step_call(turn_two_kernel, "turn_two", operands, operator, outs)
            before = (between, mid, near)
        mid, near = next_mid, next_near
    shape = (parts, count * length // parts // TILE, TILE) if packs(count, length // parts) else whole
    return step_call(functools.partial(last_kernel, parts), "last_part", (*operands, near), operator, [shape])[0]


def pair_perm(mask):
    narrow, wide = lax.axis_size("narrow"), lax.axis_size("wide")
    return [(n * wide + w, (n ^ mask[0]) * wide + (w ^ mask[1])) for n in range(narrow) for w in range(wide)]


def swap(x, mask):
    return lax.ppermute(x, ("narrow", "wide"), pair_perm(mask))


def bit_groups():
    narrow = [(1 << b, 0) for b in range(lax.axis_size("narrow").bit_length() - 1)]
    wide = [(0, 1 << b) for b in range(lax.axis_size("wide").bit_length() - 1)]
    rest = wide[1:] + narrow[2:]
    return [narrow[:1], narrow[1:2] + wide[:1]] + [rest[i : i + 2] for i in range(0, len(rest), 2)]


def masks(bits):
    out = []
    for d in range(1 << len(bits)):
        chosen = [b for k, b in enumerate(bits) if d >> k & 1]
        out.append((sum(b[0] for b in chosen), sum(b[1] for b in chosen)))
    return out


def place_in(bits):
    n, w = lax.axis_index("narrow"), lax.axis_index("wide")
    place = 0
    for k, b in enumerate(bits):
        bit = lax.rem(lax.div(n, b[0]), 2) if b[0] else lax.rem(lax.div(w, b[1]), 2)
        place = place + bit * (1 << k)
    return place


def relative(place, d, count):
    out = 0
    for k in range(count.bit_length() - 1):
        bit = lax.rem(lax.div(place, 1 << k), 2)
        out = out + (1 << k) * (1 - bit if d >> k & 1 else bit)
    return out


def chunk_at(place, d, count, rows):
    return pl.ds(pl.multiple_of(relative(place, d, count) * rows, 8), rows)


def fold_kernel(bits, *refs):
    count = 1 << len(bits)
    parts, outs = refs[:-count], refs[-count:]
    place = place_in(bits)
    rows = outs[0].shape[0]
    for d in range(count):
        here = chunk_at(place, d, count, rows)
        total = parts[0][here, :]
        for part in parts[1:]:
            total = total + part[here, :]
        outs[d][...] = total


def fold(parts, bits):
    count = 1 << len(bits)
    rows, width = parts[0].shape
    return pl.pallas_call(
        functools.partial(fold_kernel, bits),
        in_specs=[VM] * len(parts),
        out_specs=[VM] * count,
        out_shape=[jax.ShapeDtypeStruct((rows // count, width), F32)] * count,
        compiler_params=params(),
        name="fold",
    )(*parts)


def fan(parts, bits):
    members = masks(bits)
    return [parts[0]] + [swap(parts[d], members[d]) for d in range(1, len(members))]


def all_sum(halves):
    groups = bit_groups()
    parts = fan(halves, groups[0])
    for bits in groups[1:-1]:
        parts = fan(fold(parts, bits), bits)
    x = sum(parts)
    x = sum(fan([x] * (1 << len(groups[-1])), groups[-1]))
    for bits in groups[1:-1][::-1]:
        blocks = fan([x] * (1 << len(bits)), bits)
        x = jnp.concatenate(blocks)
    return x, swap(x, masks(groups[0])[1])


def sum_order():
    groups = bit_groups()
    return groups[1:-1]


def tile_pairs(count):
    return [(i, j) for i in range(count) for j in range(i + 1, count)]


def packed_rows(count):
    rows = len(tile_pairs(count)) * TILE + count * TILE // 2 + count // 2 * TILE // 2
    blocks = 8
    for bits in bit_groups()[:-1]:
        blocks <<= len(bits)
    return -(-rows // blocks) * blocks


def gram_kernel(own, parts_ref, keep_ref, send_ref, rows_ref, packed):
    if parts_ref.ndim == 2:
        rows = parts_ref[...]
    else:
        parts, length, _ = parts_ref.shape
        count, half = length * TILE // own, TILE // 2
        heads = (own - half) // TILE
        pieces = []
        for part in range(parts):
            head = [parts_ref[part, h * count : (h + 1) * count, :] for h in range(heads)]
            tails = parts_ref[part, heads * count :, :]
            swapped = pltpu.roll(tails, half, 1)
            low = lax.broadcasted_iota(jnp.int32, tails.shape, 1) < half
            tail = jnp.concatenate([jnp.where(low, tails, swapped), jnp.where(low, swapped, tails)], axis=0)
            pieces.append(jnp.concatenate(head + [tail], axis=1)[:, :own])
        rows = jnp.concatenate(pieces, axis=0)
    rows_ref[...] = rows
    tiles, half = rows.shape[0] // TILE, TILE // 2
    hi, lo = split(rows)
    hi_turned, lo_turned = hi.T, lo.T
    at, tops = 0, len(tile_pairs(tiles)) * TILE
    lasts = tops + tiles * half
    for i in range(tiles):
        here, there = slice(i * TILE, (i + 1) * TILE), slice(i * TILE, None)
        both = jnp.concatenate([hi[here], lo[here]], axis=0)
        strip = dot_split(hi[here], both, hi_turned[:, there], lo_turned[:, there], NN)
        packed[tops + i * half : tops + (i + 1) * half, :] = strip[:half, :TILE]
        last = strip[half:, half:TILE]
        if i % 2 == 0:
            held = last
        else:
            packed[lasts + i // 2 * half : lasts + (i // 2 + 1) * half, :] = jnp.concatenate([held, last], axis=1)
        for j in range(i + 1, tiles):
            packed[at : at + TILE, :] = strip[:, (j - i) * TILE : (j - i + 1) * TILE]
            at += TILE
    used = lasts + tiles // 2 * half
    if used < packed.shape[0]:
        packed[used:, :] = jnp.zeros((packed.shape[0] - used, TILE), F32)
    odd, size = odd_device(), keep_ref.shape[0]
    keep_ref[...] = packed[pl.ds(pl.multiple_of(jnp.where(odd, size, 0), 8), size), :]
    send_ref[...] = packed[pl.ds(pl.multiple_of(jnp.where(odd, 0, size), 8), size), :]


def gram(parts, own):
    total = parts.size // own
    size = packed_rows(total // TILE)
    half = jax.ShapeDtypeStruct((size // 2, TILE), F32)
    return pl.pallas_call(
        functools.partial(gram_kernel, own),
        in_specs=[VM],
        out_specs=[VM] * 3,
        out_shape=[half, half, jax.ShapeDtypeStruct((total, own), F32)],
        scratch_shapes=[pltpu.VMEM((size, TILE), F32)],
        compiler_params=params(),
        name="gram",
    )(parts)


def turned_kernel(packed, rows_ref, out_ref):
    rows = rows_ref[...].T
    if packed:
        half = TILE // 2
        rows = jnp.where(odd_place("wide"), jnp.concatenate([rows[-half:], rows[:-half]], axis=0), rows)
    out_ref[...] = rows


def turned(rows, packed):
    return pl.pallas_call(
        functools.partial(turned_kernel, packed),
        in_specs=[VM],
        out_specs=VM,
        out_shape=jax.ShapeDtypeStruct(rows.shape[::-1], F32),
        compiler_params=params(),
        name="turned",
    )(rows)


def rotate_kernel(total_rows, groups, own_ref, other_ref, rows_ref, out_ref, packed, hi_ref, lo_ref, held, sems):
    size = own_ref.shape[0]
    places = [place_in(bits) for bits in groups]
    blocks = 1
    for bits in groups:
        blocks <<= len(bits)
    length = size // blocks
    odd = odd_device()
    for block in range(blocks):
        at, rest, step = 0, block, blocks
        for bits, place in zip(groups, places):
            count = 1 << len(bits)
            step //= count
            at = at + relative(place, rest // step, count) * (step * length)
            rest %= step
        here = slice(block * length, (block + 1) * length)
        packed[pl.ds(pl.multiple_of(jnp.where(odd, size, 0) + at, 8), length), :] = own_ref[here, :]
        packed[pl.ds(pl.multiple_of(jnp.where(odd, 0, size) + at, 8), length), :] = other_ref[here, :]
    tiles, half = rows_ref.shape[1] // TILE, TILE // 2
    order = tile_pairs(tiles)
    tops = len(order) * TILE
    lasts = tops + tiles * half
    above = packed[:tops, :].reshape(len(order), TILE, TILE)
    squares = jnp.sum(above * above, axis=0) * 2.0
    top = packed[tops:lasts, :].reshape(tiles, half, TILE)
    weight = jnp.where(lax.broadcasted_iota(jnp.int32, (half, TILE), 1) < half, 1.0, 2.0)
    last = packed[lasts : lasts + tiles // 2 * half, :].reshape(tiles // 2, half, TILE)
    squares = squares[:half] + squares[half:] + jnp.sum(top * top, axis=0) * weight + jnp.sum(last * last, axis=0)
    frob = jnp.sqrt(jnp.sum(squares, axis=(0, 1), keepdims=True) + 1e-06)
    factor = 0.5 / frob
    gain = jnp.sqrt(total_rows / frob)
    for at, (i, j) in enumerate(order):
        hi, lo = split(packed[at * TILE : (at + 1) * TILE, :] * factor)
        one, two = slice(i * TILE, (i + 1) * TILE), slice(j * TILE, (j + 1) * TILE)
        hi_ref[one, two] = hi
        lo_ref[one, two] = lo
        hi_ref[two, one] = hi.T
        lo_ref[two, one] = lo.T
    for i in range(tiles):
        upper = packed[tops + i * half : tops + (i + 1) * half, :]
        quarter = packed[lasts + i // 2 * half : lasts + (i // 2 + 1) * half, :][:, i % 2 * half : (i % 2 + 1) * half]
        lower = jnp.concatenate([upper[:, half:].T, quarter], axis=1)
        hi, lo = split(jnp.concatenate([upper, lower], axis=0) * factor)
        one = slice(i * TILE, (i + 1) * TILE)
        hi_ref[one, one] = hi
        lo_ref[one, one] = lo
    rows = rows_ref[...]
    rows_hi, rows_lo = split(rows)
    both = jnp.concatenate([rows_hi, rows_lo], axis=0)
    copies = []
    for strip in range(tiles // 2):
        here = slice(strip * 2 * TILE, (strip + 1) * 2 * TILE)
        turned = dot_split(rows_hi, both, hi_ref[:, here], lo_ref[:, here], NN)
        held[:, here] = gain * (1.5 * rows[:, here] - turned)
        copies.append(pltpu.make_async_copy(held.at[:, here], out_ref.at[:, here], sems.at[strip]))
        copies[-1].start()
    for copy in copies:
        copy.wait()


def rotate(halves, rows, total_rows):
    own, total = rows.shape
    return pl.pallas_call(
        functools.partial(rotate_kernel, float(total_rows), sum_order()),
        in_specs=[VM, VM, VM],
        out_specs=HBM,
        out_shape=pltpu.HBM(rows.shape, F32),
        scratch_shapes=[
            pltpu.VMEM((packed_rows(total // TILE), TILE), F32),
            pltpu.VMEM((total, total), BF16),
            pltpu.VMEM((total, total), BF16),
            pltpu.VMEM(rows.shape, F32),
            pltpu.SemaphoreType.DMA((total // TILE // 2,)),
        ],
        compiler_params=params(),
        name="rotate",
    )(*halves, rows).T


def regroup(parts):
    size = lax.axis_size("wide")
    if parts.ndim == 3:
        return lax.all_to_all(parts, "wide", split_axis=0, concat_axis=0, tiled=True)
    count, length = parts.shape
    own = length // size
    parts = parts.reshape(count, size, own).transpose(1, 0, 2).reshape(size, count * own // TILE, TILE)
    parts = lax.all_to_all(parts, "wide", split_axis=0, concat_axis=0, tiled=True)
    return parts.reshape(size * count, own)


def on_device(vectors, blocks, columns, lower_bound, upper_bound):
    length = vectors.shape[1]
    parts = regroup(filtered_parts(vectors, blocks, columns, lower_bound, upper_bound))
    *halves, rows = gram(parts, length // lax.axis_size("wide"))
    return rotate(all_sum(halves), turned(rows, parts.ndim == 3), length * lax.axis_size("narrow"))


def solution(mesh):
    return jax.shard_map(
        on_device,
        mesh=mesh,
        in_specs=(P("wide", "narrow"), P("narrow", None, None, None), P("narrow", None), P(), P()),
        out_specs=P(None, ("narrow", "wide")),
        check_vma=False,
    )
```

```python
import functools

import jax
import jax.numpy as jnp
from jax import lax
from jax.experimental import pallas as pl
from jax.experimental.pallas import tpu as pltpu
from jax.sharding import PartitionSpec as P

REACH = 3
CROSS_PARTS = 4
STEPS = 8
TILE = 128
VM = pl.BlockSpec(memory_space=pltpu.VMEM)
SM = pl.BlockSpec(memory_space=pltpu.SMEM)
HBM = pl.BlockSpec(memory_space=pltpu.HBM)
NT = (((1,), (1,)), ((), ()))
NN = (((1,), (0,)), ((), ()))
F32 = jnp.float32
BF16 = jnp.bfloat16


def params():
    return pltpu.CompilerParams(vmem_limit_bytes=40 * 1024 * 1024)


def split(x):
    hi = x.astype(BF16)
    return hi, (x - hi.astype(F32)).astype(BF16)


def in_hbm(x):
    return pltpu.with_memory_space_constraint(x, pltpu.HBM)


def odd_place(axis):
    return lax.rem(lax.axis_index(axis), 2) == 1


def odd_device():
    return odd_place("narrow")


def dot(a, b, dims):
    return lax.dot_general(a, b, dims, preferred_element_type=F32)


def dot_split(a_hi, a_both, b_hi, b_lo, dims):
    rows = a_hi.shape[0]
    upper = dot(a_both, b_hi, dims)
    return upper[:rows] + (upper[rows:] + dot(a_hi, b_lo, dims))


def cross_at(row, place):
    return sum(REACH - r for r in range(row)) + place + REACH - row


def spread_kernel(total_blocks, columns_hbm, vectors_hbm, blocks_hbm, far_ref, near_ref, vectors_ref, part_ref, hi_ref, lo_ref, held, straight, cross_ref, columns_ref, sems, pair_sems):
    rows, slots, size, _ = blocks_hbm.shape
    edge = far_ref.shape[1]
    odd = odd_device()
    source = [jnp.where(odd, rows - 1 - row, row) for row in range(rows)]
    copies = [
        pltpu.make_async_copy(columns_hbm, columns_ref, sems.at[0]),
        pltpu.make_async_copy(vectors_hbm, straight, sems.at[1]),
    ]
    large = []
    for pair in range(rows // 2):
        begin = jnp.where(odd, rows - 2 - 2 * pair, 2 * pair)
        large.append(pltpu.make_async_copy(blocks_hbm.at[pl.ds(begin, 2)], held.at[pl.ds(2 * pair, 2)], pair_sems.at[pair]))
    for copy in copies + large:
        copy.start()
    for half in range(2):
        always = {half + offset + REACH for offset in (-1, 1, REACH if half else -REACH)}
        for slot in set(range(2 * REACH + 2)) - always:
            empty = jnp.zeros((rows // 2, size, size), BF16)
            hi_ref[:, slot * size : (slot + 1) * size, half * size : (half + 1) * size] = empty
            lo_ref[:, slot * size : (slot + 1) * size, half * size : (half + 1) * size] = empty
    cross_ref[...] = jnp.zeros_like(cross_ref)
    first = lax.axis_index("narrow") * rows
    copies[0].wait()
    for row in range(rows):
        pair, half = divmod(row, 2)
        if half == 0:
            large[pair].wait()
        place = 2 * pair + jnp.where(odd, 1 - half, half)
        here = slice(half * size, half * size + size)
        for slot in range(slots):
            offset = columns_ref[slot, source[row]] - (first + source[row])
            offset = jnp.where(offset > REACH, offset - total_blocks, offset)
            offset = jnp.where(offset < -REACH, offset + total_blocks, offset)
            offset = jnp.where(odd, -offset, offset)
            block = held[place, slot]
            hi, lo = split(block)
            there = pl.ds(pl.multiple_of((half + offset + REACH) * size, size), size)
            hi_ref[pair, there, here] = hi.T
            lo_ref[pair, there, here] = lo.T
            if row < REACH:

                @pl.when(row + offset < 0)
                def _():
                    at = pl.multiple_of(cross_at(row, row + offset) * size, size)
                    cross_ref[pl.ds(at, size), :] = block

    count = part_ref.shape[0]
    part_ref[...] = cross_ref[pl.ds(pl.multiple_of(lax.rem(lax.axis_index("wide"), CROSS_PARTS) * count, 8), count), :]
    copies[1].wait()
    whole = straight[...]
    vectors_ref[...] = jnp.where(odd, jnp.concatenate(reversed_blocks(whole, size), axis=1), whole)
    far_ref[...] = vectors_ref[:, :edge]
    near_ref[...] = vectors_ref[:, -edge:]


def spread_part(columns, vectors, blocks, total_blocks):
    rows, slots, size, _ = blocks.shape
    spread = jax.ShapeDtypeStruct((rows // 2, (2 * REACH + 2) * size, 2 * size), BF16)
    edge = jax.ShapeDtypeStruct((vectors.shape[0], REACH * size), F32)
    crossing = REACH * (REACH + 1) // 2 * size
    cross = jax.ShapeDtypeStruct((crossing // CROSS_PARTS, size), F32)
    return pl.pallas_call(
        functools.partial(spread_kernel, total_blocks),
        in_specs=[HBM, HBM, HBM],
        out_specs=[VM] * 6,
        out_shape=[edge, edge, jax.ShapeDtypeStruct(vectors.shape, F32), cross, spread, spread],
        scratch_shapes=[
            pltpu.VMEM(blocks.shape, F32),
            pltpu.VMEM(vectors.shape, F32),
            pltpu.VMEM((crossing, size), F32),
            pltpu.SMEM((slots, rows), jnp.int32),
            pltpu.SemaphoreType.DMA((2,)),
            pltpu.SemaphoreType.DMA((rows // 2,)),
        ],
        compiler_params=params(),
        name="spread_part",
    )(in_hbm(columns.T), in_hbm(vectors), in_hbm(blocks))


class Strip:
    def __init__(self, values, at, size):
        self.hi, lo = split(values)
        self.both = jnp.concatenate([self.hi, lo], axis=0)
        self.at, self.size = at, size

    def band(self, operator, pair, begin, end, half=None):
        hi_ref, lo_ref = operator
        size, start = self.size, 2 * pair - REACH
        there = slice((begin - self.at) * size, (end - self.at) * size)
        inside = slice((begin - start) * size, (end - start) * size)
        rows = slice(None) if half is None else slice(half * size, (half + 1) * size)
        hi, lo = hi_ref[pair, inside, rows], lo_ref[pair, inside, rows]
        return dot_split(self.hi[:, there], self.both[:, there], hi, lo, NN)


def reversed_blocks(edge, size):
    return [edge[:, k * size : (k + 1) * size] for k in reversed(range(edge.shape[1] // size))]


def far_sum(operator, halo, size):
    strip = Strip(jnp.concatenate(reversed_blocks(halo, size), axis=1), -REACH, size)
    outer = strip.band(operator, 0, -REACH, 0)
    inner = strip.band(operator, 1, -1, 0, 0)
    return jnp.concatenate([outer, inner], axis=1)


def near_sum(operator, halo, size):
    pairs = operator[0].shape[0]
    strip = Strip(jnp.concatenate(reversed_blocks(halo, size), axis=1), 2 * pairs, size)
    outer = strip.band(operator, pairs - 1, 2 * pairs, 2 * pairs + REACH)
    inner = strip.band(operator, pairs - 2, 2 * pairs, 2 * pairs + 1, 1)
    return jnp.concatenate([inner, outer], axis=1)


def own_sum(operator, strip, pair, lowest=0):
    pairs = operator[0].shape[0]
    return strip.band(operator, pair, max(2 * pair - REACH, lowest), min(2 * pair + REACH + 2, 2 * pairs))


def first_kernel(terms_ref, vectors_ref, hi_ref, lo_ref, out_ref):
    pairs, _, width = hi_ref.shape
    scale, diag = terms_ref[0:1, :], terms_ref[1:2, :]
    strip = Strip(vectors_ref[...], 0, width // 2)
    for pair in range(pairs):
        here = slice(pair * width, pair * width + width)
        total = scale * own_sum((hi_ref, lo_ref), strip, pair) + diag * vectors_ref[:, here]
        out_ref[:, here] = 0.5 * total


def local_kernel(first_pair, terms_ref, far_ref, mid_ref, near_ref, far_before_ref, mid_before_ref, near_before_ref, hi_ref, lo_ref, out_ref, *full_ref):
    pairs, _, width = hi_ref.shape
    edge, start = near_ref.shape[1], far_ref.shape[1]
    scale, diag = terms_ref[0:1, :], terms_ref[1:2, :]
    current = jnp.concatenate([far_ref[...], mid_ref[:, start:-edge], near_ref[...]], axis=1)
    before = jnp.concatenate([far_before_ref[...], mid_before_ref[:, edge:-edge], near_before_ref[...]], axis=1)
    if full_ref:
        full_ref[0][...] = current
    strip = Strip(current, 0, width // 2)
    for pair in range(first_pair, pairs):
        here = slice(pair * width, pair * width + width)
        total = scale * own_sum((hi_ref, lo_ref), strip, pair) + diag * current[:, here]
        out_ref[:, here] = total - before[:, here]


def second_kernel(terms_ref, mid_ref, near_ref, before_ref, hi_ref, lo_ref, out_ref):
    pairs, _, width = hi_ref.shape
    edge = near_ref.shape[1]
    scale, diag = terms_ref[0:1, :], terms_ref[1:2, :]
    current = jnp.concatenate([mid_ref[:, edge:-edge], near_ref[...]], axis=1)
    padded = jnp.concatenate([jnp.zeros(near_ref.shape, F32), current], axis=1)
    strip = Strip(current, REACH, width // 2)
    for pair in range(pairs):
        here = slice(pair * width, pair * width + width)
        total = scale * own_sum((hi_ref, lo_ref), strip, pair, REACH) + diag * padded[:, here]
        out_ref[:, here] = total - before_ref[:, here]


def step_call(kernel, name, operands, operator, outs):
    size = operands[1].size
    width = operator[0].shape[-1]
    return pl.pallas_call(
        kernel,
        in_specs=[VM] * (len(operands) + 2),
        out_specs=[VM] * len(outs),
        out_shape=[jax.ShapeDtypeStruct(shape, F32) for shape in outs],
        compiler_params=params(),
        cost_estimate=pl.CostEstimate(flops=24 * size * width, bytes_accessed=8 * size, transcendentals=0),
        name=name,
    )(*operands, *operator)


def near_kernel(factor, terms_ref, mid_ref, halo_ref, hi_ref, lo_ref, out_ref):
    size, edge = hi_ref.shape[2] // 2, halo_ref.shape[1]
    scale = factor * terms_ref[0:1, 0:1]
    out_ref[...] = mid_ref[:, -edge:] + scale * near_sum((hi_ref, lo_ref), halo_ref[...], size)


def edge_ahead(operator, scale, diag, far, before, size):
    strip = Strip(far, 0, size)
    outer = strip.band(operator, 0, 0, REACH + 2)
    inner = strip.band(operator, 1, 0, 2 * REACH, 0)
    total = jnp.concatenate([outer, inner], axis=1)
    return scale * total + diag * far[:, : total.shape[1]] - before


def far_kernel(terms_ref, mid_ref, halo_ref, hi_ref, lo_ref, far_ref):
    size, edge = hi_ref.shape[2] // 2, halo_ref.shape[1]
    far_ref[...] = mid_ref[:, :edge] + 0.5 * terms_ref[0:1, 0:1] * far_sum((hi_ref, lo_ref), halo_ref[...], size)


def turn_one_kernel(terms_ref, mid_ref, halo_ref, before_ref, hi_ref, lo_ref, far_ref, send_ref):
    operator = (hi_ref, lo_ref)
    size, edge = hi_ref.shape[2] // 2, halo_ref.shape[1]
    scale, diag = terms_ref[0:1, 0:1], terms_ref[1:2, 0:1]
    edge_rows = mid_ref[:, :edge] + scale * far_sum(operator, halo_ref[...], size)
    far = jnp.concatenate([edge_rows, mid_ref[:, edge : 2 * edge]], axis=1)
    far_ref[...] = far
    send_ref[0] = edge_rows
    send_ref[1] = edge_ahead(operator, scale, diag, far, before_ref[...], size)


def beyond_sum(terms_ref, sent_ref, cross_hi_ref, cross_lo_ref):
    size = cross_hi_ref.shape[1]

    def cross(ref, row):
        rows = [slice(at * size, (at + 1) * size) for at in (cross_at(row, -1 - place) for place in range(REACH - row))]
        return jnp.concatenate([ref[here, :] for here in rows], axis=1)

    own = Strip(sent_ref[0], 0, size)
    pieces = []
    for row in range(REACH):
        there = slice(0, (REACH - row) * size)
        hi, lo = cross(cross_hi_ref, row), cross(cross_lo_ref, row)
        pieces.append(dot_split(own.hi[:, there], own.both[:, there], hi, lo, NT))
    return terms_ref[0:1, 0:1] * jnp.concatenate(pieces, axis=1)


def beyond_kernel(terms_ref, sent_ref, cross_hi_ref, cross_lo_ref, out_ref):
    out_ref[...] = beyond_sum(terms_ref, sent_ref, cross_hi_ref, cross_lo_ref)


def turn(terms_ref, mid_ref, sent_ref, got_ref, beyond_refs, operator):
    size, edge = operator[0].shape[2] // 2, sent_ref.shape[2]
    scale, diag = terms_ref[0:1, 0:1], terms_ref[1:2, 0:1]
    between = sent_ref[1] + scale * far_sum(operator, got_ref[0], size)
    beyond = beyond_refs[0][...] if len(beyond_refs) == 1 else beyond_sum(terms_ref, sent_ref, *beyond_refs)
    beyond = got_ref[1] + beyond
    strip = Strip(jnp.concatenate(reversed_blocks(beyond, size) + [between], axis=1), -REACH, size)
    total = [strip.band(operator, pair, 2 * pair - REACH, REACH) for pair in range(REACH)]
    known = jnp.concatenate([diag * between, jnp.zeros_like(between)], axis=1)
    return between, mid_ref[:, : 2 * edge] + scale * jnp.concatenate(total, axis=1) + known


def cross_kernel(mine_ref, one_ref, two_ref, hi_ref, lo_ref):
    rows = mine_ref.shape[0]
    place = lax.rem(lax.axis_index("wide"), CROSS_PARTS)
    for d, part in enumerate([mine_ref[...], one_ref[...], two_ref[:rows, :], two_ref[rows:, :]]):
        here = chunk_at(place, d, CROSS_PARTS, rows)
        hi, lo = split(part)
        hi_ref[here, :] = hi
        lo_ref[here, :] = lo


def cross_part(mine):
    one = wide_swap(mine, 1)
    two = wide_swap(jnp.concatenate([mine, one]), 2)
    rows, width = mine.shape
    return pl.pallas_call(
        cross_kernel,
        in_specs=[VM] * 3,
        out_specs=[VM] * 2,
        out_shape=[jax.ShapeDtypeStruct((CROSS_PARTS * rows, width), BF16)] * 2,
        compiler_params=params(),
        name="cross_part",
    )(mine, one, two)


def turn_two_kernel(terms_ref, mid_ref, sent_ref, got_ref, *refs):
    *beyond_refs, hi_ref, lo_ref, between_ref, far_ref, send_ref = refs
    operator = (hi_ref, lo_ref)
    size, edge = hi_ref.shape[2] // 2, between_ref.shape[1]
    between, far = turn(terms_ref, mid_ref, sent_ref, got_ref, beyond_refs, operator)
    between_ref[...] = between
    far_ref[...] = far
    send_ref[0] = far[:, :edge]
    send_ref[1] = edge_ahead(operator, terms_ref[0:1, 0:1], terms_ref[1:2, 0:1], far, between, size)


def packs(count, own):
    return own % TILE == TILE // 2 and own > TILE and count % 16 == 0


def last_kernel(parts, terms_ref, mid_ref, sent_ref, got_ref, beyond_ref, near_ref, hi_ref, lo_ref, out_ref):
    size = hi_ref.shape[2] // 2
    _, far = turn(terms_ref, mid_ref, sent_ref, got_ref, (beyond_ref,), (hi_ref, lo_ref))
    whole = jnp.concatenate([far, mid_ref[:, far.shape[1] : -near_ref.shape[1]], near_ref[...]], axis=1)
    mirrored = jnp.concatenate(reversed_blocks(whole, size), axis=1)
    whole = jnp.where(odd_device(), mirrored, whole)
    if len(out_ref.shape) == 2:
        out_ref[...] = whole
        return
    count, own, half = whole.shape[0], whole.shape[1] // parts, TILE // 2
    for part in range(parts):
        begin = part * own
        head, tail = (begin, begin + own - half) if part % 2 == 0 else (begin + half, begin)
        at = 0
        for column in range(head, head + own - half, TILE):
            out_ref[part, at : at + count, :] = whole[:, column : column + TILE]
            at += count
        tails = whole[:, tail : tail + half]
        out_ref[part, at:, :] = jnp.concatenate([tails[: count // 2], tails[count // 2 :]], axis=1)


def far_swap(x):
    size = lax.axis_size("narrow")
    return lax.ppermute(x, "narrow", [(i, (i + 1) % size if i % 2 else (i - 1) % size) for i in range(size)])


def wide_swap(x, mask):
    return lax.ppermute(x, "wide", [(i, i ^ mask) for i in range(lax.axis_size("wide"))])


def near_swap(x):
    return lax.ppermute(x, "narrow", [(i, i ^ 1) for i in range(lax.axis_size("narrow"))])


def filtered_parts(vectors, blocks, columns, lower_bound, upper_bound):
    size = blocks.shape[2]
    width, edge, parts = 2 * size, REACH * size, lax.axis_size("wide")
    count, length = vectors.shape
    half_width = (upper_bound - lower_bound) * 0.5
    scale = 2.0 / half_width
    diag = scale * (1.0 - (upper_bound + lower_bound) * 0.5)
    terms = jnp.concatenate([jnp.broadcast_to(scale, (1, width)), jnp.broadcast_to(diag, (1, width))])
    total_blocks = blocks.shape[0] * lax.axis_size("narrow")
    far, near, vectors, cross, *operator = spread_part(columns, vectors, blocks, total_blocks)
    whole, side, double = (count, length), (count, edge), (2, count, edge)

    def near_part(factor, mid, halo):
        kernel = functools.partial(near_kernel, factor)
        return step_call(kernel, "near_part", (terms, mid, halo), operator, [side])[0]

    def local_part(first_pair, outs):
        kernel = functools.partial(local_kernel, first_pair)
        return step_call(kernel, "local_part", (terms, far, mid, near, *before), operator, [whole] * outs)

    halo, near_halo = far_swap(far), near_swap(near)
    cross = cross_part(far_swap(cross))
    (mid,) = step_call(first_kernel, "first_part", (terms, vectors), operator, [whole])
    before = (far, vectors, near)
    near = near_part(0.5, mid, near_halo)
    (far,) = step_call(far_kernel, "far_part", (terms, mid, halo), operator, [side])
    halo, near_halo = far_swap(far), near_swap(near)
    (next_mid,) = local_part(0, 1)
    before = (far, mid, near)
    mid, near = next_mid, near_part(1.0, next_mid, near_halo)
    far, send = step_call(turn_one_kernel, "turn_one", (terms, mid, halo, far), operator, [(count, 2 * edge), double])
    for step in range(2, STEPS, 2):
        got, near_halo = far_swap(send), near_swap(near)
        mid, full = local_part(1, 2)
        near = near_part(1.0, mid, near_halo)
        near_halo = near_swap(near)
        (next_mid,) = step_call(second_kernel, "second_part", (terms, mid, near, full), operator, [whole])
        next_near = near_part(1.0, next_mid, near_halo)
        beyond = cross
        if step > 2:
            beyond = step_call(beyond_kernel, "beyond_part", (terms, send), cross, [side])
        operands = (terms, next_mid, send, got, *beyond)
        if step < STEPS - 2:
            outs = [side, (count, 2 * edge), double]
            between, far, send = step_call(turn_two_kernel, "turn_two", operands, operator, outs)
            before = (between, mid, near)
        mid, near = next_mid, next_near
    shape = (parts, count * length // parts // TILE, TILE) if packs(count, length // parts) else whole
    return step_call(functools.partial(last_kernel, parts), "last_part", (*operands, near), operator, [shape])[0]


def pair_perm(mask):
    narrow, wide = lax.axis_size("narrow"), lax.axis_size("wide")
    return [(n * wide + w, (n ^ mask[0]) * wide + (w ^ mask[1])) for n in range(narrow) for w in range(wide)]


def swap(x, mask):
    return lax.ppermute(x, ("narrow", "wide"), pair_perm(mask))


def bit_groups():
    narrow = [(1 << b, 0) for b in range(lax.axis_size("narrow").bit_length() - 1)]
    wide = [(0, 1 << b) for b in range(lax.axis_size("wide").bit_length() - 1)]
    rest = wide[1:] + narrow[2:]
    return [narrow[:1], narrow[1:2] + wide[:1]] + [rest[i : i + 2] for i in range(0, len(rest), 2)]


def masks(bits):
    out = []
    for d in range(1 << len(bits)):
        chosen = [b for k, b in enumerate(bits) if d >> k & 1]
        out.append((sum(b[0] for b in chosen), sum(b[1] for b in chosen)))
    return out


def place_in(bits):
    n, w = lax.axis_index("narrow"), lax.axis_index("wide")
    place = 0
    for k, b in enumerate(bits):
        bit = lax.rem(lax.div(n, b[0]), 2) if b[0] else lax.rem(lax.div(w, b[1]), 2)
        place = place + bit * (1 << k)
    return place


def relative(place, d, count):
    out = 0
    for k in range(count.bit_length() - 1):
        bit = lax.rem(lax.div(place, 1 << k), 2)
        out = out + (1 << k) * (1 - bit if d >> k & 1 else bit)
    return out


def chunk_at(place, d, count, rows):
    return pl.ds(pl.multiple_of(relative(place, d, count) * rows, 8), rows)


def fold_kernel(bits, *refs):
    count = 1 << len(bits)
    parts, outs = refs[:-count], refs[-count:]
    place = place_in(bits)
    rows = outs[0].shape[0]
    for d in range(count):
        here = chunk_at(place, d, count, rows)
        total = parts[0][here, :]
        for part in parts[1:]:
            total = total + part[here, :]
        outs[d][...] = total


def fold(parts, bits):
    count = 1 << len(bits)
    rows, width = parts[0].shape
    return pl.pallas_call(
        functools.partial(fold_kernel, bits),
        in_specs=[VM] * len(parts),
        out_specs=[VM] * count,
        out_shape=[jax.ShapeDtypeStruct((rows // count, width), F32)] * count,
        compiler_params=params(),
        name="fold",
    )(*parts)


def fan(parts, bits):
    members = masks(bits)
    return [parts[0]] + [swap(parts[d], members[d]) for d in range(1, len(members))]


def all_sum(halves):
    groups = bit_groups()
    parts = fan(halves, groups[0])
    for bits in groups[1:-1]:
        parts = fan(fold(parts, bits), bits)
    x = sum(parts)
    x = sum(fan([x] * (1 << len(groups[-1])), groups[-1]))
    for bits in groups[1:-1][::-1]:
        blocks = fan([x] * (1 << len(bits)), bits)
        x = jnp.concatenate(blocks)
    return x, swap(x, masks(groups[0])[1])


def sum_order():
    groups = bit_groups()
    return groups[1:-1]


def tile_pairs(count):
    return [(i, j) for i in range(count) for j in range(i + 1, count)]


def packed_rows(count):
    rows = len(tile_pairs(count)) * TILE + count * TILE // 2 + count // 2 * TILE // 2
    blocks = 8
    for bits in bit_groups()[:-1]:
        blocks <<= len(bits)
    return -(-rows // blocks) * blocks


def gram_kernel(own, parts_ref, keep_ref, send_ref, rows_ref, packed):
    if parts_ref.ndim == 2:
        rows = parts_ref[...]
    else:
        parts, length, _ = parts_ref.shape
        count, half = length * TILE // own, TILE // 2
        heads = (own - half) // TILE
        pieces = []
        for part in range(parts):
            head = [parts_ref[part, h * count : (h + 1) * count, :] for h in range(heads)]
            tails = parts_ref[part, heads * count :, :]
            swapped = pltpu.roll(tails, half, 1)
            low = lax.broadcasted_iota(jnp.int32, tails.shape, 1) < half
            tail = jnp.concatenate([jnp.where(low, tails, swapped), jnp.where(low, swapped, tails)], axis=0)
            pieces.append(jnp.concatenate(head + [tail], axis=1)[:, :own])
        rows = jnp.concatenate(pieces, axis=0)
    rows_ref[...] = rows
    tiles, half = rows.shape[0] // TILE, TILE // 2
    hi, lo = split(rows)
    at, tops = 0, len(tile_pairs(tiles)) * TILE
    lasts = tops + tiles * half
    for i in range(tiles):
        here, there = slice(i * TILE, (i + 1) * TILE), slice(i * TILE, None)
        both = jnp.concatenate([hi[here], lo[here]], axis=0)
        strip = dot_split(hi[here], both, hi[there], lo[there], NT)
        packed[tops + i * half : tops + (i + 1) * half, :] = strip[:half, :TILE]
        last = strip[half:, half:TILE]
        if i % 2 == 0:
            held = last
        else:
            packed[lasts + i // 2 * half : lasts + (i // 2 + 1) * half, :] = jnp.concatenate([held, last], axis=1)
        for j in range(i + 1, tiles):
            packed[at : at + TILE, :] = strip[:, (j - i) * TILE : (j - i + 1) * TILE]
            at += TILE
    used = lasts + tiles // 2 * half
    if used < packed.shape[0]:
        packed[used:, :] = jnp.zeros((packed.shape[0] - used, TILE), F32)
    odd, size = odd_device(), keep_ref.shape[0]
    keep_ref[...] = packed[pl.ds(pl.multiple_of(jnp.where(odd, size, 0), 8), size), :]
    send_ref[...] = packed[pl.ds(pl.multiple_of(jnp.where(odd, 0, size), 8), size), :]


def gram(parts, own):
    total = parts.size // own
    size = packed_rows(total // TILE)
    half = jax.ShapeDtypeStruct((size // 2, TILE), F32)
    return pl.pallas_call(
        functools.partial(gram_kernel, own),
        in_specs=[VM],
        out_specs=[VM] * 3,
        out_shape=[half, half, jax.ShapeDtypeStruct((total, own), F32)],
        scratch_shapes=[pltpu.VMEM((size, TILE), F32)],
        compiler_params=params(),
        name="gram",
    )(parts)


def turned_kernel(packed, rows_ref, out_ref):
    rows = rows_ref[...].T
    if packed:
        half = TILE // 2
        rows = jnp.where(odd_place("wide"), jnp.concatenate([rows[-half:], rows[:-half]], axis=0), rows)
    out_ref[...] = rows


def turned(rows, packed):
    return pl.pallas_call(
        functools.partial(turned_kernel, packed),
        in_specs=[VM],
        out_specs=VM,
        out_shape=jax.ShapeDtypeStruct(rows.shape[::-1], F32),
        compiler_params=params(),
        name="turned",
    )(rows)


def rotate_kernel(total_rows, groups, own_ref, other_ref, rows_ref, out_ref, packed, hi_ref, lo_ref, held, sems):
    size = own_ref.shape[0]
    places = [place_in(bits) for bits in groups]
    blocks = 1
    for bits in groups:
        blocks <<= len(bits)
    length = size // blocks
    odd = odd_device()
    for block in range(blocks):
        at, rest, step = 0, block, blocks
        for bits, place in zip(groups, places):
            count = 1 << len(bits)
            step //= count
            at = at + relative(place, rest // step, count) * (step * length)
            rest %= step
        here = slice(block * length, (block + 1) * length)
        packed[pl.ds(pl.multiple_of(jnp.where(odd, size, 0) + at, 8), length), :] = own_ref[here, :]
        packed[pl.ds(pl.multiple_of(jnp.where(odd, 0, size) + at, 8), length), :] = other_ref[here, :]
    tiles, half = rows_ref.shape[1] // TILE, TILE // 2
    order = tile_pairs(tiles)
    tops = len(order) * TILE
    lasts = tops + tiles * half
    above = packed[:tops, :].reshape(len(order), TILE, TILE)
    squares = jnp.sum(above * above, axis=0) * 2.0
    top = packed[tops:lasts, :].reshape(tiles, half, TILE)
    weight = jnp.where(lax.broadcasted_iota(jnp.int32, (half, TILE), 1) < half, 1.0, 2.0)
    last = packed[lasts : lasts + tiles // 2 * half, :].reshape(tiles // 2, half, TILE)
    squares = squares[:half] + squares[half:] + jnp.sum(top * top, axis=0) * weight + jnp.sum(last * last, axis=0)
    frob = jnp.sqrt(jnp.sum(squares, axis=(0, 1), keepdims=True) + 1e-06)
    factor = 0.5 / frob
    gain = jnp.sqrt(total_rows / frob)
    for at, (i, j) in enumerate(order):
        hi, lo = split(packed[at * TILE : (at + 1) * TILE, :] * factor)
        one, two = slice(i * TILE, (i + 1) * TILE), slice(j * TILE, (j + 1) * TILE)
        hi_ref[one, two] = hi
        lo_ref[one, two] = lo
        hi_ref[two, one] = hi.T
        lo_ref[two, one] = lo.T
    for i in range(tiles):
        upper = packed[tops + i * half : tops + (i + 1) * half, :]
        quarter = packed[lasts + i // 2 * half : lasts + (i // 2 + 1) * half, :][:, i % 2 * half : (i % 2 + 1) * half]
        lower = jnp.concatenate([upper[:, half:].T, quarter], axis=1)
        hi, lo = split(jnp.concatenate([upper, lower], axis=0) * factor)
        one = slice(i * TILE, (i + 1) * TILE)
        hi_ref[one, one] = hi
        lo_ref[one, one] = lo
    rows = rows_ref[...]
    rows_hi, rows_lo = split(rows)
    both = jnp.concatenate([rows_hi, rows_lo], axis=0)
    copies = []
    for strip in range(tiles // 2):
        here = slice(strip * 2 * TILE, (strip + 1) * 2 * TILE)
        turned = dot_split(rows_hi, both, hi_ref[:, here], lo_ref[:, here], NN)
        held[:, here] = gain * (1.5 * rows[:, here] - turned)
        copies.append(pltpu.make_async_copy(held.at[:, here], out_ref.at[:, here], sems.at[strip]))
        copies[-1].start()
    for copy in copies:
        copy.wait()


def rotate(halves, rows, total_rows):
    own, total = rows.shape
    return pl.pallas_call(
        functools.partial(rotate_kernel, float(total_rows), sum_order()),
        in_specs=[VM, VM, VM],
        out_specs=HBM,
        out_shape=pltpu.HBM(rows.shape, F32),
        scratch_shapes=[
            pltpu.VMEM((packed_rows(total // TILE), TILE), F32),
            pltpu.VMEM((total, total), BF16),
            pltpu.VMEM((total, total), BF16),
            pltpu.VMEM(rows.shape, F32),
            pltpu.SemaphoreType.DMA((total // TILE // 2,)),
        ],
        compiler_params=params(),
        name="rotate",
    )(*halves, rows).T


def regroup(parts):
    size = lax.axis_size("wide")
    if parts.ndim == 3:
        return lax.all_to_all(parts, "wide", split_axis=0, concat_axis=0, tiled=True)
    count, length = parts.shape
    own = length // size
    parts = parts.reshape(count, size, own).transpose(1, 0, 2).reshape(size, count * own // TILE, TILE)
    parts = lax.all_to_all(parts, "wide", split_axis=0, concat_axis=0, tiled=True)
    return parts.reshape(size * count, own)


def on_device(vectors, blocks, columns, lower_bound, upper_bound):
    length = vectors.shape[1]
    parts = regroup(filtered_parts(vectors, blocks, columns, lower_bound, upper_bound))
    *halves, rows = gram(parts, length // lax.axis_size("wide"))
    return rotate(all_sum(halves), turned(rows, parts.ndim == 3), length * lax.axis_size("narrow"))


def solution(mesh):
    return jax.shard_map(
        on_device,
        mesh=mesh,
        in_specs=(P("wide", "narrow"), P("narrow", None, None, None), P("narrow", None), P(), P()),
        out_specs=P(None, ("narrow", "wide")),
        check_vma=False,
    )
```
